32 devices in a mesh: row: 16 (over z, y, core), col: 2 (over x).
Axes of the slice: x: 2, y: 2, z: 4, core: 2. Of those that a mesh axis runs over, the one named last changes fastest.
Arguments:
- features: bfloat16 [4096, 2048], P('col', 'row'), may hold values from -6 to 6
- weight: bfloat16 [2048, 2048], replicated, may hold values from -0.125 to 0.125
- bias: bfloat16 [2048], replicated, may hold values from -3 to 3
- self_scale: float32 [4096], P('row'), may hold values from 0.5 to 2
- adj_tiles: bfloat16 [16, 2, 32, 128, 128], P('row', 'col'), may hold values from 0 to 1, as said below
- tile_ids: int32 [16, 2, 32], P('row', 'col'), may hold values from 0 to 31, as said below
- tile_counts: int32 [16, 2], P('row', 'col'), may hold values from 4 to 32, as said below
- cotangent: bfloat16 [4096, 2048], P(('row', 'col')), may hold values from -6 to 6
Outputs:
- outputs: float32 [4096, 2048], P(('row', 'col'))
- d_features: float32 [4096, 2048], P('col', 'row')
- d_weight: float32 [2048, 2048], replicated
- d_bias: float32 [2048], replicated
The draws below stay inside these ranges and needn't reach their ends.
Inputs may be any that keep to these rules, and one draw needn't show every extreme that they name: `adj_tiles`: entries are non-negative. `tile_ids`: within a block all 32 ids differ, live or not. `tile_counts`: some block is full in every draw.
All inputs are finite; a program needn't handle non-finite values.
Results may differ from the reference program's by a relative error of at most 0.0055.
Values may be sent and summed in bfloat16 or wider, within the bound.
A program may use at most 320 MiB of HBM per device.

```python
import math
import jax
import jax.numpy as jnp
from jax import lax

F = 2048
NODES = 4096
ROW_BLOCK = 256
COL_BLOCK = 2048
TILE_ROWS = 2
TILE_COLS = 16
MAXT = 32
RB = 16
CB = 2


def draw_adj_tiles(key, part):
    entries = max(1, MAXT * 16384 * CB * 2 // (5 * ROW_BLOCK))
    upper_end = (5.0 / entries) ** 0.5
    uniform_draw = jax.random.uniform(key, (RB, CB, MAXT, 128, 128), jnp.float32)
    values = uniform_draw * upper_end
    return values.astype(jnp.bfloat16)


def draw_tile_ids(key, part):
    block_keys = jax.random.split(jax.random.fold_in(key, 11), RB * CB)
    chosen = jax.vmap(lambda one_key: jax.random.permutation(one_key, TILE_ROWS * TILE_COLS)[:MAXT])(block_keys)
    return chosen.reshape(RB, CB, MAXT).astype(jnp.int32)


def draw_tile_counts(key, part):
    light_key = jax.random.fold_in(key, 21)
    heavy_key = jax.random.fold_in(key, 22)
    forced_key = jax.random.fold_in(key, 23)
    light = jax.random.randint(light_key, (RB * CB,), max(1, MAXT // 8), MAXT // 2 + 1)
    heavy = jax.random.randint(heavy_key, (RB * CB,), 0, 8) == 0
    forced = jax.random.randint(forced_key, (), 0, RB * CB)
    position = jnp.arange(RB * CB, dtype=jnp.int32)
    counts = jnp.where(heavy | (position == forced), MAXT, light)
    return counts.reshape(RB, CB).astype(jnp.int32)


def block_levels(rng, shape, cuts, low, high):
    loudness = 1.0
    for axis_at, blocks in cuts:
        steps = jax.random.uniform(jax.random.fold_in(jax.random.fold_in(rng, 6), axis_at), (blocks,), jnp.float32, low / len(cuts), high / len(cuts))
        loudness = loudness * jnp.repeat(jnp.exp(steps), shape[axis_at] // blocks).reshape((-1,) + (1,) * (len(shape) - 1 - axis_at))
    return loudness


def bell_draw(rng, extent, scale, bound, cuts=(), kind=jnp.bfloat16):
    values = scale * jax.random.normal(rng, extent, jnp.float32)
    if cuts:
        values = values * block_levels(rng, extent, cuts, -0.22, 0.18)
    return jnp.clip(values, -bound, bound).astype(kind)


def setup_inputs(seed: int = 0) -> dict:
    keys = jax.random.split(jax.random.key(seed), 9)
    return {
        "features": bell_draw(keys[0], (NODES, F), 1.0, 6.0, ((0, 2), (1, 16))),
        "weight": bell_draw(keys[1], (F, F), F ** -0.5, 0.125),
        "bias": bell_draw(keys[2], (F,), 0.5, 3.0),
        "self_scale": jnp.clip(jnp.exp(math.log(2.0) - 1.3862944 * jax.random.uniform(keys[3], (NODES,), jnp.float32) ** block_levels(keys[3], (NODES,), ((0, 16),), -0.2, 0.2)), 0.5, 2.0),
        "adj_tiles": draw_adj_tiles(jax.random.fold_in(keys[8], 71), 0),
        "tile_ids": draw_tile_ids(jax.random.fold_in(keys[8], 71), 0),
        "tile_counts": draw_tile_counts(jax.random.fold_in(keys[8], 71), 0),
        "cotangent": bell_draw(keys[7], (NODES, F), 1.0, 6.0, ((0, 32),)),
    }


@jax.custom_vjp
def low(v):
    return lax.optimization_barrier(v.astype(jnp.bfloat16)).astype(jnp.float32)

@jax.custom_vjp
def low_back(v):
    return v

def low_keep(v):
    return (low(v), None)

def low_pass(kept, grad):
    return (grad,)

def back_keep(v):
    return (v, None)

def back_low(kept, grad):
    return (low(grad),)
low.defvjp(low_keep, low_pass)
low_back.defvjp(back_keep, back_low)

def reference(features, weight, bias, self_scale, adj_tiles, tile_ids, tile_counts, cotangent):
    feats = features.astype(jnp.float32)
    weight_val = weight.astype(jnp.float32)
    bias_val = bias.astype(jnp.float32)
    grad_out = cotangent.astype(jnp.float32)
    scale_val = self_scale.astype(jnp.float32)
    slot_index = jnp.arange(MAXT, dtype=jnp.int32)

    def aggregate(source):

        def one_block(row_no):
            row_no = row_no.astype(jnp.int32)
            running = jnp.zeros((TILE_ROWS, 128, F), source.dtype)
            for col_no in range(CB):
                column = lax.dynamic_slice_in_dim(source, col_no * COL_BLOCK, COL_BLOCK, 0).reshape(TILE_COLS, 128, F)
                tile_list = tile_ids[row_no, col_no].astype(jnp.int32)
                live_slot = (slot_index < tile_counts[row_no, col_no].astype(jnp.int32)).astype(source.dtype)
                tile_set = adj_tiles[row_no, col_no].astype(source.dtype) * live_slot[:, None, None]
                col_pick = (tile_list % TILE_COLS).astype(jnp.int32)
                row_pick = (tile_list // TILE_COLS).astype(jnp.int32)
                pieces = jnp.take(column, col_pick, axis=0)
                products = jnp.einsum('tij,tjf->tif', tile_set, pieces, precision=lax.Precision.HIGHEST)
                running = running.at[row_pick].add(products)
            first_row = (row_no * ROW_BLOCK).astype(jnp.int32)
            own_rows = lax.dynamic_slice_in_dim(source, first_row, ROW_BLOCK, 0)
            self_rows = lax.dynamic_slice_in_dim(scale_val, first_row, ROW_BLOCK, 0).astype(source.dtype)
            return running.reshape(ROW_BLOCK, F) + self_rows[:, None] * own_rows
        blocks = lax.map(jax.checkpoint(one_block), jnp.arange(RB, dtype=jnp.int32))
        return blocks.reshape(NODES, F)

    def forward(source, weight_in, bias_in):
        aggregated = aggregate(source)
        layer_in = low(low_back(aggregated))
        pre_act = low_back(jnp.dot(layer_in, weight_in, precision=lax.Precision.HIGHEST) + bias_in)
        return pre_act * jax.nn.sigmoid(pre_act)
    result, pull = jax.vjp(forward, feats, weight_val, bias_val)
    d_features, d_weight, d_bias = pull(grad_out)
    return (result, d_features, d_weight, d_bias)
```

```python
import jax
import jax.numpy as jnp
from jax import lax
from jax.experimental import pallas as pl
from jax.experimental.pallas import tpu as pltpu
from jax.sharding import PartitionSpec as P

MESH = pl.DeviceIdType.MESH
F32 = jnp.float32
BF16 = jnp.bfloat16
MIB = 2**20


def dense_block(tiles, ids, count, tile_rows, tile_cols):
    slots = jnp.arange(tiles.shape[0], dtype=jnp.int32)
    live = jnp.where((slots < count)[:, None, None], tiles, jnp.zeros_like(tiles))
    blank = jnp.zeros((tile_rows * tile_cols, 128, 128), tiles.dtype)
    placed = blank.at[ids].add(live, unique_indices=True)
    placed = placed.reshape(tile_rows, tile_cols, 128, 128)
    return placed.transpose(0, 2, 1, 3).reshape(tile_rows * 128, tile_cols * 128)


def per_device_any(features, weight, bias, self_scale, adj_tiles, tile_ids, tile_counts, cotangent):
    row_block = self_scale.shape[0]
    col_block = features.shape[0]
    block = dense_block(
        adj_tiles[0, 0], tile_ids[0, 0], tile_counts[0, 0], row_block // 128, col_block // 128
    )
    start_row = lax.axis_index("row") * row_block
    col_no = lax.axis_index("col")
    inside = col_no == start_row // col_block
    offset = jnp.where(inside, start_row - col_no * col_block, 0)
    self_rows = jnp.where(inside, self_scale, 0.0)[:, None]
    piece = lax.all_gather(features, "row", axis=1, tiled=True)
    terms = jnp.dot(block, piece, preferred_element_type=F32)
    terms = terms + self_rows * lax.dynamic_slice_in_dim(piece, offset, row_block, 0)
    layer_in = lax.psum_scatter(terms, "col", scatter_dimension=0, tiled=True).astype(BF16)
    pre_act = jnp.dot(layer_in, weight, preferred_element_type=F32) + bias.astype(F32)
    sig = jax.nn.sigmoid(pre_act)
    outputs = pre_act * sig
    slope = sig * (1.0 + pre_act * (1.0 - sig))
    d_pre = (cotangent.astype(F32) * slope).astype(BF16)
    d_weight = lax.dot_general(
        layer_in, d_pre, (((0,), (0,)), ((), ())), preferred_element_type=F32
    )
    d_bias = jnp.sum(d_pre.astype(F32), axis=0)
    d_weight, d_bias = lax.psum((d_weight, d_bias), ("row", "col"))
    d_layer = lax.dot_general(
        d_pre, weight, (((1,), (1,)), ((), ())), preferred_element_type=F32
    ).astype(BF16)
    whole = lax.all_gather(d_layer, "col", axis=0, tiled=True)
    spread = lax.dot_general(block, whole, (((0,), (0,)), ((), ())), preferred_element_type=F32)
    own = lax.dynamic_slice_in_dim(spread, offset, row_block, 0) + self_rows * whole
    spread = lax.dynamic_update_slice_in_dim(spread, own, offset, 0)
    d_features = lax.psum_scatter(spread, "row", scatter_dimension=1, tiled=True)
    return outputs, d_features, d_weight, d_bias


def fused_kernel(
    slot_ref, live_ref, tiles_ref, feat_ref, w_ref, bias_ref, scale_ref, cot_ref,
    out_ref, dfeat_ref, dw_ref, db_ref,
    adj, hid, wv, sbuf, scol, xs, xr, keep, lay, xrow, pre, pt, ptg, dls, dlq,
    dwf, dwp, dwr, fw, dff, dfp, agg, fin, bsum, ssem, rsem, lsem,
):
    r = lax.axis_index("row")
    x = lax.axis_index("col")
    z = r // 4
    y = (r // 2) % 2
    k = r % 2
    q = 2 * y + k
    ends = (z == 0) | (z == 3)
    mids = (z == 1) | (z == 2)

    def at(xx, yy, zz, kk):
        return (zz * 4 + yy * 2 + kk, xx)

    sib = at(x, y, z, 1 - k)
    xn = at(1 - x, y, z, k)
    yn = at(x, 1 - y, z, k)
    dg = at(x, 1 - y, z, 1 - k)
    zr = at(x, y, jnp.minimum(z + 1, 3), k)
    zl = at(x, y, jnp.maximum(z - 1, 0), k)
    q_y = 2 * (1 - y) + k
    q_s = 2 * y + 1 - k
    q_d = 3 - q

    count = [0]
    sent = []

    def new():
        count[0] += 1
        return count[0] - 1

    def when(cond, fn):
        if cond is None:
            fn()
        else:
            pl.when(cond)(fn)

    def copy(i, src, dst, to):
        return pltpu.make_async_remote_copy(
            src_ref=src, dst_ref=dst, send_sem=ssem.at[i], recv_sem=rsem.at[i],
            device_id=to, device_id_type=MESH,
        )

    def send(i, src, dst, to, cond=None):
        c = copy(i, src, dst, to)
        when(cond, c.start)
        sent.append((c, cond))

    def recv(i, dst, cond=None):
        c = copy(i, dst, dst, sib)
        when(cond, c.wait_recv)

    def slice_at(o):
        return [z, z + 1 - 2 * (z % 2), 2 - z // 2, 3 - 3 * (z // 2)][o]

    def mult(v, n):
        return pl.multiple_of(v, n)

    barrier = pltpu.get_barrier_semaphore()
    peers = [at(xx, yy, z, kk) for xx, yy, kk in (
        (x, y, 1 - k), (x, 1 - y, k), (x, 1 - y, 1 - k), (1 - x, y, k),
        (1 - x, y, 1 - k), (1 - x, 1 - y, k), (1 - x, 1 - y, 1 - k))]
    peers += [at(x, y, (z + d) % 4, k) for d in (1, 2, 3)]
    for peer in peers:
        pl.semaphore_signal(barrier, inc=1, device_id=peer, device_id_type=MESH)

    w_copy = pltpu.make_async_copy(w_ref, wv, lsem.at[0])
    h_copy = pltpu.make_async_copy(feat_ref, hid.at[z], lsem.at[1])
    h_copy.start()

    for c in range(2):
        @pl.loop(0, 16)
        def _(t, c=c):
            p = c * 16 + t
            tile = tiles_ref[slot_ref[p]].astype(F32) * live_ref[p]
            adj[pl.ds(mult(c * 512 + q * 128, 128), 128), pl.ds(mult(t * 128, 128), 128)] = (
                tile.astype(BF16)
            )
    for i in range(4):
        sbuf[q, 2 * i:2 * i + 2, :] = scale_ref[...]
    h_copy.wait()
    w_copy.start()
    pl.semaphore_wait(barrier, len(peers))

    def h_part(s, c):
        return hid.at[s, pl.ds(c * 1024, 1024)]

    right = {(d, c): new() for d in (1, 2, 3) for c in (0, 1)}
    left = {(d, c): new() for d in (1, 2, 3) for c in (0, 1)}

    def line_send(ids, part, d, c, own_ok=True):
        sr, sl = jnp.maximum(z - (d - 1), 0), jnp.minimum(z + d - 1, 3)
        send(ids[0][d, c], part(sr, c), part(sr, c), zr, (z >= d - 1) & (z <= 2))
        send(ids[1][d, c], part(sl, c), part(sl, c), zl, (z <= 4 - d) & (z >= 1))

    def line_recv(ids, part, d, c):
        sr, sl = jnp.maximum(z - d, 0), jnp.minimum(z + d, 3)
        recv(ids[0][d, c], part(sr, c), z >= d)
        recv(ids[1][d, c], part(sl, c), z <= 3 - d)

    hz = (right, left)
    line_send(hz, h_part, 1, 0)
    line_send(hz, h_part, 1, 1)

    s_id = [new() for _ in range(3)]
    for i, to in zip(s_id, (yn, sib, dg)):
        send(i, sbuf.at[q], sbuf.at[q], to)

    def a_part(qq, c):
        return adj.at[pl.ds(mult(c * 512 + qq * 128, 128), 128)]

    ay = [new() for _ in range(2)]
    asib = [new() for _ in range(2)]
    afwd = [new() for _ in range(2)]
    for c in range(2):
        send(ay[c], a_part(q, c), a_part(q, c), yn)
    for c in range(2):
        send(asib[c], a_part(q, c), a_part(q, c), sib)

    line_recv(hz, h_part, 1, 0)
    line_send(hz, h_part, 2, 0)
    line_recv(hz, h_part, 1, 1)
    line_send(hz, h_part, 2, 1)
    recv(ay[0], a_part(q_y, 0))
    send(afwd[0], a_part(q_y, 0), a_part(q_y, 0), sib)

    for i, qq in zip(s_id, (q_y, q_s, q_d)):
        recv(i, sbuf.at[qq])
    inside = jnp.where(x == z // 2, 1.0, 0.0)
    for b in range(8):
        row = sbuf[b % 4, b // 4:b // 4 + 1, :] * inside
        scol[b] = jnp.broadcast_to(row, (128, 128)).T

    line_recv(hz, h_part, 2, 0)
    line_send(hz, h_part, 3, 0)
    line_recv(hz, h_part, 2, 1)
    line_send(hz, h_part, 3, 1)
    recv(ay[1], a_part(q_y, 1))
    send(afwd[1], a_part(q_y, 1), a_part(q_y, 1), sib)
    for c in range(2):
        recv(asib[c], a_part(q_s, c))
    for c in range(2):
        recv(afwd[c], a_part(q_d, c))

    x_id = [new() for _ in range(4)]
    l_id = [new() for _ in range(4)]
    row_id = [[new() for _ in range(3)] for _ in range(4)]
    w_waited = []

    def aggregate(o):
        s = slice_at(o)
        for c, sending in ((1 - x, True), (x, False)):
            acc = jnp.dot(
                adj[pl.ds(mult(c * 512, 512), 512), :], hid[s], preferred_element_type=F32
            )
            own = []
            for qq in range(4):
                first = mult((z % 2) * 1024 + qq * 256 + c * 128, 128)
                own.append(scol[c * 4 + qq] * hid[s, pl.ds(first, 128), :].astype(F32))
            acc = acc + jnp.concatenate(own, axis=0)
            if sending:
                xs[o] = acc.astype(BF16)
                send(x_id[o], xs.at[o], xr.at[o], xn)
            else:
                keep[o] = acc

    def combine(o):
        s = slice_at(o)
        recv(x_id[o], xr.at[o])
        mine = pl.ds(mult(x * 512, 512), 512)
        lay[s, mine, :] = (keep[o] + xr[o].astype(F32)).astype(BF16)
        for i, qq, to in zip(row_id[o], (q_y, q_d, q_s), (yn, dg, sib)):
            rows = pl.ds(mult(x * 512 + qq * 128, 128), 128)
            send(i, lay.at[s, rows], xrow.at[s * 4 + q], to)
        send(l_id[o], lay.at[s, mine], lay.at[s, mine], xn)
        xrow[s * 4 + q] = lay[s, pl.ds(mult(x * 512 + q * 128, 128), 128), :]

    def linear(o):
        s = slice_at(o)
        for i, qq in zip(row_id[o], (q_y, q_d, q_s)):
            recv(i, xrow.at[s * 4 + qq])
        if not w_waited:
            w_copy.wait()
            w_waited.append(True)
        part = jnp.concatenate([xrow[s * 4 + i] for i in range(4)], axis=1)

        @pl.loop(0, 4)
        def _(t):
            cols = pl.ds(mult(t * 512, 512), 512)
            prod = jnp.dot(
                part, wv[pl.ds(mult(s * 512, 512), 512), cols], preferred_element_type=F32
            )
            if o == 0:
                pre[:, cols] = prod + bias_ref[:, cols]
            else:
                pre[:, cols] += prod

    aggregate(0)
    aggregate(1)
    combine(0)
    aggregate(2)
    combine(1)
    linear(0)
    combine(2)
    linear(1)
    line_recv(hz, h_part, 3, 0)
    line_recv(hz, h_part, 3, 1)
    aggregate(3)
    linear(2)
    combine(3)
    linear(3)

    @pl.loop(0, 16)
    def _(t):
        cols = pl.ds(mult(t * 128, 128), 128)
        v = pre[:, cols]
        sig = jax.nn.sigmoid(v)
        out_ref[:, cols] = v * sig
        slope = sig * (1.0 + v * (1.0 - sig))
        d = (cot_ref[:, cols].astype(F32) * slope).astype(BF16)
        d32 = d.astype(F32)
        pt[pl.ds(mult(t * 128, 128), 128), :] = d32.T.astype(BF16)
        bsum[0, pl.ds(t, 1), :] = jnp.sum(d32, axis=0, keepdims=True)

    def p_half(c):
        return pt.at[pl.ds(mult(c * 1024, 1024), 1024)]

    b_own, b_x = x * 4 + q, (1 - x) * 4 + q
    px, py, pyf, ps, psf, pd, pdf = (new() for _ in range(7))
    send(px, p_half(1 - x), ptg.at[b_own], xn)
    send(py, p_half(x), ptg.at[b_own], yn)
    send(ps, p_half(x), ptg.at[b_own], sib)
    b_ids = [new() for _ in range(6)]
    send(b_ids[0], bsum.at[0], bsum.at[1], xn)
    ptg[b_own] = pt[pl.ds(mult(x * 1024, 1024), 1024), :]

    dl_ids = [new() for _ in range(7)]
    dl_to = [
        (x, 1 - y, k), (x, 1 - y, 1 - k), (x, y, 1 - k),
        (1 - x, y, k), (1 - x, y, 1 - k), (1 - x, 1 - y, k), (1 - x, 1 - y, 1 - k),
    ]

    @pl.loop(0, 4)
    def _(s):
        acc = jnp.dot(
            wv[pl.ds(mult(s * 512, 512), 512), :], pt[...], preferred_element_type=F32
        ).astype(BF16)
        for qq in range(4):
            dls[qq, s] = acc[qq * 128:(qq + 1) * 128]

    recv(px, ptg.at[b_x])
    send(pyf, ptg.at[b_x], ptg.at[b_x], yn)
    for i, (xx, yy, kk) in zip(dl_ids, dl_to):
        send(i, dls.at[2 * yy + kk], dlq.at[b_own], at(xx, yy, z, kk))
    send(psf, ptg.at[b_x], ptg.at[b_x], sib)
    recv(b_ids[0], bsum.at[1])
    bsum[2] = bsum[0] + bsum[1]
    send(b_ids[1], bsum.at[2], bsum.at[3], yn)
    dlq[b_own] = dls[q]
    recv(py, ptg.at[x * 4 + q_y])
    send(pd, ptg.at[x * 4 + q_y], ptg.at[x * 4 + q_y], sib)
    recv(b_ids[1], bsum.at[3])
    bsum[4] = bsum[2] + bsum[3]
    send(b_ids[2], bsum.at[4], bsum.at[5], sib)
    recv(pyf, ptg.at[(1 - x) * 4 + q_y])
    send(pdf, ptg.at[(1 - x) * 4 + q_y], ptg.at[(1 - x) * 4 + q_y], sib)
    recv(ps, ptg.at[x * 4 + q_s])
    recv(psf, ptg.at[(1 - x) * 4 + q_s])
    recv(pd, ptg.at[x * 4 + q_d])
    recv(pdf, ptg.at[(1 - x) * 4 + q_d])
    for o in range(4):
        recv(l_id[o], lay.at[slice_at(o), pl.ds(mult((1 - x) * 512, 512), 512)])

    dw_ids = [[new() for _ in range(3)] for _ in range(2)]
    for h in range(2):
        rows = pl.ds(h * 512, 512)
        lhs = jnp.concatenate([ptg[b, rows, :] for b in range(8)], axis=1)
        rhs = jnp.concatenate([lay[s] for s in range(4)], axis=1)
        acc = jnp.dot(lhs, rhs, preferred_element_type=F32)
        for s in range(4):
            dwf[s, rows, :] = acc[:, s * 128:(s + 1) * 128]
            dwp[s, rows, :] = acc[:, s * 128:(s + 1) * 128].astype(BF16)
        for d in (2, 1, 3):
            to = (z + d) % 4
            send(dw_ids[h][d - 1], dwp.at[to, rows], dwr.at[z, rows], at(x, y, to, k))
    recv(b_ids[2], bsum.at[5])
    bsum[6] = bsum[4] + bsum[5]
    for d in (1, 2, 3):
        send(b_ids[2 + d], bsum.at[6], bsum.at[6 + d], at(x, y, (z + d) % 4, k))

    for i, (xx, yy, kk) in zip(dl_ids, dl_to):
        recv(i, dlq.at[xx * 4 + 2 * yy + kk])

    pair = z // 2
    e, m = 3 * pair, 1 + pair
    e2, m2 = 3 - 3 * pair, 2 - pair
    f_ids = [new() for _ in range(6)]

    def input_grad(first):
        lhs = jnp.concatenate(
            [dlq[b, pl.ds(first, 2)].reshape(256, 128) for b in range(8)], axis=1
        )

        @pl.loop(0, 8)
        def _(t):
            cols = pl.ds(mult(t * 256, 256), 256)
            acc = jnp.dot(lhs, adj[:, cols], preferred_element_type=F32)
            qq = t % 4
            own = jnp.where((x == z // 2) & (t // 4 == z % 2), 1.0, 0.0)
            diag = []
            for c in range(2):
                row = sbuf[qq, c:c + 1, :] * own
                diag.append(dlq[c * 4 + qq, pl.ds(first, 2)].reshape(256, 128).astype(F32) * row)
            acc = acc + jnp.concatenate(diag, axis=1)
            for i in range(2):
                dff[first + i, :, cols] = acc[i * 128:(i + 1) * 128]
                dfp[first + i, :, cols] = acc[i * 128:(i + 1) * 128].astype(BF16)

    mid_dev, end_dev = at(x, y, m, k), at(x, y, e, k)
    input_grad(2 * (1 - pair))
    send(f_ids[0], dfp.at[m2], agg.at[0], mid_dev, ends)
    send(f_ids[1], dfp.at[e2], agg.at[1], mid_dev, ends)
    input_grad(2 * pair)
    send(f_ids[2], dfp.at[m], fin.at[0], mid_dev, ends)
    send(f_ids[3], dfp.at[e], fin.at[0], end_dev, mids)

    for h in range(2):
        rows = pl.ds(h * 512, 512)
        for d in (1, 2, 3):
            recv(dw_ids[h][d - 1], dwr.at[(z - d) % 4, rows])
        for t in range(4):
            rr = pl.ds(h * 512 + t * 128, 128)
            tot = dwf[z, rr, :]
            for d in (1, 2, 3):
                tot = tot + dwr[(z + d) % 4, rr, :].astype(F32)
            fw[:, rr] = tot.T.astype(BF16)
    for d in (1, 2, 3):
        recv(b_ids[2 + d], bsum.at[6 + d])
    db_ref[...] = bsum[6] + bsum[7] + bsum[8] + bsum[9]

    def piece(s, qq, c, first=0, rows=128):
        return dw_ref.at[
            pl.ds(mult(s * 512 + qq * 128 + first, 64), rows), pl.ds(mult(c * 1024, 1024), 1024)
        ]

    own_copy = pltpu.make_async_copy(fw, piece(z, q, x), lsem.at[2])
    own_copy.start()
    gz = ({(d, 0): new() for d in (1, 2, 3)}, {(d, 0): new() for d in (1, 2, 3)})
    gx, gy, gs, gxy, gyx, gsx, gsy, gsd1, gsd2 = (
        [new() for _ in range(4)] for _ in range(9)
    )

    def z_piece(s, c):
        return piece(s, q, x)

    send(gz[0][1, 0], fw, piece(z, q, x), zr, z <= 2)
    send(gz[1][1, 0], fw, piece(z, q, x), zl, z >= 1)

    def spread(o):
        s = slice_at(o)
        src = fw if o == 0 else piece(s, q, x)
        send(gx[o], src, piece(s, q, x), xn)
        send(gy[o], src, piece(s, q, x), yn)
        send(gs[o], src, piece(s, q, x), sib)

    def relay(o):
        s = slice_at(o)
        from_x, from_y = piece(s, q, 1 - x), piece(s, q_y, x)
        recv(gx[o], from_x)
        top = piece(s, q, 1 - x, 0, 64)
        send(gxy[o], top, top, yn)
        send(gsx[o], from_x, from_x, sib)
        recv(gy[o], from_y)
        low = piece(s, q_y, x, 64, 64)
        send(gyx[o], low, low, xn)
        send(gsy[o], from_y, from_y, sib)

    def relay_diag(o):
        s = slice_at(o)
        top = piece(s, q_y, 1 - x, 0, 64)
        recv(gxy[o], top)
        send(gsd1[o], top, top, sib)
        low = piece(s, q_y, 1 - x, 64, 64)
        recv(gyx[o], low)
        send(gsd2[o], low, low, sib)

    def last(o):
        s = slice_at(o)
        recv(gs[o], piece(s, q_s, x))
        recv(gsx[o], piece(s, q_s, 1 - x))
        recv(gsy[o], piece(s, q_d, x))
        recv(gsd1[o], piece(s, q_d, 1 - x, 0, 64))
        recv(gsd2[o], piece(s, q_d, 1 - x, 64, 64))

    spread(0)

    for j, (s_to, to) in enumerate(((m2, at(x, y, m2, k)), (e2, at(x, y, e2, k)))):
        recv(f_ids[j], agg.at[j], mids)

        @pl.when(mids)
        def _(j=j, s_to=s_to):
            dfp[s_to] = (dff[s_to] + agg[j].astype(F32)).astype(BF16)
        send(f_ids[4 + j], dfp.at[s_to], fin.at[1], to, mids)

    line_recv(gz, z_piece, 1, 0)
    line_send(gz, z_piece, 2, 0)
    spread(1)
    relay(0)
    line_recv(gz, z_piece, 2, 0)
    line_send(gz, z_piece, 3, 0)
    spread(2)
    relay(1)
    relay_diag(0)
    line_recv(gz, z_piece, 3, 0)
    spread(3)
    relay(2)
    relay_diag(1)

    recv(f_ids[2], fin.at[0], mids)
    recv(f_ids[3], fin.at[0], ends)
    recv(f_ids[4], fin.at[1], mids)
    recv(f_ids[5], fin.at[1], ends)

    @pl.loop(0, 16)
    def _(t):
        cols = pl.ds(mult(t * 128, 128), 128)
        tot = dff[z, :, cols] + fin[0, :, cols].astype(F32) + fin[1, :, cols].astype(F32)
        dfeat_ref[pl.ds(mult(t * 128, 128), 128), :] = tot.T

    relay(3)
    relay_diag(2)
    relay_diag(3)
    for o in range(4):
        last(o)
    own_copy.wait()
    for c, cond in sent:
        when(cond, c.wait_send)


N_SEMS = 140


def per_device_fused(features, weight, bias, self_scale, adj_tiles, tile_ids, tile_counts, cotangent):
    ids = tile_ids[0, 0]
    slots = jnp.arange(32, dtype=jnp.int32)
    hit = ids[None, :] == slots[:, None]
    slot_of = jnp.sum(jnp.where(hit, slots[None, :], 0), axis=1)
    live = (slot_of < tile_counts[0, 0]).astype(F32)
    vmem = pl.BlockSpec(memory_space=pltpu.VMEM)
    smem = pl.BlockSpec(memory_space=pltpu.SMEM)
    hbm = pl.BlockSpec(memory_space=pl.ANY)
    outputs, d_features, d_weight, d_bias = pl.pallas_call(
        fused_kernel,
        out_shape=(
            jax.ShapeDtypeStruct((128, 2048), F32),
            jax.ShapeDtypeStruct((2048, 128), F32),
            jax.ShapeDtypeStruct((2048, 2048), BF16),
            jax.ShapeDtypeStruct((16, 128), F32),
        ),
        in_specs=[smem, smem, vmem, hbm, hbm, vmem, vmem, vmem],
        out_specs=(vmem, vmem, hbm, vmem),
        scratch_shapes=[
            pltpu.VMEM((1024, 2048), BF16),
            pltpu.VMEM((4, 2048, 128), BF16),
            pltpu.VMEM((2048, 2048), BF16),
            pltpu.VMEM((4, 8, 128), F32),
            pltpu.VMEM((8, 128, 128), F32),
            pltpu.VMEM((4, 512, 128), BF16),
            pltpu.VMEM((4, 512, 128), BF16),
            pltpu.VMEM((4, 512, 128), F32),
            pltpu.VMEM((4, 1024, 128), BF16),
            pltpu.VMEM((16, 128, 128), BF16),
            pltpu.VMEM((128, 2048), F32),
            pltpu.VMEM((2048, 128), BF16),
            pltpu.VMEM((8, 1024, 128), BF16),
            pltpu.VMEM((4, 4, 128, 128), BF16),
            pltpu.VMEM((8, 4, 128, 128), BF16),
            pltpu.VMEM((4, 1024, 128), F32),
            pltpu.VMEM((4, 1024, 128), BF16),
            pltpu.VMEM((4, 1024, 128), BF16),
            pltpu.VMEM((128, 1024), BF16),
            pltpu.VMEM((4, 128, 2048), F32),
            pltpu.VMEM((4, 128, 2048), BF16),
            pltpu.VMEM((2, 128, 2048), BF16),
            pltpu.VMEM((2, 128, 2048), BF16),
            pltpu.VMEM((10, 16, 128), F32),
            pltpu.SemaphoreType.DMA((N_SEMS,)),
            pltpu.SemaphoreType.DMA((N_SEMS,)),
            pltpu.SemaphoreType.DMA((3,)),
        ],
        compiler_params=pltpu.CompilerParams(
            collective_id=0, has_side_effects=True, vmem_limit_bytes=62 * MIB
        ),
        cost_estimate=pl.CostEstimate(
            flops=7_600_000_000, bytes_accessed=24 * MIB, transcendentals=262144
        ),
    )(
        slot_of, live, adj_tiles[0, 0], features, weight,
        bias.astype(F32).reshape(1, 2048), self_scale.reshape(2, 128), cotangent,
    )
    return outputs, d_features, d_weight.astype(F32), d_bias.reshape(2048)


def solution(mesh):
    fits = dict(mesh.shape) == {"row": 16, "col": 2}

    def run(*arrays):
        fused = fits and arrays[0].shape == (4096, 2048) and arrays[4].shape[2] == 32
        return jax.shard_map(
            per_device_fused if fused else per_device_any,
            mesh=mesh,
            in_specs=(
                P("col", "row"),
                P(),
                P(),
                P("row"),
                P("row", "col", None, None, None),
                P("row", "col", None),
                P("row", "col"),
                P(("row", "col"), None),
            ),
            out_specs=(P(("row", "col"), None), P("col", "row"), P(), P()),
            check_vma=False,
        )(*arrays)

    return run
```

```python
import jax
import jax.numpy as jnp
from jax import lax
from jax.experimental import pallas as pl
from jax.experimental.pallas import tpu as pltpu
from jax.sharding import PartitionSpec as P

MESH = pl.DeviceIdType.MESH
F32 = jnp.float32
BF16 = jnp.bfloat16
MIB = 2**20


def dense_block(tiles, ids, count, tile_rows, tile_cols):
    slots = jnp.arange(tiles.shape[0], dtype=jnp.int32)
    live = jnp.where((slots < count)[:, None, None], tiles, jnp.zeros_like(tiles))
    blank = jnp.zeros((tile_rows * tile_cols, 128, 128), tiles.dtype)
    placed = blank.at[ids].add(live, unique_indices=True)
    placed = placed.reshape(tile_rows, tile_cols, 128, 128)
    return placed.transpose(0, 2, 1, 3).reshape(tile_rows * 128, tile_cols * 128)


def per_device_any(features, weight, bias, self_scale, adj_tiles, tile_ids, tile_counts, cotangent):
    row_block = self_scale.shape[0]
    col_block = features.shape[0]
    block = dense_block(
        adj_tiles[0, 0], tile_ids[0, 0], tile_counts[0, 0], row_block // 128, col_block // 128
    )
    start_row = lax.axis_index("row") * row_block
    col_no = lax.axis_index("col")
    inside = col_no == start_row // col_block
    offset = jnp.where(inside, start_row - col_no * col_block, 0)
    self_rows = jnp.where(inside, self_scale, 0.0)[:, None]
    piece = lax.all_gather(features, "row", axis=1, tiled=True)
    terms = jnp.dot(block, piece, preferred_element_type=F32)
    terms = terms + self_rows * lax.dynamic_slice_in_dim(piece, offset, row_block, 0)
    layer_in = lax.psum_scatter(terms, "col", scatter_dimension=0, tiled=True).astype(BF16)
    pre_act = jnp.dot(layer_in, weight, preferred_element_type=F32) + bias.astype(F32)
    sig = jax.nn.sigmoid(pre_act)
    outputs = pre_act * sig
    slope = sig * (1.0 + pre_act * (1.0 - sig))
    d_pre = (cotangent.astype(F32) * slope).astype(BF16)
    d_weight = lax.dot_general(
        layer_in, d_pre, (((0,), (0,)), ((), ())), preferred_element_type=F32
    )
    d_bias = jnp.sum(d_pre.astype(F32), axis=0)
    d_weight, d_bias = lax.psum((d_weight, d_bias), ("row", "col"))
    d_layer = lax.dot_general(
        d_pre, weight, (((1,), (1,)), ((), ())), preferred_element_type=F32
    ).astype(BF16)
    whole = lax.all_gather(d_layer, "col", axis=0, tiled=True)
    spread = lax.dot_general(block, whole, (((0,), (0,)), ((), ())), preferred_element_type=F32)
    own = lax.dynamic_slice_in_dim(spread, offset, row_block, 0) + self_rows * whole
    spread = lax.dynamic_update_slice_in_dim(spread, own, offset, 0)
    d_features = lax.psum_scatter(spread, "row", scatter_dimension=1, tiled=True)
    return outputs, d_features, d_weight, d_bias


def fused_kernel(
    ids_ref, count_ref, tiles_ref, feat_ref, w_ref, bias_ref, scale_ref, cot_ref,
    out_ref, dfeat_ref, dw_ref, db_ref,
    adj, hid, wv, sbuf, scol, xs, xr, keep, lay, xrow, pre, pt, ptg, dls, dlq,
    dwf, dwp, dwr, dff, dfp, agg, fin, bsum, ssem, rsem, lsem,
):
    r = lax.axis_index("row")
    x = lax.axis_index("col")
    z = r // 4
    y = (r // 2) % 2
    k = r % 2
    q = 2 * y + k
    ends = (z == 0) | (z == 3)
    mids = (z == 1) | (z == 2)

    def at(xx, yy, zz, kk):
        return (zz * 4 + yy * 2 + kk, xx)

    sib = at(x, y, z, 1 - k)
    xn = at(1 - x, y, z, k)
    yn = at(x, 1 - y, z, k)
    dg = at(x, 1 - y, z, 1 - k)
    zr = at(x, y, jnp.minimum(z + 1, 3), k)
    zl = at(x, y, jnp.maximum(z - 1, 0), k)
    q_y = 2 * (1 - y) + k
    q_s = 2 * y + 1 - k
    q_d = 3 - q

    count = [0]
    sent_by = {}
    pending = {}

    def new():
        count[0] += 1
        return count[0] - 1

    def when(cond, fn):
        if cond is None:
            fn()
        else:
            pl.when(cond)(fn)

    def copy(i, src, dst, to):
        return pltpu.make_async_remote_copy(
            src_ref=src, dst_ref=dst, send_sem=ssem.at[i], recv_sem=rsem.at[i],
            device_id=to, device_id_type=MESH,
        )

    def send(i, src, dst, to, cond=None, rcond=None):
        c = copy(i, src, dst, to)
        when(cond, c.start)
        sent_by[i] = (c, cond)
        pending[i] = (dst, rcond)

    def recv(i, dst, cond=None):
        pending.pop(i)
        c = copy(i, dst, dst, sib)
        when(cond, c.wait_recv)

    def slice_at(o):
        return [z, z + 1 - 2 * (z % 2), 2 - z // 2, 3 - 3 * (z // 2)][o]

    def mult(v, n):
        return pl.multiple_of(v, n)

    barrier = pltpu.get_barrier_semaphore()
    peers = [at(xx, yy, z, kk) for xx, yy, kk in (
        (x, y, 1 - k), (x, 1 - y, k), (x, 1 - y, 1 - k), (1 - x, y, k),
        (1 - x, y, 1 - k), (1 - x, 1 - y, k), (1 - x, 1 - y, 1 - k))]
    peers += [at(x, y, (z + d) % 4, k) for d in (1, 2, 3)]
    for peer in peers:
        pl.semaphore_signal(barrier, inc=1, device_id=peer, device_id_type=MESH)

    w_copy = pltpu.make_async_copy(w_ref, wv, lsem.at[0])
    h_copy = pltpu.make_async_copy(feat_ref, hid.at[z], lsem.at[1])
    h_copy.start()

    for c in range(2):
        @pl.loop(0, 16)
        def _(t, c=c):
            slot = jnp.int32(0)
            for i in range(32):
                slot = jnp.where(ids_ref[i] == c * 16 + t, i, slot)
            live = jnp.where(slot < count_ref[0], 1.0, 0.0)
            tile = tiles_ref[slot].astype(F32) * live
            adj[pl.ds(mult(c * 512 + q * 128, 128), 128), pl.ds(mult(t * 128, 128), 128)] = (
                tile.astype(BF16)
            )
    for i in range(4):
        sbuf[q, 2 * i:2 * i + 2, :] = scale_ref[...]
    h_copy.wait()
    w_copy.start()
    pl.semaphore_wait(barrier, len(peers))

    def h_part(s, c):
        return hid.at[s, pl.ds(c * 1024, 1024)]

    right = {(d, c): new() for d in (1, 2, 3) for c in (0, 1)}
    left = {(d, c): new() for d in (1, 2, 3) for c in (0, 1)}

    def line_send(ids, part, d, c, own_ok=True):
        sr, sl = jnp.maximum(z - (d - 1), 0), jnp.minimum(z + d - 1, 3)
        send(ids[0][d, c], part(sr, c), part(sr, c), zr, (z >= d - 1) & (z <= 2), z >= d)
        send(ids[1][d, c], part(sl, c), part(sl, c), zl, (z <= 4 - d) & (z >= 1), z <= 3 - d)

    def line_recv(ids, part, d, c):
        sr, sl = jnp.maximum(z - d, 0), jnp.minimum(z + d, 3)
        recv(ids[0][d, c], part(sr, c), z >= d)
        recv(ids[1][d, c], part(sl, c), z <= 3 - d)

    hz = (right, left)
    line_send(hz, h_part, 1, 0)
    line_send(hz, h_part, 1, 1)

    s_id = [new() for _ in range(3)]
    for i, to in zip(s_id, (yn, sib, dg)):
        send(i, sbuf.at[q], sbuf.at[q], to)

    def a_part(qq, c):
        return adj.at[pl.ds(mult(c * 512 + qq * 128, 128), 128)]

    ay = [new() for _ in range(2)]
    asib = [new() for _ in range(2)]
    afwd = [new() for _ in range(2)]
    for c in range(2):
        send(ay[c], a_part(q, c), a_part(q, c), yn)
    for c in range(2):
        send(asib[c], a_part(q, c), a_part(q, c), sib)

    line_recv(hz, h_part, 1, 0)
    line_send(hz, h_part, 2, 0)
    line_recv(hz, h_part, 1, 1)
    line_send(hz, h_part, 2, 1)
    recv(ay[0], a_part(q_y, 0))
    send(afwd[0], a_part(q_y, 0), a_part(q_y, 0), sib)

    for i, qq in zip(s_id, (q_y, q_s, q_d)):
        recv(i, sbuf.at[qq])
    inside = jnp.where(x == z // 2, 1.0, 0.0)
    for b in range(8):
        row = sbuf[b % 4, b // 4:b // 4 + 1, :] * inside
        scol[b] = jnp.broadcast_to(row, (128, 128)).T

    line_recv(hz, h_part, 2, 0)
    line_send(hz, h_part, 3, 0)
    line_recv(hz, h_part, 2, 1)
    line_send(hz, h_part, 3, 1)
    recv(ay[1], a_part(q_y, 1))
    send(afwd[1], a_part(q_y, 1), a_part(q_y, 1), sib)
    for c in range(2):
        recv(asib[c], a_part(q_s, c))
    for c in range(2):
        recv(afwd[c], a_part(q_d, c))

    x_id = [new() for _ in range(4)]
    l_id = [new() for _ in range(4)]
    row_id = [[new() for _ in range(3)] for _ in range(4)]
    w_waited = []

    def aggregate(o):
        s = slice_at(o)
        for c, sending in ((1 - x, True), (x, False)):
            acc = jnp.dot(
                adj[pl.ds(mult(c * 512, 512), 512), :], hid[s], preferred_element_type=F32
            )
            own = []
            for qq in range(4):
                first = mult((z % 2) * 1024 + qq * 256 + c * 128, 128)
                own.append(scol[c * 4 + qq] * hid[s, pl.ds(first, 128), :].astype(F32))
            acc = acc + jnp.concatenate(own, axis=0)
            if sending:
                xs[o] = acc.astype(BF16)
                send(x_id[o], xs.at[o], xr.at[o], xn)
            else:
                keep[o] = acc

    def combine(o):
        s = slice_at(o)
        recv(x_id[o], xr.at[o])
        mine = pl.ds(mult(x * 512, 512), 512)
        lay[s, mine, :] = (keep[o] + xr[o].astype(F32)).astype(BF16)
        for i, qq, to in zip(row_id[o], (q_y, q_d, q_s), (yn, dg, sib)):
            rows = pl.ds(mult(x * 512 + qq * 128, 128), 128)
            send(i, lay.at[s, rows], xrow.at[s * 4 + q], to)
        send(l_id[o], lay.at[s, mine], lay.at[s, mine], xn)
        xrow[s * 4 + q] = lay[s, pl.ds(mult(x * 512 + q * 128, 128), 128), :]

    def linear(o):
        s = slice_at(o)
        for i, qq in zip(row_id[o], (q_y, q_d, q_s)):
            recv(i, xrow.at[s * 4 + qq])
        if not w_waited:
            w_copy.wait()
            w_waited.append(True)
        part = jnp.concatenate([xrow[s * 4 + i] for i in range(4)], axis=1)

        @pl.loop(0, 4)
        def _(t):
            cols = pl.ds(mult(t * 512, 512), 512)
            prod = jnp.dot(
                part, wv[pl.ds(mult(s * 512, 512), 512), cols], preferred_element_type=F32
            )
            if o == 0:
                pre[:, cols] = prod + bias_ref[:, cols]
            else:
                pre[:, cols] += prod

    aggregate(0)
    aggregate(1)
    combine(0)
    aggregate(2)
    combine(1)
    linear(0)
    combine(2)
    linear(1)
    line_recv(hz, h_part, 3, 0)
    line_recv(hz, h_part, 3, 1)
    aggregate(3)
    linear(2)
    combine(3)
    linear(3)

    def p_half(c):
        return pt.at[pl.ds(mult(c * 1024, 1024), 1024)]

    def activate(c):
        @pl.loop(0, 8)
        def _(i):
            t = c * 8 + i
            cols = pl.ds(mult(t * 128, 128), 128)
            v = pre[:, cols]
            sig = jax.nn.sigmoid(v)
            out_ref[:, cols] = v * sig
            slope = sig * (1.0 + v * (1.0 - sig))
            d32 = (cot_ref[:, cols].astype(F32) * slope).astype(BF16).astype(F32)
            pt[pl.ds(mult(t * 128, 128), 128), :] = d32.T.astype(BF16)
            bsum[0, pl.ds(t, 1), :] = jnp.sum(d32, axis=0, keepdims=True)

    b_own, b_x = x * 4 + q, (1 - x) * 4 + q
    px, py, pyf, ps, psf, pd, pdf = (new() for _ in range(7))
    b_ids = [new() for _ in range(6)]
    activate(1 - x)
    send(px, p_half(1 - x), ptg.at[b_own], xn)
    activate(x)
    send(py, p_half(x), ptg.at[b_own], yn)
    send(ps, p_half(x), ptg.at[b_own], sib)
    send(b_ids[0], bsum.at[0], bsum.at[1], xn)
    ptg[b_own] = pt[pl.ds(mult(x * 1024, 1024), 1024), :]

    @pl.loop(0, 2)
    def _(i):
        acc = jnp.dot(
            wv[pl.ds(mult(i * 1024, 1024), 1024), :], pt[...], preferred_element_type=F32
        ).astype(BF16)
        for j in range(2):
            for qq in range(4):
                first = j * 512 + qq * 128
                dls[qq, i * 2 + j] = acc[first:first + 128]

    dl_to = [
        (1 - x, y, k), (1 - x, y, 1 - k), (x, y, 1 - k),
        (x, 1 - y, k), (x, 1 - y, 1 - k), (1 - x, 1 - y, k), (1 - x, 1 - y, 1 - k),
    ]
    dl_ids = [new() for _ in dl_to]

    def send_layer_grad(which):
        for i in which:
            xx, yy, kk = dl_to[i]
            send(dl_ids[i], dls.at[2 * yy + kk], dlq.at[b_own], at(xx, yy, z, kk))

    recv(px, ptg.at[b_x])
    send(pyf, ptg.at[b_x], ptg.at[b_x], yn)
    send_layer_grad((0, 1, 2))
    send(psf, ptg.at[b_x], ptg.at[b_x], sib)
    recv(b_ids[0], bsum.at[1])
    bsum[2] = bsum[0] + bsum[1]
    send(b_ids[1], bsum.at[2], bsum.at[3], yn)
    dlq[b_own] = dls[q]
    recv(py, ptg.at[x * 4 + q_y])
    send(pd, ptg.at[x * 4 + q_y], ptg.at[x * 4 + q_y], sib)
    recv(pyf, ptg.at[(1 - x) * 4 + q_y])
    send(pdf, ptg.at[(1 - x) * 4 + q_y], ptg.at[(1 - x) * 4 + q_y], sib)
    send_layer_grad((3, 4, 5, 6))
    recv(b_ids[1], bsum.at[3])
    bsum[4] = bsum[2] + bsum[3]
    send(b_ids[2], bsum.at[4], bsum.at[5], sib)
    recv(ps, ptg.at[x * 4 + q_s])
    recv(psf, ptg.at[(1 - x) * 4 + q_s])
    recv(pd, ptg.at[x * 4 + q_d])
    recv(pdf, ptg.at[(1 - x) * 4 + q_d])
    for o in range(4):
        recv(l_id[o], lay.at[slice_at(o), pl.ds(mult((1 - x) * 512, 512), 512)])

    dw_ids = [[new() for _ in range(3)] for _ in range(2)]
    for h in range(2):
        rows = pl.ds(h * 512, 512)
        lhs = jnp.concatenate([ptg[b, rows, :] for b in range(8)], axis=1)
        rhs = jnp.concatenate([lay[s] for s in range(4)], axis=1)
        acc = jnp.dot(lhs, rhs, preferred_element_type=F32)
        for s in range(4):
            dwf[s, rows, :] = acc[:, s * 128:(s + 1) * 128]
            dwp[s, rows, :] = acc[:, s * 128:(s + 1) * 128].astype(BF16)
        for d in (2, 1, 3):
            to = (z + d) % 4
            send(dw_ids[h][d - 1], dwp.at[to, rows], dwr.at[z, rows], at(x, y, to, k))
    recv(b_ids[2], bsum.at[5])
    bsum[6] = bsum[4] + bsum[5]
    for d in (1, 2, 3):
        send(b_ids[2 + d], bsum.at[6], bsum.at[6 + d], at(x, y, (z + d) % 4, k))

    for i, (xx, yy, kk) in zip(dl_ids, dl_to):
        recv(i, dlq.at[xx * 4 + 2 * yy + kk])

    pair = z // 2
    e, m = 3 * pair, 1 + pair
    e2, m2 = 3 - 3 * pair, 2 - pair
    f_in = [[new() for _ in range(2)] for _ in range(2)]
    f_out = [[new() for _ in range(2)] for _ in range(2)]
    f_fin = [new() for _ in range(2)]

    def input_grad(first):
        lhs = jnp.concatenate(
            [dlq[b, pl.ds(first, 2)].reshape(256, 128) for b in range(8)], axis=1
        )

        @pl.loop(0, 4)
        def _(t):
            cols = pl.ds(mult(t * 512, 512), 512)
            acc = jnp.dot(lhs, adj[:, cols], preferred_element_type=F32)
            own = jnp.where((x == z // 2) & (t // 2 == z % 2), 1.0, 0.0)
            diag = []
            for j in range(2):
                qq = (t % 2) * 2 + j
                for c in range(2):
                    row = sbuf[qq, c:c + 1, :] * own
                    diag.append(dlq[c * 4 + qq, pl.ds(first, 2)].reshape(256, 128).astype(F32) * row)
            acc = acc + jnp.concatenate(diag, axis=1)
            for i in range(2):
                dff[first + i, :, cols] = acc[i * 128:(i + 1) * 128]
                dfp[first + i, :, cols] = acc[i * 128:(i + 1) * 128].astype(BF16)

    mid_dev, end_dev = at(x, y, m, k), at(x, y, e, k)
    input_grad(2 * pair)
    send(f_fin[0], dfp.at[e], fin.at[0], end_dev, mids, ends)
    input_grad(2 * (1 - pair))

    def cut(c):
        return pl.ds(c * 1024, 1024)

    def end_send(j, c):
        s_to = (m2, e2)[j]
        send(f_in[j][c], dfp.at[s_to, :, cut(c)], agg.at[j, :, cut(c)], mid_dev, ends, mids)

    def end_wait(j, c):
        out, cond = sent_by.pop(f_in[j][c])
        pl.when(cond)(out.wait_send)

    def mid_send(j, c):
        s_to, to = ((m2, at(x, y, m2, k)), (e2, at(x, y, e2, k)))[j]
        recv(f_in[j][c], agg.at[j, :, cut(c)], mids)

        @pl.when(mids)
        def _():
            dfp[s_to, :, cut(c)] = (
                dff[s_to, :, cut(c)] + agg[j, :, cut(c)].astype(F32)
            ).astype(BF16)
        send(f_out[j][c], dfp.at[s_to, :, cut(c)], fin.at[1, :, cut(c)], to, mids, (mids, ends)[j])

    def piece(s, qq, c, h):
        return dw_ref.at[(s * 4 + qq) * 4 + c * 2 + h]

    gz = tuple({(d, h): new() for d in (1, 2, 3) for h in (0, 1)} for _ in range(2))
    gx, gy, gs, gxy, gyx, gsx, gsy, gsd1, gsd2 = (
        {(h, o): new() for h in (0, 1) for o in range(4)} for _ in range(9)
    )

    def z_piece(s, h):
        return piece(s, q, x, h)

    def finish(h):
        for d in (1, 2, 3):
            recv(dw_ids[h][d - 1], dwr.at[(z - d) % 4, pl.ds(h * 512, 512)])
        for t in range(4):
            rr = pl.ds(h * 512 + t * 128, 128)
            tot = dwf[z, rr, :]
            for d in (1, 2, 3):
                tot = tot + dwr[(z + d) % 4, rr, :].astype(F32)
            dw_ref[(z * 4 + q) * 4 + x * 2 + h, :, t * 128:(t + 1) * 128] = tot.T.astype(BF16)
        line_send(gz, z_piece, 1, h)
        spread(h, 0)

    def spread(h, o):
        src = piece(slice_at(o), q, x, h)
        send(gx[h, o], src, src, xn)
        send(gy[h, o], src, src, yn)
        send(gs[h, o], src, src, sib)

    def part(ref, i):
        return ref.at[pl.ds(i * 64, 64)]

    def relay(h, o):
        s = slice_at(o)
        from_x, from_y = piece(s, q, 1 - x, h), piece(s, q_y, x, h)
        recv(gx[h, o], from_x)
        send(gxy[h, o], part(from_x, 0), part(from_x, 0), yn)
        send(gsx[h, o], from_x, from_x, sib)
        recv(gy[h, o], from_y)
        send(gyx[h, o], part(from_y, 1), part(from_y, 1), xn)
        send(gsy[h, o], from_y, from_y, sib)

    def relay_diag(h, o):
        block = piece(slice_at(o), q_y, 1 - x, h)
        recv(gxy[h, o], part(block, 0))
        send(gsd1[h, o], part(block, 0), part(block, 0), sib)
        recv(gyx[h, o], part(block, 1))
        send(gsd2[h, o], part(block, 1), part(block, 1), sib)

    def last(h, o):
        s = slice_at(o)
        recv(gs[h, o], piece(s, q_s, x, h))
        recv(gsx[h, o], piece(s, q_s, 1 - x, h))
        recv(gsy[h, o], piece(s, q_d, x, h))
        block = piece(s, q_d, 1 - x, h)
        recv(gsd1[h, o], part(block, 0))
        recv(gsd2[h, o], part(block, 1))

    def along(h, d):
        line_recv(gz, z_piece, d, h)
        if d < 3:
            line_send(gz, z_piece, d + 1, h)
        spread(h, d)

    finish(0)
    along(0, 1)
    relay(0, 0)
    finish(1)
    end_send(0, 0)
    end_send(0, 1)
    along(0, 2)
    relay(0, 1)
    relay_diag(0, 0)
    along(1, 1)
    mid_send(0, 0)
    end_wait(0, 0)
    end_send(1, 0)
    relay(1, 0)
    relay_diag(0, 1)
    along(0, 3)
    mid_send(0, 1)
    end_wait(0, 1)
    end_send(1, 1)
    relay(0, 2)
    relay_diag(1, 0)
    along(1, 2)
    mid_send(1, 0)
    end_wait(1, 0)
    send(f_fin[1], dfp.at[m], fin.at[0], mid_dev, ends, mids)
    relay(1, 1)
    relay_diag(0, 2)
    along(1, 3)
    mid_send(1, 1)
    relay(0, 3)
    relay_diag(1, 1)
    relay(1, 2)
    relay_diag(0, 3)
    relay(1, 3)
    relay_diag(1, 2)
    relay_diag(1, 3)
    for d in (1, 2, 3):
        recv(b_ids[2 + d], bsum.at[6 + d])
    db_ref[...] = bsum[6] + bsum[7] + bsum[8] + bsum[9]

    recv(f_fin[0], fin.at[0], ends)
    recv(f_fin[1], fin.at[0], mids)
    for c in range(2):
        recv(f_out[0][c], fin.at[1, :, cut(c)], mids)
        recv(f_out[1][c], fin.at[1, :, cut(c)], ends)

    @pl.loop(0, 16)
    def _(t):
        cols = pl.ds(mult(t * 128, 128), 128)
        tot = dff[z, :, cols] + fin[0, :, cols].astype(F32) + fin[1, :, cols].astype(F32)
        dfeat_ref[pl.ds(mult(t * 128, 128), 128), :] = tot.T

    for h in range(2):
        for o in range(4):
            last(h, o)
    assert not pending
    for i, (c, cond) in sent_by.items():
        when(cond, c.wait_send)


def widen_kernel(dw_ref, out_ref, dfeat_ref, db_ref, dw_out, out_out, dfeat_out, db_out, sem):
    step = pl.program_id(0)
    copies = [
        pltpu.make_async_copy(src, dst, sem.at[i])
        for i, (src, dst) in enumerate(
            ((out_ref, out_out), (dfeat_ref, dfeat_out), (db_ref, db_out))
        )
    ]

    @pl.when(step == 0)
    def _():
        for c in copies:
            c.start()

    for i in range(2):
        for j in range(4):
            dw_out[i * 128:(i + 1) * 128, j * 512:(j + 1) * 512] = (
                dw_ref[(2 * step + i) * 4 + j].astype(F32)
            )

    @pl.when(step == pl.num_programs(0) - 1)
    def _():
        for c in copies:
            c.wait()


N_SEMS = 180


def per_device_fused(features, weight, bias, self_scale, adj_tiles, tile_ids, tile_counts, cotangent):
    vmem = pl.BlockSpec(memory_space=pltpu.VMEM)
    smem = pl.BlockSpec(memory_space=pltpu.SMEM)
    hbm = pl.BlockSpec(memory_space=pl.ANY)
    outputs, d_features, gathered, d_bias = pl.pallas_call(
        fused_kernel,
        out_shape=(
            pltpu.VMEM((128, 2048), F32),
            pltpu.VMEM((2048, 128), F32),
            pltpu.VMEM((64, 128, 512), BF16),
            pltpu.VMEM((16, 128), F32),
        ),
        in_specs=[smem, smem, vmem, hbm, hbm, vmem, vmem, vmem],
        out_specs=(vmem, vmem, vmem, vmem),
        scratch_shapes=[
            pltpu.VMEM((1024, 2048), BF16),
            pltpu.VMEM((4, 2048, 128), BF16),
            pltpu.VMEM((2048, 2048), BF16),
            pltpu.VMEM((4, 8, 128), F32),
            pltpu.VMEM((8, 128, 128), F32),
            pltpu.VMEM((4, 512, 128), BF16),
            pltpu.VMEM((4, 512, 128), BF16),
            pltpu.VMEM((4, 512, 128), F32),
            pltpu.VMEM((4, 1024, 128), BF16),
            pltpu.VMEM((16, 128, 128), BF16),
            pltpu.VMEM((128, 2048), F32),
            pltpu.VMEM((2048, 128), BF16),
            pltpu.VMEM((8, 1024, 128), BF16),
            pltpu.VMEM((4, 4, 128, 128), BF16),
            pltpu.VMEM((8, 4, 128, 128), BF16),
            pltpu.VMEM((4, 1024, 128), F32),
            pltpu.VMEM((4, 1024, 128), BF16),
            pltpu.VMEM((4, 1024, 128), BF16),
            pltpu.VMEM((4, 128, 2048), F32),
            pltpu.VMEM((4, 128, 2048), BF16),
            pltpu.VMEM((2, 128, 2048), BF16),
            pltpu.VMEM((2, 128, 2048), BF16),
            pltpu.VMEM((10, 16, 128), F32),
            pltpu.SemaphoreType.DMA((N_SEMS,)),
            pltpu.SemaphoreType.DMA((N_SEMS,)),
            pltpu.SemaphoreType.DMA((3,)),
        ],
        compiler_params=pltpu.CompilerParams(
            collective_id=0, has_side_effects=True, vmem_limit_bytes=50 * MIB
        ),
        cost_estimate=pl.CostEstimate(
            flops=7_600_000_000, bytes_accessed=24 * MIB, transcendentals=262144
        ),
    )(
        tile_ids[0, 0], tile_counts[0], adj_tiles[0, 0], features, weight,
        bias.astype(F32).reshape(1, 2048), self_scale.reshape(2, 128), cotangent,
    )
    d_weight, outputs, d_features, d_bias = pl.pallas_call(
        widen_kernel,
        grid=(8,),
        out_shape=(
            jax.ShapeDtypeStruct((2048, 2048), F32),
            jax.ShapeDtypeStruct((128, 2048), F32),
            jax.ShapeDtypeStruct((2048, 128), F32),
            jax.ShapeDtypeStruct((16, 128), F32),
        ),
        in_specs=[vmem] * 4,
        out_specs=(pl.BlockSpec((256, 2048), lambda i: (i, 0)), hbm, hbm, hbm),
        scratch_shapes=[pltpu.SemaphoreType.DMA((3,))],
        compiler_params=pltpu.CompilerParams(vmem_limit_bytes=20 * MIB),
    )(gathered, outputs, d_features, d_bias)
    return outputs, d_features, d_weight, d_bias.reshape(2048)


def solution(mesh):
    fits = dict(mesh.shape) == {"row": 16, "col": 2}

    def run(*arrays):
        fused = fits and arrays[0].shape == (4096, 2048) and arrays[4].shape[2] == 32
        return jax.shard_map(
            per_device_fused if fused else per_device_any,
            mesh=mesh,
            in_specs=(
                P("col", "row"),
                P(),
                P(),
                P("row"),
                P("row", "col", None, None, None),
                P("row", "col", None),
                P("row", "col"),
                P(("row", "col"), None),
            ),
            out_specs=(P(("row", "col"), None), P("col", "row"), P(), P()),
            check_vma=False,
        )(*arrays)

    return run
```

```python
import jax
import jax.numpy as jnp
from jax import lax
from jax.experimental import pallas as pl
from jax.experimental.pallas import tpu as pltpu
from jax.sharding import PartitionSpec as P

MESH = pl.DeviceIdType.MESH
F32 = jnp.float32
BF16 = jnp.bfloat16
MIB = 2**20
NC = 2


def dense_block(tiles, ids, count, tile_rows, tile_cols):
    slots = jnp.arange(tiles.shape[0], dtype=jnp.int32)
    live = jnp.where((slots < count)[:, None, None], tiles, jnp.zeros_like(tiles))
    blank = jnp.zeros((tile_rows * tile_cols, 128, 128), tiles.dtype)
    placed = blank.at[ids].add(live, unique_indices=True)
    placed = placed.reshape(tile_rows, tile_cols, 128, 128)
    return placed.transpose(0, 2, 1, 3).reshape(tile_rows * 128, tile_cols * 128)


def per_device_any(features, weight, bias, self_scale, adj_tiles, tile_ids, tile_counts, cotangent):
    row_block = self_scale.shape[0]
    col_block = features.shape[0]
    block = dense_block(
        adj_tiles[0, 0], tile_ids[0, 0], tile_counts[0, 0], row_block // 128, col_block // 128
    )
    start_row = lax.axis_index("row") * row_block
    col_no = lax.axis_index("col")
    inside = col_no == start_row // col_block
    offset = jnp.where(inside, start_row - col_no * col_block, 0)
    self_rows = jnp.where(inside, self_scale, 0.0)[:, None]
    piece = lax.all_gather(features, "row", axis=1, tiled=True)
    terms = jnp.dot(block, piece, preferred_element_type=F32)
    terms = terms + self_rows * lax.dynamic_slice_in_dim(piece, offset, row_block, 0)
    layer_in = lax.psum_scatter(terms, "col", scatter_dimension=0, tiled=True).astype(BF16)
    pre_act = jnp.dot(layer_in, weight, preferred_element_type=F32) + bias.astype(F32)
    sig = jax.nn.sigmoid(pre_act)
    outputs = pre_act * sig
    slope = sig * (1.0 + pre_act * (1.0 - sig))
    d_pre = (cotangent.astype(F32) * slope).astype(BF16)
    d_weight = lax.dot_general(
        layer_in, d_pre, (((0,), (0,)), ((), ())), preferred_element_type=F32
    )
    d_bias = jnp.sum(d_pre.astype(F32), axis=0)
    d_weight, d_bias = lax.psum((d_weight, d_bias), ("row", "col"))
    d_layer = lax.dot_general(
        d_pre, weight, (((1,), (1,)), ((), ())), preferred_element_type=F32
    ).astype(BF16)
    whole = lax.all_gather(d_layer, "col", axis=0, tiled=True)
    spread = lax.dot_general(block, whole, (((0,), (0,)), ((), ())), preferred_element_type=F32)
    own = lax.dynamic_slice_in_dim(spread, offset, row_block, 0) + self_rows * whole
    spread = lax.dynamic_update_slice_in_dim(spread, own, offset, 0)
    d_features = lax.psum_scatter(spread, "row", scatter_dimension=1, tiled=True)
    return outputs, d_features, d_weight, d_bias


def fused_kernel(
    ids_ref, count_ref, tiles_ref, feat_ref, w_ref, bias_ref, scale_ref, cot_ref,
    out_ref, dfeat_ref, dw_ref, db_ref,
    adj, hid, wv, sbuf, scol, xs, xr, keep, lay, xrow, pre, pt, ptg, dls, dlq,
    dwf, dwp, dwr, dff, dfp, agg, fin, bsum, bias32, ssem, rsem, lsem,
):
    r = lax.axis_index("row")
    x = lax.axis_index("col")
    z = r // 4
    y = (r // 2) % 2
    k = r % 2
    q = 2 * y + k
    ends = (z == 0) | (z == 3)
    mids = (z == 1) | (z == 2)

    def at(xx, yy, zz, kk):
        return (zz * 4 + yy * 2 + kk, xx)

    sib = at(x, y, z, 1 - k)
    xn = at(1 - x, y, z, k)
    yn = at(x, 1 - y, z, k)
    dg = at(x, 1 - y, z, 1 - k)
    zr = at(x, y, jnp.minimum(z + 1, 3), k)
    zl = at(x, y, jnp.maximum(z - 1, 0), k)
    q_y = 2 * (1 - y) + k
    q_s = 2 * y + 1 - k
    q_d = 3 - q

    count = [0]
    sent_by = {}
    pending = {}

    def new():
        count[0] += 1
        return count[0] - 1

    def when(cond, fn):
        if cond is None:
            fn()
        else:
            pl.when(cond)(fn)

    def copy(i, src, dst, to):
        return pltpu.make_async_remote_copy(
            src_ref=src, dst_ref=dst, send_sem=ssem.at[i], recv_sem=rsem.at[i],
            device_id=to, device_id_type=MESH,
        )

    def send(i, src, dst, to, cond=None, rcond=None):
        c = copy(i, src, dst, to)
        when(cond, c.start)
        sent_by[i] = (c, cond)
        pending[i] = (dst, rcond)

    def recv(i, dst, cond=None):
        pending.pop(i, None)
        c = copy(i, dst, dst, sib)
        when(cond, c.wait_recv)

    def slice_at(o):
        return [z, z + 1 - 2 * (z % 2), 2 - z // 2, 3 - 3 * (z // 2)][o]

    def mult(v, n):
        return pl.multiple_of(v, n)

    barrier = pltpu.get_barrier_semaphore()
    near = [(sib, None), (xn, None), (yn, None), (zr, z <= 2), (zl, z >= 1)]
    for peer, cond in near:
        when(cond, lambda peer=peer: pl.semaphore_signal(
            barrier, inc=1, device_id=peer, device_id_type=MESH
        ))

    w_copy = pltpu.make_async_copy(w_ref, wv, lsem.at[0])
    h_copy = pltpu.make_async_copy(feat_ref, hid.at[z], lsem.at[1])
    h_copy.start()

    for c in range(2):
        @pl.loop(0, 16)
        def _(t, c=c):
            slot = jnp.int32(0)
            for i in range(32):
                slot = jnp.where(ids_ref[i] == c * 16 + t, i, slot)
            live = jnp.where(slot < count_ref[0], 1.0, 0.0)
            tile = tiles_ref[slot].astype(F32) * live
            adj[pl.ds(mult(c * 512 + q * 128, 128), 128), pl.ds(mult(t * 128, 128), 128)] = (
                tile.astype(BF16)
            )
    for i in range(4):
        sbuf[q, 2 * i:2 * i + 2, :] = scale_ref[...]
    bias32[...] = bias_ref[...].astype(F32)
    h_copy.wait()
    w_copy.start()
    pl.semaphore_wait(barrier, jnp.where(ends, 4, 5))

    def h_part(s, c):
        return hid.at[s, pl.ds(c * (2048 // NC), 2048 // NC)]

    right = {(d, c): new() for d in (1, 2, 3) for c in range(NC)}
    left = {(d, c): new() for d in (1, 2, 3) for c in range(NC)}

    def line_send(ids, part, d, c, own_ok=True):
        sr, sl = jnp.maximum(z - (d - 1), 0), jnp.minimum(z + d - 1, 3)
        send(ids[0][d, c], part(sr, c), part(sr, c), zr, (z >= d - 1) & (z <= 2), z >= d)
        send(ids[1][d, c], part(sl, c), part(sl, c), zl, (z <= 4 - d) & (z >= 1), z <= 3 - d)

    def line_recv(ids, part, d, c):
        sr, sl = jnp.maximum(z - d, 0), jnp.minimum(z + d, 3)
        recv(ids[0][d, c], part(sr, c), z >= d)
        recv(ids[1][d, c], part(sl, c), z <= 3 - d)

    hz = (right, left)
    for c in range(NC):
        line_send(hz, h_part, 1, c)

    s_id = [new() for _ in range(3)]
    send(s_id[0], sbuf.at[q], sbuf.at[q], yn)
    send(s_id[1], sbuf.at[q], sbuf.at[q], sib)

    def a_part(qq, c):
        return adj.at[pl.ds(mult(c * 512 + qq * 128, 128), 128)]

    ay = [new() for _ in range(2)]
    asib = [new() for _ in range(2)]
    afwd = [new() for _ in range(2)]
    for c in range(2):
        send(ay[c], a_part(q, c), a_part(q, c), yn)
    for c in range(2):
        send(asib[c], a_part(q, c), a_part(q, c), sib)

    for c in range(NC):
        line_recv(hz, h_part, 1, c)
        line_send(hz, h_part, 2, c)
    recv(ay[0], a_part(q_y, 0))
    send(afwd[0], a_part(q_y, 0), a_part(q_y, 0), sib)

    recv(s_id[0], sbuf.at[q_y])
    send(s_id[2], sbuf.at[q_y], sbuf.at[q_y], sib)
    recv(s_id[1], sbuf.at[q_s])
    recv(s_id[2], sbuf.at[q_d])
    inside = jnp.where(x == z // 2, 1.0, 0.0)
    for b in range(8):
        row = sbuf[b % 4, b // 4:b // 4 + 1, :] * inside
        scol[b] = jnp.broadcast_to(row, (128, 128)).T

    for c in range(NC):
        line_recv(hz, h_part, 2, c)
        line_send(hz, h_part, 3, c)
    recv(ay[1], a_part(q_y, 1))
    send(afwd[1], a_part(q_y, 1), a_part(q_y, 1), sib)
    for c in range(2):
        recv(asib[c], a_part(q_s, c))
    for c in range(2):
        recv(afwd[c], a_part(q_d, c))

    n_parts = (1, 1, 1, 2)
    x_id = [[new() for _ in range(n)] for n in n_parts]
    l_id = [new() for _ in range(4)]
    row_id = [[new() for _ in range(3)] for _ in range(4)]
    w_waited = []

    def row_part(o, u):
        return (0, 512) if n_parts[o] == 1 else ((1 - y if u == 0 else y) * 256, 256)

    def aggregate(o):
        s = slice_at(o)
        for c, sending in ((1 - x, True), (x, False)):
            for u in range(n_parts[o]):
                first, n = row_part(o, u)
                rows = pl.ds(mult(first, 256), n)
                acc = jnp.dot(
                    adj[pl.ds(mult(c * 512 + first, 256), n), :], hid[s],
                    preferred_element_type=F32,
                )
                own = []
                for i in range(n // 128):
                    qq = first // 128 + i
                    at_node = mult((z % 2) * 1024 + qq * 256 + c * 128, 128)
                    own.append(scol[c * 4 + qq] * hid[s, pl.ds(at_node, 128), :].astype(F32))
                acc = acc + jnp.concatenate(own, axis=0)
                if sending:
                    xs[o, rows] = acc.astype(BF16)
                    send(x_id[o][u], xs.at[o, rows], xr.at[o, rows], xn)
                else:
                    keep[o, rows] = acc

    def combine(o):
        s = slice_at(o)
        sends = list(zip(row_id[o], (q_y, q_d, q_s), (yn, dg, sib)))
        for u in range(n_parts[o]):
            first, n = row_part(o, u)
            rows = pl.ds(mult(first, 256), n)
            recv(x_id[o][u], xr.at[o, rows])
            mine = pl.ds(mult(x * 512 + first, 256), n)
            lay[s, mine, :] = (keep[o, rows] + xr[o, rows].astype(F32)).astype(BF16)
            for i, qq, to in (sends if n_parts[o] == 1 else (sends[:2], sends[2:])[u]):
                piece_rows = pl.ds(mult(x * 512 + qq * 128, 128), 128)
                send(i, lay.at[s, piece_rows], xrow.at[s * 4 + q], to)
        half = pl.ds(mult(x * 512, 512), 512)
        send(l_id[o], lay.at[s, half], lay.at[s, half], xn)
        xrow[s * 4 + q] = lay[s, pl.ds(mult(x * 512 + q * 128, 128), 128), :]

    def linear(o):
        s = slice_at(o)
        for i, qq in zip(row_id[o], (q_y, q_d, q_s)):
            recv(i, xrow.at[s * 4 + qq])
        if not w_waited:
            w_copy.wait()
            w_waited.append(True)
        block = jnp.concatenate([xrow[s * 4 + i] for i in range(4)], axis=1)

        @pl.loop(0, 2)
        def _(t):
            cols = pl.ds(mult(t * 1024, 1024), 1024)
            prod = jnp.dot(
                block, wv[pl.ds(mult(s * 512, 512), 512), cols], preferred_element_type=F32
            )
            if o == 0:
                pre[:, cols] = prod
            else:
                pre[:, cols] += prod

    aggregate(0)
    aggregate(1)
    aggregate(2)
    combine(0)
    combine(1)
    linear(0)
    for c in range(NC):
        line_recv(hz, h_part, 3, c)
    aggregate(3)
    combine(2)
    linear(1)
    linear(2)
    combine(3)
    linear(3)

    def p_part(c, h):
        return pt.at[pl.ds(mult(c * 1024 + h * 512, 512), 512)]

    def activate(c, h):
        @pl.loop(0, 4)
        def _(i):
            t = c * 8 + h * 4 + i
            cols = pl.ds(mult(t * 128, 128), 128)
            v = pre[:, cols] + bias32[pl.ds(t, 1), :]
            sig = jax.nn.sigmoid(v)
            out_ref[:, cols] = v * sig
            slope = sig * (1.0 + v * (1.0 - sig))
            d32 = (cot_ref[:, cols].astype(F32) * slope).astype(BF16).astype(F32)
            pt[pl.ds(mult(t * 128, 128), 128), :] = d32.T.astype(BF16)
            bsum[0, pl.ds(t, 1), :] = jnp.sum(d32, axis=0, keepdims=True)

    b_own, b_x = x * 4 + q, (1 - x) * 4 + q
    px, py, pyf, ps, psf, pd, pdf = ([new(), new()] for _ in range(7))
    b_ids = [new() for _ in range(6)]

    def p_at(b, h):
        return ptg.at[b, pl.ds(h * 512, 512)]

    def p_send(h):
        send(px[h], p_part(1 - x, h), p_at(b_own, h), xn)
        send(py[h], p_part(x, h), p_at(b_own, h), yn)
        send(ps[h], p_part(x, h), p_at(b_own, h), sib)
        ptg[b_own, h * 512:(h + 1) * 512] = pt[pl.ds(mult(x * 1024 + h * 512, 512), 512), :]

    def p_relay_x(h):
        recv(px[h], p_at(b_x, h))
        send(pyf[h], p_at(b_x, h), p_at(b_x, h), yn)
        send(psf[h], p_at(b_x, h), p_at(b_x, h), sib)
        recv(py[h], p_at(x * 4 + q_y, h))
        send(pd[h], p_at(x * 4 + q_y, h), p_at(x * 4 + q_y, h), sib)

    def p_relay_y(h):
        recv(pyf[h], p_at((1 - x) * 4 + q_y, h))
        send(pdf[h], p_at((1 - x) * 4 + q_y, h), p_at((1 - x) * 4 + q_y, h), sib)

    def p_last(h):
        recv(ps[h], p_at(x * 4 + q_s, h))
        recv(psf[h], p_at((1 - x) * 4 + q_s, h))
        recv(pd[h], p_at(x * 4 + q_d, h))
        recv(pdf[h], p_at((1 - x) * 4 + q_d, h))

    activate(1 - x, 0)
    activate(x, 0)
    p_send(0)
    activate(1 - x, 1)
    activate(x, 1)

    @pl.loop(0, 2)
    def _(i):
        acc = jnp.dot(
            wv[pl.ds(mult(i * 1024, 1024), 1024), :], pt[...], preferred_element_type=F32
        ).astype(BF16)
        for j in range(2):
            for qq in range(4):
                first = j * 512 + qq * 128
                dls[qq, i * 2 + j] = acc[first:first + 128]

    dl_to = [
        (1 - x, y, k), (1 - x, y, 1 - k), (x, y, 1 - k),
        (x, 1 - y, k), (x, 1 - y, 1 - k), (1 - x, 1 - y, k), (1 - x, 1 - y, 1 - k),
    ]
    dl_ids = [new() for _ in dl_to]

    def send_layer_grad(which):
        for i in which:
            xx, yy, kk = dl_to[i]
            send(dl_ids[i], dls.at[2 * yy + kk], dlq.at[b_own], at(xx, yy, z, kk))

    p_send(1)
    send(b_ids[0], bsum.at[0], bsum.at[1], xn)
    dlq[b_own] = dls[q]
    p_relay_x(0)
    send_layer_grad((0, 1, 2))
    p_relay_x(1)
    p_relay_y(0)
    recv(b_ids[0], bsum.at[1])
    bsum[2] = bsum[0] + bsum[1]
    send(b_ids[1], bsum.at[2], bsum.at[3], yn)
    for o in range(4):
        recv(l_id[o], lay.at[slice_at(o), pl.ds(mult((1 - x) * 512, 512), 512)])
    p_last(0)

    dw_ids = [[new() for _ in range(3)] for _ in range(2)]

    def weight_grad(h):
        rows = pl.ds(h * 512, 512)
        lhs = jnp.concatenate([ptg[b, rows, :] for b in range(8)], axis=1)
        rhs = jnp.concatenate([lay[s] for s in range(4)], axis=1)
        acc = jnp.dot(lhs, rhs, preferred_element_type=F32)
        for s in range(4):
            dwf[s, rows, :] = acc[:, s * 128:(s + 1) * 128]
            dwp[s, rows, :] = acc[:, s * 128:(s + 1) * 128].astype(BF16)
        for d in (2, 1, 3):
            to = (z + d) % 4
            send(dw_ids[h][d - 1], dwp.at[to, rows], dwr.at[z, rows], at(x, y, to, k))

    weight_grad(0)
    p_relay_y(1)
    send_layer_grad((3, 4, 5, 6))
    recv(b_ids[1], bsum.at[3])
    bsum[4] = bsum[2] + bsum[3]
    send(b_ids[2], bsum.at[4], bsum.at[5], sib)
    p_last(1)
    weight_grad(1)
    recv(b_ids[2], bsum.at[5])
    bsum[6] = bsum[4] + bsum[5]
    for d in (1, 2, 3):
        send(b_ids[2 + d], bsum.at[6], bsum.at[6 + d], at(x, y, (z + d) % 4, k))

    def layer_grads_here(cond):
        for i, (xx, yy, kk) in zip(dl_ids, dl_to):
            recv(i, dlq.at[xx * 4 + 2 * yy + kk], cond)

    pair = z // 2
    e, m = 3 * pair, 1 + pair
    e2, m2 = 3 - 3 * pair, 2 - pair
    f_in = [[new() for _ in range(2)] for _ in range(2)]
    f_out = [[new() for _ in range(2)] for _ in range(2)]
    f_fin = [new() for _ in range(2)]

    def input_grad(first):
        lhs = jnp.concatenate(
            [dlq[b, pl.ds(first, 2)].reshape(256, 128) for b in range(8)], axis=1
        )

        @pl.loop(0, 4)
        def _(t):
            cols = pl.ds(mult(t * 512, 512), 512)
            acc = jnp.dot(lhs, adj[:, cols], preferred_element_type=F32)
            own = jnp.where((x == z // 2) & (t // 2 == z % 2), 1.0, 0.0)
            diag = []
            for j in range(2):
                qq = (t % 2) * 2 + j
                for c in range(2):
                    row = sbuf[qq, c:c + 1, :] * own
                    diag.append(dlq[c * 4 + qq, pl.ds(first, 2)].reshape(256, 128).astype(F32) * row)
            acc = acc + jnp.concatenate(diag, axis=1)
            for i in range(2):
                dff[first + i, :, cols] = acc[i * 128:(i + 1) * 128]
                dfp[first + i, :, cols] = acc[i * 128:(i + 1) * 128].astype(BF16)

    mid_dev, end_dev = at(x, y, m, k), at(x, y, e, k)
    layer_grads_here(mids)

    @pl.when(mids)
    def _():
        input_grad(2 * pair)
    send(f_fin[0], dfp.at[e], fin.at[0], end_dev, mids, ends)

    def cut(c):
        return pl.ds(c * 1024, 1024)

    def end_send(j, c):
        s_to = (m2, e2)[j]
        send(f_in[j][c], dfp.at[s_to, :, cut(c)], agg.at[j, :, cut(c)], mid_dev, ends, mids)

    def end_wait(j, c):
        out, cond = sent_by.pop(f_in[j][c])
        pl.when(cond)(out.wait_send)

    def mid_send(j, c):
        s_to, to = ((m2, at(x, y, m2, k)), (e2, at(x, y, e2, k)))[j]
        recv(f_in[j][c], agg.at[j, :, cut(c)], mids)

        @pl.when(mids)
        def _():
            dfp[s_to, :, cut(c)] = (
                dff[s_to, :, cut(c)] + agg[j, :, cut(c)].astype(F32)
            ).astype(BF16)
        send(f_out[j][c], dfp.at[s_to, :, cut(c)], fin.at[1, :, cut(c)], to, mids, (mids, ends)[j])

    def piece(s, qq, c, h):
        return dw_ref.at[(s * 4 + qq) * 4 + c * 2 + h]

    gz = tuple({(d, h): new() for d in (1, 2, 3) for h in (0, 1)} for _ in range(2))
    gx, gy, gxy, gyx = ({(h, o): new() for h in (0, 1) for o in range(4)} for _ in range(4))
    gs, gsd = ([new() for _ in range(4)] for _ in range(2))

    def z_piece(s, h):
        return piece(s, q, x, h)

    def finish(h):
        for d in (1, 2, 3):
            recv(dw_ids[h][d - 1], dwr.at[(z - d) % 4, pl.ds(h * 512, 512)])
        for t in range(4):
            rr = pl.ds(h * 512 + t * 128, 128)
            tot = dwf[z, rr, :]
            for d in (1, 2, 3):
                tot = tot + dwr[(z + d) % 4, rr, :].astype(F32)
            dw_ref[(z * 4 + q) * 4 + x * 2 + h, :, t * 128:(t + 1) * 128] = tot.T.astype(BF16)
        line_send(gz, z_piece, 1, h)
        spread(h, 0)

    def spread(h, o):
        src = piece(slice_at(o), q, x, h)
        send(gx[h, o], src, src, xn)
        send(gy[h, o], src, src, yn)

    def whole(s, qq):
        return dw_ref.at[pl.ds((s * 4 + qq) * 4, 4)]

    def part(ref, i):
        return ref.at[pl.ds(i * 64, 64)]

    def relay(h, o):
        s = slice_at(o)
        from_x, from_y = piece(s, q, 1 - x, h), piece(s, q_y, x, h)
        recv(gx[h, o], from_x)
        send(gxy[h, o], part(from_x, 0), part(from_x, 0), yn)
        if h == 1:
            send(gs[o], whole(s, q), whole(s, q), sib)
        recv(gy[h, o], from_y)
        send(gyx[h, o], part(from_y, 1), part(from_y, 1), xn)

    def relay_diag(h, o):
        block = piece(slice_at(o), q_y, 1 - x, h)
        recv(gxy[h, o], part(block, 0))
        recv(gyx[h, o], part(block, 1))
        if h == 1:
            send(gsd[o], whole(slice_at(o), q_y), whole(slice_at(o), q_y), sib)

    def last(o):
        recv(gs[o], whole(slice_at(o), q_s))
        recv(gsd[o], whole(slice_at(o), q_d))

    def along(h, d):
        line_recv(gz, z_piece, d, h)
        if d < 3:
            line_send(gz, z_piece, d + 1, h)
        spread(h, d)

    finish(0)
    layer_grads_here(ends)
    input_grad(2 * (1 - pair))

    @pl.when(ends)
    def _():
        input_grad(2 * pair)
    along(0, 1)
    relay(0, 0)
    finish(1)
    end_send(0, 0)
    end_send(0, 1)
    along(0, 2)
    relay(0, 1)
    relay_diag(0, 0)
    along(1, 1)
    mid_send(0, 0)
    end_wait(0, 0)
    end_send(1, 0)
    relay(1, 0)
    relay_diag(0, 1)
    along(0, 3)
    mid_send(0, 1)
    end_wait(0, 1)
    end_send(1, 1)
    relay(0, 2)
    relay_diag(1, 0)
    along(1, 2)
    mid_send(1, 0)
    end_wait(1, 0)
    send(f_fin[1], dfp.at[m], fin.at[0], mid_dev, ends, mids)
    relay(1, 1)
    relay_diag(0, 2)
    along(1, 3)
    mid_send(1, 1)
    relay(0, 3)
    relay_diag(1, 1)
    relay(1, 2)
    relay_diag(0, 3)
    relay(1, 3)
    relay_diag(1, 2)
    relay_diag(1, 3)
    for d in (1, 2, 3):
        recv(b_ids[2 + d], bsum.at[6 + d])
    db_ref[...] = bsum[6] + bsum[7] + bsum[8] + bsum[9]

    recv(f_fin[0], fin.at[0], ends)
    recv(f_fin[1], fin.at[0], mids)
    for c in range(2):
        recv(f_out[0][c], fin.at[1, :, cut(c)], mids)
        recv(f_out[1][c], fin.at[1, :, cut(c)], ends)

    @pl.loop(0, 16)
    def _(t):
        cols = pl.ds(mult(t * 128, 128), 128)
        tot = dff[z, :, cols] + fin[0, :, cols].astype(F32) + fin[1, :, cols].astype(F32)
        dfeat_ref[pl.ds(mult(t * 128, 128), 128), :] = tot.T

    for o in range(4):
        last(o)
    assert not pending and count[0] <= N_SEMS, count
    for i, (c, cond) in sent_by.items():
        when(cond, c.wait_send)


def widen_kernel(dw_ref, out_ref, dfeat_ref, db_ref, dw_out, out_out, dfeat_out, db_out, wide, sem):
    copies = [
        pltpu.make_async_copy(src, dst, sem.at[16 + i])
        for i, (src, dst) in enumerate(
            ((out_ref, out_out), (dfeat_ref, dfeat_out), (db_ref, db_out))
        )
    ]
    for c in copies:
        c.start()
    rows = [
        pltpu.make_async_copy(wide.at[i], dw_out.at[pl.ds(i * 128, 128)], sem.at[i])
        for i in range(16)
    ]
    for i in range(16):
        for j in range(4):
            wide[i, :, j * 512:(j + 1) * 512] = dw_ref[4 * i + j].astype(F32)
        rows[i].start()
    for c in copies + rows:
        c.wait()


N_SEMS = 137


def per_device_fused(features, weight, bias, self_scale, adj_tiles, tile_ids, tile_counts, cotangent):
    vmem = pl.BlockSpec(memory_space=pltpu.VMEM)
    smem = pl.BlockSpec(memory_space=pltpu.SMEM)
    hbm = pl.BlockSpec(memory_space=pl.ANY)
    outputs, d_features, gathered, d_bias = pl.pallas_call(
        fused_kernel,
        out_shape=(
            pltpu.VMEM((128, 2048), F32),
            pltpu.VMEM((2048, 128), F32),
            pltpu.VMEM((64, 128, 512), BF16),
            pltpu.VMEM((16, 128), F32),
        ),
        in_specs=[smem, smem, vmem, hbm, hbm, vmem, vmem, vmem],
        out_specs=(vmem, vmem, vmem, vmem),
        scratch_shapes=[
            pltpu.VMEM((1024, 2048), BF16),
            pltpu.VMEM((4, 2048, 128), BF16),
            pltpu.VMEM((2048, 2048), BF16),
            pltpu.VMEM((4, 8, 128), F32),
            pltpu.VMEM((8, 128, 128), F32),
            pltpu.VMEM((4, 512, 128), BF16),
            pltpu.VMEM((4, 512, 128), BF16),
            pltpu.VMEM((4, 512, 128), F32),
            pltpu.VMEM((4, 1024, 128), BF16),
            pltpu.VMEM((16, 128, 128), BF16),
            pltpu.VMEM((128, 2048), F32),
            pltpu.VMEM((2048, 128), BF16),
            pltpu.VMEM((8, 1024, 128), BF16),
            pltpu.VMEM((4, 4, 128, 128), BF16),
            pltpu.VMEM((8, 4, 128, 128), BF16),
            pltpu.VMEM((4, 1024, 128), F32),
            pltpu.VMEM((4, 1024, 128), BF16),
            pltpu.VMEM((4, 1024, 128), BF16),
            pltpu.VMEM((4, 128, 2048), F32),
            pltpu.VMEM((4, 128, 2048), BF16),
            pltpu.VMEM((2, 128, 2048), BF16),
            pltpu.VMEM((2, 128, 2048), BF16),
            pltpu.VMEM((10, 16, 128), F32),
            pltpu.VMEM((16, 128), F32),
            pltpu.SemaphoreType.DMA((N_SEMS,)),
            pltpu.SemaphoreType.DMA((N_SEMS,)),
            pltpu.SemaphoreType.DMA((3,)),
        ],
        compiler_params=pltpu.CompilerParams(
            collective_id=0, has_side_effects=True, vmem_limit_bytes=50 * MIB
        ),
        cost_estimate=pl.CostEstimate(
            flops=7_600_000_000, bytes_accessed=24 * MIB, transcendentals=262144
        ),
    )(
        tile_ids[0, 0], tile_counts[0], adj_tiles[0, 0], features, weight,
        bias.reshape(16, 128), self_scale.reshape(2, 128), cotangent,
    )
    d_weight, outputs, d_features, d_bias = pl.pallas_call(
        widen_kernel,
        out_shape=(
            jax.ShapeDtypeStruct((2048, 2048), F32),
            jax.ShapeDtypeStruct((128, 2048), F32),
            jax.ShapeDtypeStruct((2048, 128), F32),
            jax.ShapeDtypeStruct((16, 128), F32),
        ),
        in_specs=[vmem] * 4,
        out_specs=(hbm, hbm, hbm, hbm),
        scratch_shapes=[pltpu.VMEM((16, 128, 2048), F32), pltpu.SemaphoreType.DMA((19,))],
        compiler_params=pltpu.CompilerParams(vmem_limit_bytes=30 * MIB),
    )(gathered, outputs, d_features, d_bias)
    return outputs, d_features, d_weight, d_bias.reshape(2048)


def solution(mesh):
    fits = dict(mesh.shape) == {"row": 16, "col": 2}

    def run(*arrays):
        fused = fits and arrays[0].shape == (4096, 2048) and arrays[4].shape[2] == 32
        return jax.shard_map(
            per_device_fused if fused else per_device_any,
            mesh=mesh,
            in_specs=(
                P("col", "row"),
                P(),
                P(),
                P("row"),
                P("row", "col", None, None, None),
                P("row", "col", None),
                P("row", "col"),
                P(("row", "col"), None),
            ),
            out_specs=(P(("row", "col"), None), P("col", "row"), P(), P()),
            check_vma=False,
        )(*arrays)

    return run
```

```python
import jax
import jax.numpy as jnp
from jax import lax
from jax.experimental import pallas as pl
from jax.experimental.pallas import tpu as pltpu
from jax.sharding import PartitionSpec as P

MESH = pl.DeviceIdType.MESH
F32 = jnp.float32
BF16 = jnp.bfloat16
MIB = 2**20
NC = 2


def dense_block(tiles, ids, count, tile_rows, tile_cols):
    slots = jnp.arange(tiles.shape[0], dtype=jnp.int32)
    live = jnp.where((slots < count)[:, None, None], tiles, jnp.zeros_like(tiles))
    blank = jnp.zeros((tile_rows * tile_cols, 128, 128), tiles.dtype)
    placed = blank.at[ids].add(live, unique_indices=True)
    placed = placed.reshape(tile_rows, tile_cols, 128, 128)
    return placed.transpose(0, 2, 1, 3).reshape(tile_rows * 128, tile_cols * 128)


def per_device_any(features, weight, bias, self_scale, adj_tiles, tile_ids, tile_counts, cotangent):
    row_block = self_scale.shape[0]
    col_block = features.shape[0]
    block = dense_block(
        adj_tiles[0, 0], tile_ids[0, 0], tile_counts[0, 0], row_block // 128, col_block // 128
    )
    start_row = lax.axis_index("row") * row_block
    col_no = lax.axis_index("col")
    inside = col_no == start_row // col_block
    offset = jnp.where(inside, start_row - col_no * col_block, 0)
    self_rows = jnp.where(inside, self_scale, 0.0)[:, None]
    piece = lax.all_gather(features, "row", axis=1, tiled=True)
    terms = jnp.dot(block, piece, preferred_element_type=F32)
    terms = terms + self_rows * lax.dynamic_slice_in_dim(piece, offset, row_block, 0)
    layer_in = lax.psum_scatter(terms, "col", scatter_dimension=0, tiled=True).astype(BF16)
    pre_act = jnp.dot(layer_in, weight, preferred_element_type=F32) + bias.astype(F32)
    sig = jax.nn.sigmoid(pre_act)
    outputs = pre_act * sig
    slope = sig * (1.0 + pre_act * (1.0 - sig))
    d_pre = (cotangent.astype(F32) * slope).astype(BF16)
    d_weight = lax.dot_general(
        layer_in, d_pre, (((0,), (0,)), ((), ())), preferred_element_type=F32
    )
    d_bias = jnp.sum(d_pre.astype(F32), axis=0)
    d_weight, d_bias = lax.psum((d_weight, d_bias), ("row", "col"))
    d_layer = lax.dot_general(
        d_pre, weight, (((1,), (1,)), ((), ())), preferred_element_type=F32
    ).astype(BF16)
    whole = lax.all_gather(d_layer, "col", axis=0, tiled=True)
    spread = lax.dot_general(block, whole, (((0,), (0,)), ((), ())), preferred_element_type=F32)
    own = lax.dynamic_slice_in_dim(spread, offset, row_block, 0) + self_rows * whole
    spread = lax.dynamic_update_slice_in_dim(spread, own, offset, 0)
    d_features = lax.psum_scatter(spread, "row", scatter_dimension=1, tiled=True)
    return outputs, d_features, d_weight, d_bias


def fused_kernel(
    ids_ref, count_ref, tiles_ref, feat_ref, w_ref, bias_ref, scale_ref, cot_ref,
    out_ref, dfeat_ref, dw_ref, db_ref,
    adj, adj_e, hid, wv, sbuf, sbuf_e, scol, xs, xr, keep, lay, xrow, pre, pt, ptg, dls, dlq,
    dwf, dwp, dwr, dff, dfp, dle, fin, bsum, bias32, ssem, rsem, lsem,
):
    r = lax.axis_index("row")
    x = lax.axis_index("col")
    z = r // 4
    y = (r // 2) % 2
    k = r % 2
    q = 2 * y + k
    ends = (z == 0) | (z == 3)
    mids = (z == 1) | (z == 2)

    def at(xx, yy, zz, kk):
        return (zz * 4 + yy * 2 + kk, xx)

    sib = at(x, y, z, 1 - k)
    xn = at(1 - x, y, z, k)
    yn = at(x, 1 - y, z, k)
    dg = at(x, 1 - y, z, 1 - k)
    zr = at(x, y, jnp.minimum(z + 1, 3), k)
    zl = at(x, y, jnp.maximum(z - 1, 0), k)
    q_y = 2 * (1 - y) + k
    q_s = 2 * y + 1 - k
    q_d = 3 - q

    count = [0]
    sent_by = {}
    pending = {}

    def new():
        count[0] += 1
        return count[0] - 1

    def when(cond, fn):
        if cond is None:
            fn()
        else:
            pl.when(cond)(fn)

    def copy(i, src, dst, to):
        return pltpu.make_async_remote_copy(
            src_ref=src, dst_ref=dst, send_sem=ssem.at[i], recv_sem=rsem.at[i],
            device_id=to, device_id_type=MESH,
        )

    def send(i, src, dst, to, cond=None, rcond=None):
        c = copy(i, src, dst, to)
        when(cond, c.start)
        sent_by[i] = (c, cond)
        pending[i] = (dst, rcond)

    def recv(i, dst, cond=None):
        pending.pop(i, None)
        c = copy(i, dst, dst, sib)
        when(cond, c.wait_recv)

    def slice_at(o):
        return [z, z + 1 - 2 * (z % 2), 2 - z // 2, 3 - 3 * (z // 2)][o]

    def mult(v, n):
        return pl.multiple_of(v, n)

    barrier = pltpu.get_barrier_semaphore()
    near = [(sib, None), (xn, None), (yn, None), (zr, z <= 2), (zl, z >= 1)]
    for peer, cond in near:
        when(cond, lambda peer=peer: pl.semaphore_signal(
            barrier, inc=1, device_id=peer, device_id_type=MESH
        ))

    w_copy = pltpu.make_async_copy(w_ref, wv, lsem.at[0])
    h_copy = pltpu.make_async_copy(feat_ref, hid.at[z], lsem.at[1])
    h_copy.start()

    for c in range(2):
        @pl.loop(0, 16)
        def _(t, c=c):
            slot = jnp.int32(0)
            for i in range(32):
                slot = jnp.where(ids_ref[i] == c * 16 + t, i, slot)
            live = jnp.where(slot < count_ref[0], 1.0, 0.0)
            tile = tiles_ref[slot].astype(F32) * live
            adj[pl.ds(mult(c * 512 + q * 128, 128), 128), pl.ds(mult(t * 128, 128), 128)] = (
                tile.astype(BF16)
            )
    for i in range(4):
        sbuf[q, 2 * i:2 * i + 2, :] = scale_ref[...]
    bias32[...] = bias_ref[...].astype(F32)
    h_copy.wait()
    w_copy.start()
    pl.semaphore_wait(barrier, jnp.where(ends, 4, 5))

    def h_part(s, c):
        return hid.at[s, pl.ds(c * (2048 // NC), 2048 // NC)]

    right = {(d, c): new() for d in (1, 2, 3) for c in range(NC)}
    left = {(d, c): new() for d in (1, 2, 3) for c in range(NC)}

    def line_send(ids, part, d, c, own_ok=True):
        sr, sl = jnp.maximum(z - (d - 1), 0), jnp.minimum(z + d - 1, 3)
        send(ids[0][d, c], part(sr, c), part(sr, c), zr, (z >= d - 1) & (z <= 2), z >= d)
        send(ids[1][d, c], part(sl, c), part(sl, c), zl, (z <= 4 - d) & (z >= 1), z <= 3 - d)

    def line_recv(ids, part, d, c):
        sr, sl = jnp.maximum(z - d, 0), jnp.minimum(z + d, 3)
        recv(ids[0][d, c], part(sr, c), z >= d)
        recv(ids[1][d, c], part(sl, c), z <= 3 - d)

    hz = (right, left)
    for c in range(NC):
        line_send(hz, h_part, 1, c)

    s_id = [new() for _ in range(3)]
    send(s_id[0], sbuf.at[q], sbuf.at[q], yn)
    send(s_id[1], sbuf.at[q], sbuf.at[q], sib)

    def a_part(qq, c):
        return adj.at[pl.ds(mult(c * 512 + qq * 128, 128), 128)]

    halves = (1 - x, x)
    ay, asib, afwd = ([new(), new()] for _ in range(3))
    for i, c in enumerate(halves):
        send(asib[i], a_part(q, c), a_part(q, c), sib)
    send(ay[0], a_part(q, 1 - x), a_part(q, 1 - x), yn)

    line_recv(hz, h_part, 1, 0)
    line_send(hz, h_part, 2, 0)
    send(ay[1], a_part(q, x), a_part(q, x), yn)

    recv(s_id[0], sbuf.at[q_y])
    send(s_id[2], sbuf.at[q_y], sbuf.at[q_y], sib)
    recv(s_id[1], sbuf.at[q_s])
    recv(s_id[2], sbuf.at[q_d])
    inside = jnp.where(x == z // 2, 1.0, 0.0)
    for b in range(8):
        row = sbuf[b % 4, b // 4:b // 4 + 1, :] * inside
        scol[b] = jnp.broadcast_to(row, (128, 128)).T

    line_recv(hz, h_part, 1, 1)
    line_send(hz, h_part, 2, 1)

    pair = z // 2
    e, m = 3 * pair, 1 + pair
    e2, m2 = 3 - 3 * pair, 2 - pair
    mid_dev, end_dev = at(x, y, m, k), at(x, y, e, k)

    def e_part(qq, c):
        return adj_e.at[pl.ds(mult(c * 512 + qq * 128, 128), 128)]

    ez, ey, esib, efwd = ([new(), new()] for _ in range(4))
    es = new()
    for c in range(2):
        send(ez[c], a_part(q, c), e_part(q, c), mid_dev, ends, mids)
    send(es, sbuf, sbuf_e, mid_dev, ends, mids)

    x_id = [[new(), new()] for _ in range(4)]
    l_id = [new() for _ in range(4)]
    row_id = [[new() for _ in range(3)] for _ in range(4)]
    w_waited = []

    def aggregate(o, c, u):
        s = slice_at(o)
        first = (1 - y if u == 0 else y) * 256
        rows = pl.ds(mult(first, 256), 256)
        acc = jnp.dot(
            adj[pl.ds(mult(halves[c] * 512 + first, 256), 256), :], hid[s],
            preferred_element_type=F32,
        )
        own = []
        for i in range(2):
            qq = first // 128 + i
            at_node = mult((z % 2) * 1024 + qq * 256 + halves[c] * 128, 128)
            own.append(scol[halves[c] * 4 + qq] * hid[s, pl.ds(at_node, 128), :].astype(F32))
        acc = acc + jnp.concatenate(own, axis=0)
        if c == 0:
            xs[o, rows] = acc.astype(BF16)
            send(x_id[o][u], xs.at[o, rows], xr.at[o, rows], xn)
        else:
            keep[o, rows] = acc

    def combine(o):
        s = slice_at(o)
        sends = list(zip(row_id[o], (q_y, q_d, q_s), (yn, dg, sib)))
        for u in range(2):
            first = (1 - y if u == 0 else y) * 256
            rows = pl.ds(mult(first, 256), 256)
            recv(x_id[o][u], xr.at[o, rows])
            mine = pl.ds(mult(x * 512 + first, 256), 256)
            lay[s, mine, :] = (keep[o, rows] + xr[o, rows].astype(F32)).astype(BF16)
            for i, qq, to in (sends[:2], sends[2:])[u]:
                piece_rows = pl.ds(mult(x * 512 + qq * 128, 128), 128)
                send(i, lay.at[s, piece_rows], xrow.at[s * 4 + q], to)
        xrow[s * 4 + q] = lay[s, pl.ds(mult(x * 512 + q * 128, 128), 128), :]

    def share(o):
        half = lay.at[slice_at(o), pl.ds(mult(x * 512, 512), 512)]
        send(l_id[o], half, half, xn)

    def linear(o):
        s = slice_at(o)
        for i, qq in zip(row_id[o], (q_y, q_d, q_s)):
            recv(i, xrow.at[s * 4 + qq])
        if not w_waited:
            w_copy.wait()
            w_waited.append(True)
        block = jnp.concatenate([xrow[s * 4 + i] for i in range(4)], axis=1)

        @pl.loop(0, 2)
        def _(t):
            cols = pl.ds(mult(t * 1024, 1024), 1024)
            prod = jnp.dot(
                block, wv[pl.ds(mult(s * 512, 512), 512), cols], preferred_element_type=F32
            )
            if o == 0:
                pre[:, cols] = prod
            else:
                pre[:, cols] += prod

    for i in range(2):
        recv(asib[i], a_part(q_s, halves[i]))
    for o in range(2):
        aggregate(o, 0, 1)
        aggregate(o, 1, 1)
    recv(ay[0], a_part(q_y, 1 - x))
    send(afwd[0], a_part(q_y, 1 - x), a_part(q_y, 1 - x), sib)
    recv(afwd[0], a_part(q_d, 1 - x))
    aggregate(0, 0, 0)
    line_recv(hz, h_part, 2, 0)
    line_send(hz, h_part, 3, 0)
    aggregate(1, 0, 0)
    line_recv(hz, h_part, 2, 1)
    line_send(hz, h_part, 3, 1)
    for c, u in ((0, 0), (0, 1), (1, 1)):
        aggregate(2, c, u)
    recv(ay[1], a_part(q_y, x))
    send(afwd[1], a_part(q_y, x), a_part(q_y, x), sib)
    recv(afwd[1], a_part(q_d, x))
    for o in range(3):
        aggregate(o, 1, 0)
        combine(o)
        if o < 2:
            share(o)
    linear(0)
    linear(1)
    for c in range(NC):
        line_recv(hz, h_part, 3, c)
    for c, u in ((0, 0), (0, 1), (1, 0), (1, 1)):
        aggregate(3, c, u)
    linear(2)
    combine(3)
    share(3)
    share(2)
    linear(3)

    def p_part(c, h):
        return pt.at[pl.ds(mult(c * 1024 + h * 512, 512), 512)]

    def activate(c, h):
        @pl.loop(0, 4)
        def _(i):
            t = c * 8 + h * 4 + i
            cols = pl.ds(mult(t * 128, 128), 128)
            v = pre[:, cols] + bias32[pl.ds(t, 1), :]
            sig = jax.nn.sigmoid(v)
            out_ref[:, cols] = v * sig
            slope = sig * (1.0 + v * (1.0 - sig))
            d32 = (cot_ref[:, cols].astype(F32) * slope).astype(BF16).astype(F32)
            pt[pl.ds(mult(t * 128, 128), 128), :] = d32.T.astype(BF16)
            bsum[0, pl.ds(t, 1), :] = jnp.sum(d32, axis=0, keepdims=True)

    b_own, b_x = x * 4 + q, (1 - x) * 4 + q
    px, py, pyf, ps, psf, pd, pdf = ([new(), new()] for _ in range(7))
    b_ids = [new() for _ in range(6)]

    def p_at(b, h):
        return ptg.at[b, pl.ds(h * 512, 512)]

    def p_send(h):
        send(px[h], p_part(1 - x, h), p_at(b_own, h), xn)
        send(py[h], p_part(x, h), p_at(b_own, h), yn)
        send(ps[h], p_part(x, h), p_at(b_own, h), sib)
        ptg[b_own, h * 512:(h + 1) * 512] = pt[pl.ds(mult(x * 1024 + h * 512, 512), 512), :]

    def p_relay_x(h):
        recv(px[h], p_at(b_x, h))
        send(pyf[h], p_at(b_x, h), p_at(b_x, h), yn)
        send(psf[h], p_at(b_x, h), p_at(b_x, h), sib)
        recv(py[h], p_at(x * 4 + q_y, h))
        send(pd[h], p_at(x * 4 + q_y, h), p_at(x * 4 + q_y, h), sib)

    def p_relay_y(h):
        recv(pyf[h], p_at((1 - x) * 4 + q_y, h))
        send(pdf[h], p_at((1 - x) * 4 + q_y, h), p_at((1 - x) * 4 + q_y, h), sib)

    def p_last(h):
        recv(ps[h], p_at(x * 4 + q_s, h))
        recv(psf[h], p_at((1 - x) * 4 + q_s, h))
        recv(pd[h], p_at(x * 4 + q_d, h))
        recv(pdf[h], p_at((1 - x) * 4 + q_d, h))

    activate(1 - x, 0)
    activate(x, 0)
    p_send(0)
    activate(1 - x, 1)
    activate(x, 1)

    @pl.loop(0, 2)
    def _(i):
        acc = jnp.dot(
            wv[pl.ds(mult(i * 1024, 1024), 1024), :], pt[...], preferred_element_type=F32
        ).astype(BF16)
        for j in range(2):
            for qq in range(4):
                first = j * 512 + qq * 128
                dls[qq, i * 2 + j] = acc[first:first + 128]

    dl_to = [
        (1 - x, y, k), (1 - x, y, 1 - k), (x, y, 1 - k),
        (x, 1 - y, k), (x, 1 - y, 1 - k), (1 - x, 1 - y, k), (1 - x, 1 - y, 1 - k),
    ]
    dl_ids = [new() for _ in dl_to]

    def send_layer_grad(which):
        for i in which:
            xx, yy, kk = dl_to[i]
            send(dl_ids[i], dls.at[2 * yy + kk], dlq.at[b_own], at(xx, yy, z, kk))

    p_send(1)
    send(b_ids[0], bsum.at[0], bsum.at[1], xn)
    dlq[b_own] = dls[q]
    p_relay_x(0)
    send_layer_grad((0, 1, 2))
    p_relay_x(1)
    p_relay_y(0)
    recv(b_ids[0], bsum.at[1])
    bsum[2] = bsum[0] + bsum[1]
    send(b_ids[1], bsum.at[2], bsum.at[3], yn)
    for o in range(4):
        recv(l_id[o], lay.at[slice_at(o), pl.ds(mult((1 - x) * 512, 512), 512)])
    p_last(0)

    dw_ids = [[new() for _ in range(3)] for _ in range(2)]

    def weight_grad(h):
        rows = pl.ds(h * 512, 512)
        lhs = jnp.concatenate([ptg[b, rows, :] for b in range(8)], axis=1)
        rhs = jnp.concatenate([lay[s] for s in range(4)], axis=1)
        acc = jnp.dot(lhs, rhs, preferred_element_type=F32)
        for s in range(4):
            dwf[s, rows, :] = acc[:, s * 128:(s + 1) * 128]
            dwp[s, rows, :] = acc[:, s * 128:(s + 1) * 128].astype(BF16)
        for d in (2, 1, 3):
            to = (z + d) % 4
            send(dw_ids[h][d - 1], dwp.at[to, rows], dwr.at[z, rows], at(x, y, to, k))

    weight_grad(0)
    p_relay_y(1)
    send_layer_grad((3, 4, 5, 6))
    recv(b_ids[1], bsum.at[3])
    bsum[4] = bsum[2] + bsum[3]
    send(b_ids[2], bsum.at[4], bsum.at[5], sib)
    p_last(1)
    weight_grad(1)
    for c in range(2):
        recv(ez[c], e_part(q, c), mids)
        send(ey[c], e_part(q, c), e_part(q, c), yn, mids, mids)
        send(esib[c], e_part(q, c), e_part(q, c), sib, mids, mids)
    recv(b_ids[2], bsum.at[5])
    bsum[6] = bsum[4] + bsum[5]
    for d in (1, 2, 3):
        send(b_ids[2 + d], bsum.at[6], bsum.at[6 + d], at(x, y, (z + d) % 4, k))

    def layer_grads_here(cond):
        for i, (xx, yy, kk) in zip(dl_ids, dl_to):
            recv(i, dlq.at[xx * 4 + 2 * yy + kk], cond)

    f_in = [new() for _ in range(3)]
    f_out = [new() for _ in range(2)]
    f_fin = new()
    own_half = x == z // 2

    def grads(dl, a, scale, at_z, first, n, t, width):
        cols = pl.ds(mult(t * width, width), width)
        lhs = jnp.concatenate(
            [dl[b, pl.ds(first, n)].reshape(n * 128, 128) for b in range(8)], axis=1
        )
        acc = jnp.dot(lhs, a[:, cols], preferred_element_type=F32)
        per = width // 256
        own = jnp.where(own_half & (t // (4 // per) == at_z % 2), 1.0, 0.0)
        diag = []
        for j in range(per):
            qq = (t % (4 // per)) * per + j
            for c in range(2):
                row = scale[qq, c:c + 1, :] * own
                diag.append(
                    dl[c * 4 + qq, pl.ds(first, n)].reshape(n * 128, 128).astype(F32) * row
                )
        return acc + jnp.concatenate(diag, axis=1), cols

    def grads_here(first, n):
        @pl.loop(0, 4)
        def _(t):
            acc, cols = grads(dlq, adj, sbuf, z, first, n, t, 512)
            for i in range(n):
                dff[first + i, :, cols] = acc[i * 128:(i + 1) * 128]

    def grads_end(s):
        @pl.loop(0, 4)
        def _(t):
            acc, cols = grads(dle, adj_e, sbuf_e, e, s, 1, t, 512)
            tot = dff[s, :, cols] + acc
            dff[s, :, cols] = tot
            dfp[s, :, cols] = tot.astype(BF16)

    layer_grads_here(mids)

    @pl.when(mids)
    def _():
        grads_here(2 * pair, 2)
        dfp[e] = dff[e].astype(BF16)
    send(f_fin, dfp.at[e], fin.at[0], end_dev, mids, ends)

    @pl.when(mids)
    def _():
        grads_here(2 * (1 - pair), 2)

    def end_send():
        layer_grads_here(ends)
        for j, s in enumerate((m2, e2, m)):
            send(f_in[j], dlq.at[:, s], dle.at[:, s], mid_dev, ends, mids)

        @pl.when(ends)
        def _():
            grads_here(e, 1)

    def mid_ready():
        recv(es, sbuf_e, mids)
        for c in range(2):
            recv(ey[c], e_part(q_y, c), mids)
            send(efwd[c], e_part(q_y, c), e_part(q_y, c), sib, mids, mids)
        for c in range(2):
            recv(esib[c], e_part(q_s, c), mids)
            recv(efwd[c], e_part(q_d, c), mids)

    def mid_send(j):
        s_to = (m2, e2, m)[j]
        recv(f_in[j], dle.at[:, s_to], mids)

        @pl.when(mids)
        def _():
            grads_end(s_to)
        if j < 2:
            send(f_out[j], dfp.at[s_to], fin.at[1], at(x, y, s_to, k), mids, (mids, ends)[j])

    def piece(s, qq, c, h):
        return dw_ref.at[(s * 4 + qq) * 4 + c * 2 + h]

    gz = tuple({(d, h): new() for d in (1, 2, 3) for h in (0, 1)} for _ in range(2))
    gx, gy, gxy, gyx = ({(h, o): new() for h in (0, 1) for o in range(4)} for _ in range(4))
    gs, gsd = ([new() for _ in range(4)] for _ in range(2))

    def z_piece(s, h):
        return piece(s, q, x, h)

    def finish(h):
        for d in (1, 2, 3):
            recv(dw_ids[h][d - 1], dwr.at[(z - d) % 4, pl.ds(h * 512, 512)])
        for t in range(4):
            rr = pl.ds(h * 512 + t * 128, 128)
            tot = dwf[z, rr, :]
            for d in (1, 2, 3):
                tot = tot + dwr[(z + d) % 4, rr, :].astype(F32)
            dw_ref[(z * 4 + q) * 4 + x * 2 + h, :, t * 128:(t + 1) * 128] = tot.T.astype(BF16)
        line_send(gz, z_piece, 1, h)
        spread(h, 0)

    def spread(h, o):
        src = piece(slice_at(o), q, x, h)
        send(gx[h, o], src, src, xn)
        send(gy[h, o], src, src, yn)

    def whole(s, qq):
        return dw_ref.at[pl.ds((s * 4 + qq) * 4, 4)]

    def part(ref, i):
        return ref.at[pl.ds(i * 64, 64)]

    def relay(h, o):
        s = slice_at(o)
        from_x, from_y = piece(s, q, 1 - x, h), piece(s, q_y, x, h)
        recv(gx[h, o], from_x)
        send(gxy[h, o], part(from_x, 0), part(from_x, 0), yn)
        if h == 1:
            send(gs[o], whole(s, q), whole(s, q), sib)
        recv(gy[h, o], from_y)
        send(gyx[h, o], part(from_y, 1), part(from_y, 1), xn)

    def relay_diag(h, o):
        block = piece(slice_at(o), q_y, 1 - x, h)
        recv(gxy[h, o], part(block, 0))
        recv(gyx[h, o], part(block, 1))
        if h == 1:
            send(gsd[o], whole(slice_at(o), q_y), whole(slice_at(o), q_y), sib)

    def last(o):
        recv(gs[o], whole(slice_at(o), q_s))
        recv(gsd[o], whole(slice_at(o), q_d))

    def along(h, d):
        line_recv(gz, z_piece, d, h)
        if d < 3:
            line_send(gz, z_piece, d + 1, h)
        spread(h, d)

    finish(0)
    end_send()
    mid_ready()
    along(0, 1)
    relay(0, 0)
    finish(1)
    along(0, 2)
    relay(0, 1)
    relay_diag(0, 0)
    along(1, 1)
    mid_send(0)
    relay(1, 0)
    relay_diag(0, 1)
    along(0, 3)
    mid_send(1)
    relay(0, 2)
    relay_diag(1, 0)
    along(1, 2)
    relay(1, 1)
    relay_diag(0, 2)
    along(1, 3)
    mid_send(2)
    relay(0, 3)
    relay_diag(1, 1)
    relay(1, 2)
    relay_diag(0, 3)
    relay(1, 3)
    relay_diag(1, 2)
    relay_diag(1, 3)
    for d in (1, 2, 3):
        recv(b_ids[2 + d], bsum.at[6 + d])
    db_ref[...] = bsum[6] + bsum[7] + bsum[8] + bsum[9]

    recv(f_fin, fin.at[0], ends)
    recv(f_out[0], fin.at[1], mids)
    recv(f_out[1], fin.at[1], ends)

    @pl.loop(0, 16)
    def _(t):
        cols = pl.ds(mult(t * 128, 128), 128)
        first = jnp.where(ends, fin[0, :, cols].astype(F32), 0.0)
        tot = dff[z, :, cols] + first + fin[1, :, cols].astype(F32)
        dfeat_ref[pl.ds(mult(t * 128, 128), 128), :] = tot.T

    for o in range(4):
        last(o)
    assert not pending and count[0] <= N_SEMS, count
    for i, (c, cond) in sent_by.items():
        when(cond, c.wait_send)


def widen_kernel(dw_ref, out_ref, dfeat_ref, db_ref, dw_out, out_out, dfeat_out, db_out, wide, sem):
    copies = [
        pltpu.make_async_copy(src, dst, sem.at[16 + i])
        for i, (src, dst) in enumerate(
            ((out_ref, out_out), (dfeat_ref, dfeat_out), (db_ref, db_out))
        )
    ]
    for c in copies:
        c.start()
    rows = [
        pltpu.make_async_copy(wide.at[i], dw_out.at[pl.ds(i * 128, 128)], sem.at[i])
        for i in range(16)
    ]
    for i in range(16):
        for j in range(4):
            wide[i, :, j * 512:(j + 1) * 512] = dw_ref[4 * i + j].astype(F32)
        rows[i].start()
    for c in copies + rows:
        c.wait()


N_SEMS = 145


def per_device_fused(features, weight, bias, self_scale, adj_tiles, tile_ids, tile_counts, cotangent):
    vmem = pl.BlockSpec(memory_space=pltpu.VMEM)
    smem = pl.BlockSpec(memory_space=pltpu.SMEM)
    hbm = pl.BlockSpec(memory_space=pl.ANY)
    outputs, d_features, gathered, d_bias = pl.pallas_call(
        fused_kernel,
        out_shape=(
            pltpu.VMEM((128, 2048), F32),
            pltpu.VMEM((2048, 128), F32),
            pltpu.VMEM((64, 128, 512), BF16),
            pltpu.VMEM((16, 128), F32),
        ),
        in_specs=[smem, smem, vmem, hbm, hbm, vmem, vmem, vmem],
        out_specs=(vmem, vmem, vmem, vmem),
        scratch_shapes=[
            pltpu.VMEM((1024, 2048), BF16),
            pltpu.VMEM((1024, 2048), BF16),
            pltpu.VMEM((4, 2048, 128), BF16),
            pltpu.VMEM((2048, 2048), BF16),
            pltpu.VMEM((4, 8, 128), F32),
            pltpu.VMEM((4, 8, 128), F32),
            pltpu.VMEM((8, 128, 128), F32),
            pltpu.VMEM((4, 512, 128), BF16),
            pltpu.VMEM((4, 512, 128), BF16),
            pltpu.VMEM((4, 512, 128), F32),
            pltpu.VMEM((4, 1024, 128), BF16),
            pltpu.VMEM((16, 128, 128), BF16),
            pltpu.VMEM((128, 2048), F32),
            pltpu.VMEM((2048, 128), BF16),
            pltpu.VMEM((8, 1024, 128), BF16),
            pltpu.VMEM((4, 4, 128, 128), BF16),
            pltpu.VMEM((8, 4, 128, 128), BF16),
            pltpu.VMEM((4, 1024, 128), F32),
            pltpu.VMEM((4, 1024, 128), BF16),
            pltpu.VMEM((4, 1024, 128), BF16),
            pltpu.VMEM((4, 128, 2048), F32),
            pltpu.VMEM((4, 128, 2048), BF16),
            pltpu.VMEM((8, 4, 128, 128), BF16),
            pltpu.VMEM((2, 128, 2048), BF16),
            pltpu.VMEM((10, 16, 128), F32),
            pltpu.VMEM((16, 128), F32),
            pltpu.SemaphoreType.DMA((N_SEMS,)),
            pltpu.SemaphoreType.DMA((N_SEMS,)),
            pltpu.SemaphoreType.DMA((3,)),
        ],
        compiler_params=pltpu.CompilerParams(
            collective_id=0, has_side_effects=True, vmem_limit_bytes=53 * MIB
        ),
        cost_estimate=pl.CostEstimate(
            flops=7_600_000_000, bytes_accessed=24 * MIB, transcendentals=262144
        ),
    )(
        tile_ids[0, 0], tile_counts[0], adj_tiles[0, 0], features, weight,
        bias.reshape(16, 128), self_scale.reshape(2, 128), cotangent,
    )
    d_weight, outputs, d_features, d_bias = pl.pallas_call(
        widen_kernel,
        out_shape=(
            jax.ShapeDtypeStruct((2048, 2048), F32),
            jax.ShapeDtypeStruct((128, 2048), F32),
            jax.ShapeDtypeStruct((2048, 128), F32),
            jax.ShapeDtypeStruct((16, 128), F32),
        ),
        in_specs=[vmem] * 4,
        out_specs=(hbm, hbm, hbm, hbm),
        scratch_shapes=[pltpu.VMEM((16, 128, 2048), F32), pltpu.SemaphoreType.DMA((19,))],
        compiler_params=pltpu.CompilerParams(vmem_limit_bytes=30 * MIB),
    )(gathered, outputs, d_features, d_bias)
    return outputs, d_features, d_weight, d_bias.reshape(2048)


def solution(mesh):
    fits = dict(mesh.shape) == {"row": 16, "col": 2}

    def run(*arrays):
        fused = fits and arrays[0].shape == (4096, 2048) and arrays[4].shape[2] == 32
        return jax.shard_map(
            per_device_fused if fused else per_device_any,
            mesh=mesh,
            in_specs=(
                P("col", "row"),
                P(),
                P(),
                P("row"),
                P("row", "col", None, None, None),
                P("row", "col", None),
                P("row", "col"),
                P(("row", "col"), None),
            ),
            out_specs=(P(("row", "col"), None), P("col", "row"), P(), P()),
            check_vma=False,
        )(*arrays)

    return run
```

```python
import jax
import jax.numpy as jnp
from jax import lax
from jax.experimental import pallas as pl
from jax.experimental.pallas import tpu as pltpu
from jax.sharding import PartitionSpec as P

MESH = pl.DeviceIdType.MESH
F32 = jnp.float32
BF16 = jnp.bfloat16
MIB = 2**20
ORDER = (
    "H P f0 E0",
    "a01 r00 R f1",
    "E2 E1 a02 r01",
    "d00 a11 M0 r10",
    "d01 a03 M1 G0",
    "r02 d10 a12 r03",
    "r11 d02 a13 M2",
    "d11 r12 d03 G1",
    "r13 d12 d13",
)
NC = 2


def dense_block(tiles, ids, count, tile_rows, tile_cols):
    slots = jnp.arange(tiles.shape[0], dtype=jnp.int32)
    live = jnp.where((slots < count)[:, None, None], tiles, jnp.zeros_like(tiles))
    blank = jnp.zeros((tile_rows * tile_cols, 128, 128), tiles.dtype)
    placed = blank.at[ids].add(live, unique_indices=True)
    placed = placed.reshape(tile_rows, tile_cols, 128, 128)
    return placed.transpose(0, 2, 1, 3).reshape(tile_rows * 128, tile_cols * 128)


def per_device_any(features, weight, bias, self_scale, adj_tiles, tile_ids, tile_counts, cotangent):
    row_block = self_scale.shape[0]
    col_block = features.shape[0]
    block = dense_block(
        adj_tiles[0, 0], tile_ids[0, 0], tile_counts[0, 0], row_block // 128, col_block // 128
    )
    start_row = lax.axis_index("row") * row_block
    col_no = lax.axis_index("col")
    inside = col_no == start_row // col_block
    offset = jnp.where(inside, start_row - col_no * col_block, 0)
    self_rows = jnp.where(inside, self_scale, 0.0)[:, None]
    piece = lax.all_gather(features, "row", axis=1, tiled=True)
    terms = jnp.dot(block, piece, preferred_element_type=F32)
    terms = terms + self_rows * lax.dynamic_slice_in_dim(piece, offset, row_block, 0)
    layer_in = lax.psum_scatter(terms, "col", scatter_dimension=0, tiled=True).astype(BF16)
    pre_act = jnp.dot(layer_in, weight, preferred_element_type=F32) + bias.astype(F32)
    sig = jax.nn.sigmoid(pre_act)
    outputs = pre_act * sig
    slope = sig * (1.0 + pre_act * (1.0 - sig))
    d_pre = (cotangent.astype(F32) * slope).astype(BF16)
    d_weight = lax.dot_general(
        layer_in, d_pre, (((0,), (0,)), ((), ())), preferred_element_type=F32
    )
    d_bias = jnp.sum(d_pre.astype(F32), axis=0)
    d_weight, d_bias = lax.psum((d_weight, d_bias), ("row", "col"))
    d_layer = lax.dot_general(
        d_pre, weight, (((1,), (1,)), ((), ())), preferred_element_type=F32
    ).astype(BF16)
    whole = lax.all_gather(d_layer, "col", axis=0, tiled=True)
    spread = lax.dot_general(block, whole, (((0,), (0,)), ((), ())), preferred_element_type=F32)
    own = lax.dynamic_slice_in_dim(spread, offset, row_block, 0) + self_rows * whole
    spread = lax.dynamic_update_slice_in_dim(spread, own, offset, 0)
    d_features = lax.psum_scatter(spread, "row", scatter_dimension=1, tiled=True)
    return outputs, d_features, d_weight, d_bias


def fused_kernel(
    ids_ref, count_ref, tiles_ref, feat_ref, w_ref, bias_ref, scale_ref, cot_ref,
    out_ref, dfeat_ref, dw_ref, db_ref,
    adj, adj_e, hid, wv, sbuf, sbuf_e, scol, xs, xr, keep, lay, xrow, pre, pt, ptg, dls, dlq,
    dwf, dwp, dwr, dff, dfp, dle, fin, bsum, bias32, ssem, rsem, lsem,
):
    r = lax.axis_index("row")
    x = lax.axis_index("col")
    z = r // 4
    y = (r // 2) % 2
    k = r % 2
    q = 2 * y + k
    ends = (z == 0) | (z == 3)
    mids = (z == 1) | (z == 2)

    def at(xx, yy, zz, kk):
        return (zz * 4 + yy * 2 + kk, xx)

    sib = at(x, y, z, 1 - k)
    xn = at(1 - x, y, z, k)
    yn = at(x, 1 - y, z, k)
    dg = at(x, 1 - y, z, 1 - k)
    zr = at(x, y, jnp.minimum(z + 1, 3), k)
    zl = at(x, y, jnp.maximum(z - 1, 0), k)
    q_y = 2 * (1 - y) + k
    q_s = 2 * y + 1 - k
    q_d = 3 - q

    count = [0]
    sent_by = {}
    pending = {}

    def new():
        count[0] += 1
        return count[0] - 1

    def when(cond, fn):
        if cond is None:
            fn()
        else:
            pl.when(cond)(fn)

    def copy(i, src, dst, to):
        return pltpu.make_async_remote_copy(
            src_ref=src, dst_ref=dst, send_sem=ssem.at[i], recv_sem=rsem.at[i],
            device_id=to, device_id_type=MESH,
        )

    def send(i, src, dst, to, cond=None, rcond=None):
        c = copy(i, src, dst, to)
        when(cond, c.start)
        sent_by[i] = (c, cond)
        pending[i] = (dst, rcond)

    def recv(i, dst, cond=None):
        pending.pop(i, None)
        c = copy(i, dst, dst, sib)
        when(cond, c.wait_recv)

    def slice_at(o):
        return [z, z + 1 - 2 * (z % 2), 2 - z // 2, 3 - 3 * (z // 2)][o]

    def mult(v, n):
        return pl.multiple_of(v, n)

    barrier = pltpu.get_barrier_semaphore()
    near = [(sib, None), (xn, None), (yn, None), (zr, z <= 2), (zl, z >= 1)]
    for peer, cond in near:
        when(cond, lambda peer=peer: pl.semaphore_signal(
            barrier, inc=1, device_id=peer, device_id_type=MESH
        ))

    w_copy = pltpu.make_async_copy(w_ref, wv, lsem.at[0])
    h_copy = pltpu.make_async_copy(feat_ref, hid.at[z], lsem.at[1])
    h_copy.start()

    for c in range(2):
        @pl.loop(0, 16)
        def _(t, c=c):
            slot = jnp.int32(0)
            for i in range(32):
                slot = jnp.where(ids_ref[i] == c * 16 + t, i, slot)
            live = jnp.where(slot < count_ref[0], 1.0, 0.0)
            tile = tiles_ref[slot].astype(F32) * live
            adj[pl.ds(mult(c * 512 + q * 128, 128), 128), pl.ds(mult(t * 128, 128), 128)] = (
                tile.astype(BF16)
            )
    for i in range(4):
        sbuf[q, 2 * i:2 * i + 2, :] = scale_ref[...]
    bias32[...] = bias_ref[...].astype(F32)
    h_copy.wait()
    w_copy.start()
    pl.semaphore_wait(barrier, jnp.where(ends, 4, 5))

    def h_part(s, c):
        return hid.at[s, pl.ds(c * (2048 // NC), 2048 // NC)]

    right = {(d, c): new() for d in (1, 2, 3) for c in range(NC)}
    left = {(d, c): new() for d in (1, 2, 3) for c in range(NC)}

    def line_send(ids, part, d, c, own_ok=True):
        sr, sl = jnp.maximum(z - (d - 1), 0), jnp.minimum(z + d - 1, 3)
        send(ids[0][d, c], part(sr, c), part(sr, c), zr, (z >= d - 1) & (z <= 2), z >= d)
        send(ids[1][d, c], part(sl, c), part(sl, c), zl, (z <= 4 - d) & (z >= 1), z <= 3 - d)

    def line_recv(ids, part, d, c):
        sr, sl = jnp.maximum(z - d, 0), jnp.minimum(z + d, 3)
        recv(ids[0][d, c], part(sr, c), z >= d)
        recv(ids[1][d, c], part(sl, c), z <= 3 - d)

    hz = (right, left)
    for c in range(NC):
        line_send(hz, h_part, 1, c)

    s_id = [new() for _ in range(3)]
    send(s_id[0], sbuf.at[q], sbuf.at[q], yn)
    send(s_id[1], sbuf.at[q], sbuf.at[q], sib)

    def a_part(qq, c):
        return adj.at[pl.ds(mult(c * 512 + qq * 128, 128), 128)]

    halves = (1 - x, x)
    ay, asib, afwd = ([new(), new()] for _ in range(3))
    for i, c in enumerate(halves):
        send(asib[i], a_part(q, c), a_part(q, c), sib)
    send(ay[0], a_part(q, 1 - x), a_part(q, 1 - x), yn)

    line_recv(hz, h_part, 1, 0)
    line_send(hz, h_part, 2, 0)
    send(ay[1], a_part(q, x), a_part(q, x), yn)

    recv(s_id[0], sbuf.at[q_y])
    send(s_id[2], sbuf.at[q_y], sbuf.at[q_y], sib)
    recv(s_id[1], sbuf.at[q_s])
    recv(s_id[2], sbuf.at[q_d])
    inside = jnp.where(x == z // 2, 1.0, 0.0)
    for b in range(8):
        row = sbuf[b % 4, b // 4:b // 4 + 1, :] * inside
        scol[b] = jnp.broadcast_to(row, (128, 128)).T

    line_recv(hz, h_part, 1, 1)
    line_send(hz, h_part, 2, 1)

    pair = z // 2
    e, m = 3 * pair, 1 + pair
    e2, m2 = 3 - 3 * pair, 2 - pair
    mid_dev, end_dev = at(x, y, m, k), at(x, y, e, k)

    def e_part(qq, c):
        return adj_e.at[pl.ds(mult(c * 512 + qq * 128, 128), 128)]

    ez, ezy, esib, efwd = ([new(), new()] for _ in range(4))
    es = new()
    for c in range(2):
        send(ez[c], a_part(q, c), e_part(q, c), mid_dev, ends, mids)
    send(es, sbuf, sbuf_e, mid_dev, ends, mids)

    x_id = [[new(), new()] for _ in range(4)]
    l_id = [new() for _ in range(4)]
    row_id = [[new() for _ in range(3)] for _ in range(4)]
    w_waited = []

    def aggregate(o, c, u):
        s = slice_at(o)
        first = (1 - y if u == 0 else y) * 256
        rows = pl.ds(mult(first, 256), 256)
        acc = jnp.dot(
            adj[pl.ds(mult(halves[c] * 512 + first, 256), 256), :], hid[s],
            preferred_element_type=F32,
        )
        own = []
        for i in range(2):
            qq = first // 128 + i
            at_node = mult((z % 2) * 1024 + qq * 256 + halves[c] * 128, 128)
            own.append(scol[halves[c] * 4 + qq] * hid[s, pl.ds(at_node, 128), :].astype(F32))
        acc = acc + jnp.concatenate(own, axis=0)
        if c == 0:
            xs[o, rows] = acc.astype(BF16)
            send(x_id[o][u], xs.at[o, rows], xr.at[o, rows], xn)
        else:
            keep[o, rows] = acc

    def combine(o):
        s = slice_at(o)
        sends = list(zip(row_id[o], (q_y, q_d, q_s), (yn, dg, sib)))
        for u in range(2):
            first = (1 - y if u == 0 else y) * 256
            rows = pl.ds(mult(first, 256), 256)
            recv(x_id[o][u], xr.at[o, rows])
            mine = pl.ds(mult(x * 512 + first, 256), 256)
            lay[s, mine, :] = (keep[o, rows] + xr[o, rows].astype(F32)).astype(BF16)
            for i, qq, to in (sends[:2], sends[2:])[u]:
                piece_rows = pl.ds(mult(x * 512 + qq * 128, 128), 128)
                send(i, lay.at[s, piece_rows], xrow.at[s * 4 + q], to)
        xrow[s * 4 + q] = lay[s, pl.ds(mult(x * 512 + q * 128, 128), 128), :]

    def share(o):
        half = lay.at[slice_at(o), pl.ds(mult(x * 512, 512), 512)]
        send(l_id[o], half, half, xn)

    def linear(o):
        s = slice_at(o)
        for i, qq in zip(row_id[o], (q_y, q_d, q_s)):
            recv(i, xrow.at[s * 4 + qq])
        if not w_waited:
            w_copy.wait()
            w_waited.append(True)
        block = jnp.concatenate([xrow[s * 4 + i] for i in range(4)], axis=1)

        @pl.loop(0, 2)
        def _(t):
            cols = pl.ds(mult(t * 1024, 1024), 1024)
            prod = jnp.dot(
                block, wv[pl.ds(mult(s * 512, 512), 512), cols], preferred_element_type=F32
            )
            if o == 0:
                pre[:, cols] = prod
            else:
                pre[:, cols] += prod

    for i in range(2):
        recv(asib[i], a_part(q_s, halves[i]))
    for o in range(2):
        aggregate(o, 0, 1)
        aggregate(o, 1, 1)
    recv(ay[0], a_part(q_y, 1 - x))
    send(afwd[0], a_part(q_y, 1 - x), a_part(q_y, 1 - x), sib)
    recv(afwd[0], a_part(q_d, 1 - x))
    aggregate(0, 0, 0)
    line_recv(hz, h_part, 2, 0)
    line_send(hz, h_part, 3, 0)
    aggregate(1, 0, 0)
    line_recv(hz, h_part, 2, 1)
    line_send(hz, h_part, 3, 1)
    for c, u in ((0, 0), (0, 1), (1, 1)):
        aggregate(2, c, u)
    recv(ay[1], a_part(q_y, x))
    send(afwd[1], a_part(q_y, x), a_part(q_y, x), sib)
    for c in range(2):
        send(ezy[c], a_part(q_y, c), e_part(q_y, c), mid_dev, ends, mids)
    recv(afwd[1], a_part(q_d, x))
    for o in range(3):
        aggregate(o, 1, 0)
        combine(o)
        if o < 2:
            share(o)
    linear(0)
    linear(1)
    for c in range(NC):
        line_recv(hz, h_part, 3, c)
    for c, u in ((0, 0), (0, 1), (1, 0), (1, 1)):
        aggregate(3, c, u)
    linear(2)
    combine(3)
    share(3)
    share(2)
    linear(3)

    def p_part(c, h):
        return pt.at[pl.ds(mult(c * 1024 + h * 512, 512), 512)]

    def activate(c, h):
        @pl.loop(0, 4)
        def _(i):
            t = c * 8 + h * 4 + i
            cols = pl.ds(mult(t * 128, 128), 128)
            v = pre[:, cols] + bias32[pl.ds(t, 1), :]
            sig = jax.nn.sigmoid(v)
            out_ref[:, cols] = v * sig
            slope = sig * (1.0 + v * (1.0 - sig))
            d32 = (cot_ref[:, cols].astype(F32) * slope).astype(BF16).astype(F32)
            pt[pl.ds(mult(t * 128, 128), 128), :] = d32.T.astype(BF16)
            bsum[0, pl.ds(t, 1), :] = jnp.sum(d32, axis=0, keepdims=True)

    b_own, b_x = x * 4 + q, (1 - x) * 4 + q
    px, py, pyf, ps, psf, pd, pdf = ([new(), new()] for _ in range(7))
    b_ids = [new() for _ in range(6)]

    def p_at(b, h):
        return ptg.at[b, pl.ds(h * 512, 512)]

    def p_send(h):
        send(px[h], p_part(1 - x, h), p_at(b_own, h), xn)
        send(py[h], p_part(x, h), p_at(b_own, h), yn)
        send(ps[h], p_part(x, h), p_at(b_own, h), sib)
        ptg[b_own, h * 512:(h + 1) * 512] = pt[pl.ds(mult(x * 1024 + h * 512, 512), 512), :]

    def p_relay_x(h):
        recv(px[h], p_at(b_x, h))
        send(pyf[h], p_at(b_x, h), p_at(b_x, h), yn)
        send(psf[h], p_at(b_x, h), p_at(b_x, h), sib)
        recv(py[h], p_at(x * 4 + q_y, h))
        send(pd[h], p_at(x * 4 + q_y, h), p_at(x * 4 + q_y, h), sib)

    def p_relay_y(h):
        recv(pyf[h], p_at((1 - x) * 4 + q_y, h))
        send(pdf[h], p_at((1 - x) * 4 + q_y, h), p_at((1 - x) * 4 + q_y, h), sib)

    def p_last(h):
        recv(ps[h], p_at(x * 4 + q_s, h))
        recv(psf[h], p_at((1 - x) * 4 + q_s, h))
        recv(pd[h], p_at(x * 4 + q_d, h))
        recv(pdf[h], p_at((1 - x) * 4 + q_d, h))

    activate(1 - x, 0)
    activate(x, 0)
    p_send(0)
    activate(1 - x, 1)
    activate(x, 1)

    @pl.loop(0, 2)
    def _(i):
        acc = jnp.dot(
            wv[pl.ds(mult(i * 1024, 1024), 1024), :], pt[...], preferred_element_type=F32
        ).astype(BF16)
        for j in range(2):
            for qq in range(4):
                first = j * 512 + qq * 128
                dls[qq, i * 2 + j] = acc[first:first + 128]

    dl_to = [
        (1 - x, y, k), (1 - x, y, 1 - k), (x, y, 1 - k),
        (x, 1 - y, k), (x, 1 - y, 1 - k), (1 - x, 1 - y, k), (1 - x, 1 - y, 1 - k),
    ]
    dl_ids = [new() for _ in dl_to]

    def send_layer_grad(which):
        for i in which:
            xx, yy, kk = dl_to[i]
            send(dl_ids[i], dls.at[2 * yy + kk], dlq.at[b_own], at(xx, yy, z, kk))

    p_send(1)
    send(b_ids[0], bsum.at[0], bsum.at[1], xn)
    dlq[b_own] = dls[q]
    p_relay_x(0)
    send_layer_grad((0, 1, 2))
    p_relay_x(1)
    p_relay_y(0)
    recv(b_ids[0], bsum.at[1])
    bsum[2] = bsum[0] + bsum[1]
    send(b_ids[1], bsum.at[2], bsum.at[3], yn)
    for o in range(4):
        recv(l_id[o], lay.at[slice_at(o), pl.ds(mult((1 - x) * 512, 512), 512)])
    p_last(0)

    dw_ids = [[new() for _ in range(3)] for _ in range(2)]

    def weight_grad(h):
        rows = pl.ds(h * 512, 512)
        lhs = jnp.concatenate([ptg[b, rows, :] for b in range(8)], axis=1)
        rhs = jnp.concatenate([lay[s] for s in range(4)], axis=1)
        acc = jnp.dot(lhs, rhs, preferred_element_type=F32)
        for s in range(4):
            dwf[s, rows, :] = acc[:, s * 128:(s + 1) * 128]
            dwp[s, rows, :] = acc[:, s * 128:(s + 1) * 128].astype(BF16)

    def weight_send(h):
        rows = pl.ds(h * 512, 512)
        for d in (2, 1, 3):
            to = (z + d) % 4
            send(dw_ids[h][d - 1], dwp.at[to, rows], dwr.at[z, rows], at(x, y, to, k))

    weight_grad(0)
    weight_send(0)
    p_relay_y(1)
    send_layer_grad((3, 4, 5, 6))
    recv(b_ids[1], bsum.at[3])
    bsum[4] = bsum[2] + bsum[3]
    send(b_ids[2], bsum.at[4], bsum.at[5], sib)
    p_last(1)
    weight_grad(1)
    weight_send(1)
    recv(b_ids[2], bsum.at[5])
    bsum[6] = bsum[4] + bsum[5]
    for d in (1, 2, 3):
        send(b_ids[2 + d], bsum.at[6], bsum.at[6 + d], at(x, y, (z + d) % 4, k))

    def layer_grads_here(cond):
        for i, (xx, yy, kk) in zip(dl_ids, dl_to):
            recv(i, dlq.at[xx * 4 + 2 * yy + kk], cond)

    f_in = [new() for _ in range(3)]
    f_out = [[new(), new()] for _ in range(2)]
    f_fin = [new(), new()]
    f_slices = (e2, m2, m)
    own_half = x == z // 2

    def grads(dl, a, scale, at_z, first, n, t, width):
        cols = pl.ds(mult(t * width, width), width)
        lhs = jnp.concatenate(
            [dl[b, pl.ds(first, n)].reshape(n * 128, 128) for b in range(8)], axis=1
        )
        acc = jnp.dot(lhs, a[:, cols], preferred_element_type=F32)
        per = width // 256
        own = jnp.where(own_half & (t // (4 // per) == at_z % 2), 1.0, 0.0)
        diag = []
        for j in range(per):
            qq = (t % (4 // per)) * per + j
            for c in range(2):
                row = scale[qq, c:c + 1, :] * own
                diag.append(
                    dl[c * 4 + qq, pl.ds(first, n)].reshape(n * 128, 128).astype(F32) * row
                )
        return acc + jnp.concatenate(diag, axis=1), cols

    def grads_here(first, n):
        @pl.loop(0, 4)
        def _(t):
            acc, cols = grads(dlq, adj, sbuf, z, first, n, t, 512)
            for i in range(n):
                dff[first + i, :, cols] = acc[i * 128:(i + 1) * 128]

    def grads_end(s, c):
        @pl.loop(2 * c, 2 * c + 2)
        def _(t):
            acc, cols = grads(dle, adj_e, sbuf_e, e, s, 1, t, 512)
            tot = dff[s, :, cols] + acc
            dff[s, :, cols] = tot
            dfp[s, :, cols] = tot.astype(BF16)

    def mid_pass():
        recv(es, sbuf_e, mids)
        for i, qq, on in ((ez, q, esib), (ezy, q_y, efwd)):
            for c in range(2):
                recv(i[c], e_part(qq, c), mids)
                send(on[c], e_part(qq, c), e_part(qq, c), sib, mids, mids)

    def end_send(j):
        s = f_slices[j]
        send(f_in[j], dlq.at[:, s], dle.at[:, s], mid_dev, ends, mids)

    layer_grads_here(None)

    def grads_own():
        @pl.when(mids)
        def _():
            grads_here(2 * (1 - pair), 2)
            grads_here(2 * pair, 2)

        @pl.when(ends)
        def _():
            grads_here(e, 1)


    def mid_ready():
        for c in range(2):
            recv(esib[c], e_part(q_s, c), mids)
            recv(efwd[c], e_part(q_d, c), mids)

    def cut(c):
        return pl.ds(c * 1024, 1024)

    def mid_send(j):
        s_to = f_slices[j]
        recv(f_in[j], dle.at[:, s_to], mids)
        for c in range(2):
            @pl.when(mids)
            def _(c=c):
                grads_end(s_to, c)
            if j < 2:
                send(f_out[j][c], dfp.at[s_to, :, cut(c)], fin.at[j, :, cut(c)],
                     at(x, y, m2, k), mids, mids)

    def mid_merge(c):
        recv(f_out[0][c], fin.at[0, :, cut(c)], mids)

        @pl.when(mids)
        def _():
            dfp[e, :, cut(c)] = (
                dff[e, :, cut(c)] + fin[0, :, cut(c)].astype(F32)
            ).astype(BF16)
        send(f_fin[c], dfp.at[e, :, cut(c)], fin.at[1, :, cut(c)], end_dev, mids, ends)

    def piece(s, qq, c, h):
        return dw_ref.at[(s * 4 + qq) * 4 + c * 2 + h]

    gz = tuple({(d, h): new() for d in (1, 2, 3) for h in (0, 1)} for _ in range(2))
    gx, gy, gxy, gyx = ({(h, o): new() for h in (0, 1) for o in range(4)} for _ in range(4))
    gs, gsd = ([new() for _ in range(4)] for _ in range(2))

    def z_piece(s, h):
        return piece(s, q, x, h)

    def finish(h):
        for d in (1, 2, 3):
            recv(dw_ids[h][d - 1], dwr.at[(z - d) % 4, pl.ds(h * 512, 512)])
        for t in range(4):
            rr = pl.ds(h * 512 + t * 128, 128)
            tot = dwf[z, rr, :]
            for d in (1, 2, 3):
                tot = tot + dwr[(z + d) % 4, rr, :].astype(F32)
            dw_ref[(z * 4 + q) * 4 + x * 2 + h, :, t * 128:(t + 1) * 128] = tot.T.astype(BF16)
        line_send(gz, z_piece, 1, h)
        spread(h, 0)

    def spread(h, o):
        src = piece(slice_at(o), q, x, h)
        send(gx[h, o], src, src, xn)
        send(gy[h, o], src, src, yn)

    def whole(s, qq):
        return dw_ref.at[pl.ds((s * 4 + qq) * 4, 4)]

    def part(ref, i):
        return ref.at[pl.ds(i * 64, 64)]

    def relay(h, o):
        s = slice_at(o)
        from_x, from_y = piece(s, q, 1 - x, h), piece(s, q_y, x, h)
        recv(gx[h, o], from_x)
        send(gxy[h, o], part(from_x, 0), part(from_x, 0), yn)
        if h == 1:
            send(gs[o], whole(s, q), whole(s, q), sib)
        recv(gy[h, o], from_y)
        send(gyx[h, o], part(from_y, 1), part(from_y, 1), xn)

    def relay_diag(h, o):
        block = piece(slice_at(o), q_y, 1 - x, h)
        recv(gxy[h, o], part(block, 0))
        recv(gyx[h, o], part(block, 1))
        if h == 1:
            send(gsd[o], whole(slice_at(o), q_y), whole(slice_at(o), q_y), sib)

    def last(o):
        recv(gs[o], whole(slice_at(o), q_s))
        recv(gsd[o], whole(slice_at(o), q_d))

    def along(h, d):
        line_recv(gz, z_piece, d, h)
        if d < 3:
            line_send(gz, z_piece, d + 1, h)
        spread(h, d)

    steps = {
        "f": finish, "a": along, "r": relay, "d": relay_diag,
        "E": end_send, "M": mid_send, "G": mid_merge, "R": mid_ready, "H": grads_own, "P": mid_pass,
    }
    for step in (t for group in ORDER for t in group.split()):
        steps[step[0]](*(int(i) for i in step[1:]))
    for d in (1, 2, 3):
        recv(b_ids[2 + d], bsum.at[6 + d])
    db_ref[...] = bsum[6] + bsum[7] + bsum[8] + bsum[9]

    for c in range(2):
        recv(f_out[1][c], fin.at[1, :, cut(c)], mids)
        recv(f_fin[c], fin.at[1, :, cut(c)], ends)

    @pl.loop(0, 16)
    def _(t):
        cols = pl.ds(mult(t * 128, 128), 128)
        tot = dff[z, :, cols] + fin[1, :, cols].astype(F32)
        dfeat_ref[pl.ds(mult(t * 128, 128), 128), :] = tot.T

    for o in range(4):
        last(o)
    assert not pending and count[0] <= N_SEMS, count
    for i, (c, cond) in sent_by.items():
        when(cond, c.wait_send)


def widen_kernel(dw_ref, out_ref, dfeat_ref, db_ref, dw_out, out_out, dfeat_out, db_out, wide, sem):
    copies = [
        pltpu.make_async_copy(src, dst, sem.at[16 + i])
        for i, (src, dst) in enumerate(
            ((out_ref, out_out), (dfeat_ref, dfeat_out), (db_ref, db_out))
        )
    ]
    for c in copies:
        c.start()
    rows = [
        pltpu.make_async_copy(wide.at[i], dw_out.at[pl.ds(i * 128, 128)], sem.at[i])
        for i in range(16)
    ]
    for i in range(16):
        for j in range(4):
            wide[i, :, j * 512:(j + 1) * 512] = dw_ref[4 * i + j].astype(F32)
        rows[i].start()
    for c in copies + rows:
        c.wait()


N_SEMS = 148


def per_device_fused(features, weight, bias, self_scale, adj_tiles, tile_ids, tile_counts, cotangent):
    vmem = pl.BlockSpec(memory_space=pltpu.VMEM)
    smem = pl.BlockSpec(memory_space=pltpu.SMEM)
    hbm = pl.BlockSpec(memory_space=pl.ANY)
    outputs, d_features, gathered, d_bias = pl.pallas_call(
        fused_kernel,
        out_shape=(
            pltpu.VMEM((128, 2048), F32),
            pltpu.VMEM((2048, 128), F32),
            pltpu.VMEM((64, 128, 512), BF16),
            pltpu.VMEM((16, 128), F32),
        ),
        in_specs=[smem, smem, vmem, hbm, hbm, vmem, vmem, vmem],
        out_specs=(vmem, vmem, vmem, vmem),
        scratch_shapes=[
            pltpu.VMEM((1024, 2048), BF16),
            pltpu.VMEM((1024, 2048), BF16),
            pltpu.VMEM((4, 2048, 128), BF16),
            pltpu.VMEM((2048, 2048), BF16),
            pltpu.VMEM((4, 8, 128), F32),
            pltpu.VMEM((4, 8, 128), F32),
            pltpu.VMEM((8, 128, 128), F32),
            pltpu.VMEM((4, 512, 128), BF16),
            pltpu.VMEM((4, 512, 128), BF16),
            pltpu.VMEM((4, 512, 128), F32),
            pltpu.VMEM((4, 1024, 128), BF16),
            pltpu.VMEM((16, 128, 128), BF16),
            pltpu.VMEM((128, 2048), F32),
            pltpu.VMEM((2048, 128), BF16),
            pltpu.VMEM((8, 1024, 128), BF16),
            pltpu.VMEM((4, 4, 128, 128), BF16),
            pltpu.VMEM((8, 4, 128, 128), BF16),
            pltpu.VMEM((4, 1024, 128), F32),
            pltpu.VMEM((4, 1024, 128), BF16),
            pltpu.VMEM((4, 1024, 128), BF16),
            pltpu.VMEM((4, 128, 2048), F32),
            pltpu.VMEM((4, 128, 2048), BF16),
            pltpu.VMEM((8, 4, 128, 128), BF16),
            pltpu.VMEM((2, 128, 2048), BF16),
            pltpu.VMEM((10, 16, 128), F32),
            pltpu.VMEM((16, 128), F32),
            pltpu.SemaphoreType.DMA((N_SEMS,)),
            pltpu.SemaphoreType.DMA((N_SEMS,)),
            pltpu.SemaphoreType.DMA((3,)),
        ],
        compiler_params=pltpu.CompilerParams(
            collective_id=0, has_side_effects=True, vmem_limit_bytes=53 * MIB
        ),
        cost_estimate=pl.CostEstimate(
            flops=7_600_000_000, bytes_accessed=24 * MIB, transcendentals=262144
        ),
    )(
        tile_ids[0, 0], tile_counts[0], adj_tiles[0, 0], features, weight,
        bias.reshape(16, 128), self_scale.reshape(2, 128), cotangent,
    )
    d_weight, outputs, d_features, d_bias = pl.pallas_call(
        widen_kernel,
        out_shape=(
            jax.ShapeDtypeStruct((2048, 2048), F32),
            jax.ShapeDtypeStruct((128, 2048), F32),
            jax.ShapeDtypeStruct((2048, 128), F32),
            jax.ShapeDtypeStruct((16, 128), F32),
        ),
        in_specs=[vmem] * 4,
        out_specs=(hbm, hbm, hbm, hbm),
        scratch_shapes=[pltpu.VMEM((16, 128, 2048), F32), pltpu.SemaphoreType.DMA((19,))],
        compiler_params=pltpu.CompilerParams(vmem_limit_bytes=30 * MIB),
    )(gathered, outputs, d_features, d_bias)
    return outputs, d_features, d_weight, d_bias.reshape(2048)


def solution(mesh):
    fits = dict(mesh.shape) == {"row": 16, "col": 2}

    def run(*arrays):
        fused = fits and arrays[0].shape == (4096, 2048) and arrays[4].shape[2] == 32
        return jax.shard_map(
            per_device_fused if fused else per_device_any,
            mesh=mesh,
            in_specs=(
                P("col", "row"),
                P(),
                P(),
                P("row"),
                P("row", "col", None, None, None),
                P("row", "col", None),
                P("row", "col"),
                P(("row", "col"), None),
            ),
            out_specs=(P(("row", "col"), None), P("col", "row"), P(), P()),
            check_vma=False,
        )(*arrays)

    return run
```

```python
import jax
import jax.numpy as jnp
from jax import lax
from jax.experimental import pallas as pl
from jax.experimental.pallas import tpu as pltpu
from jax.sharding import PartitionSpec as P

MESH = pl.DeviceIdType.MESH
F32 = jnp.float32
BF16 = jnp.bfloat16
MIB = 2**20
ORDER = (
    "f0 W1 a01 r00",
    "L H0 H1 f1",
    "E0 a02 r01 P",
    "R d00 a11 E1",
    "r10 d01 M0 a03",
    "E2 r02 d10 a12",
    "G0 M1 r03 r11",
    "d02 a13 G1 d11",
    "r12 d03 M2 r13",
    "d12 d13",
)
NC = 2
PARTS = ((0, 512), (512, 512))


def dense_block(tiles, ids, count, tile_rows, tile_cols):
    slots = jnp.arange(tiles.shape[0], dtype=jnp.int32)
    live = jnp.where((slots < count)[:, None, None], tiles, jnp.zeros_like(tiles))
    blank = jnp.zeros((tile_rows * tile_cols, 128, 128), tiles.dtype)
    placed = blank.at[ids].add(live, unique_indices=True)
    placed = placed.reshape(tile_rows, tile_cols, 128, 128)
    return placed.transpose(0, 2, 1, 3).reshape(tile_rows * 128, tile_cols * 128)


def per_device_any(features, weight, bias, self_scale, adj_tiles, tile_ids, tile_counts, cotangent):
    row_block = self_scale.shape[0]
    col_block = features.shape[0]
    block = dense_block(
        adj_tiles[0, 0], tile_ids[0, 0], tile_counts[0, 0], row_block // 128, col_block // 128
    )
    start_row = lax.axis_index("row") * row_block
    col_no = lax.axis_index("col")
    inside = col_no == start_row // col_block
    offset = jnp.where(inside, start_row - col_no * col_block, 0)
    self_rows = jnp.where(inside, self_scale, 0.0)[:, None]
    piece = lax.all_gather(features, "row", axis=1, tiled=True)
    terms = jnp.dot(block, piece, preferred_element_type=F32)
    terms = terms + self_rows * lax.dynamic_slice_in_dim(piece, offset, row_block, 0)
    layer_in = lax.psum_scatter(terms, "col", scatter_dimension=0, tiled=True).astype(BF16)
    pre_act = jnp.dot(layer_in, weight, preferred_element_type=F32) + bias.astype(F32)
    sig = jax.nn.sigmoid(pre_act)
    outputs = pre_act * sig
    slope = sig * (1.0 + pre_act * (1.0 - sig))
    d_pre = (cotangent.astype(F32) * slope).astype(BF16)
    d_weight = lax.dot_general(
        layer_in, d_pre, (((0,), (0,)), ((), ())), preferred_element_type=F32
    )
    d_bias = jnp.sum(d_pre.astype(F32), axis=0)
    d_weight, d_bias = lax.psum((d_weight, d_bias), ("row", "col"))
    d_layer = lax.dot_general(
        d_pre, weight, (((1,), (1,)), ((), ())), preferred_element_type=F32
    ).astype(BF16)
    whole = lax.all_gather(d_layer, "col", axis=0, tiled=True)
    spread = lax.dot_general(block, whole, (((0,), (0,)), ((), ())), preferred_element_type=F32)
    own = lax.dynamic_slice_in_dim(spread, offset, row_block, 0) + self_rows * whole
    spread = lax.dynamic_update_slice_in_dim(spread, own, offset, 0)
    d_features = lax.psum_scatter(spread, "row", scatter_dimension=1, tiled=True)
    return outputs, d_features, d_weight, d_bias


def fused_kernel(
    ids_ref, count_ref, tiles_hbm, feat_ref, w_ref, bias_ref, scale_ref, cot_hbm,
    out_ref, dfeat_ref, dw_ref, db_ref,
    tiles_ref, cot_ref, adj, adj_e, hid, wv, sbuf, sbuf_e, scol, xs, xr, keep, lay, xrow, pre, pt, ptg, dls, dlq,
    dwf, dwp, dwr, dff, dfp, dle, fin, bsum, bias32, ssem, rsem, lsem,
):
    r = lax.axis_index("row")
    x = lax.axis_index("col")
    z = r // 4
    y = (r // 2) % 2
    k = r % 2
    q = 2 * y + k
    ends = (z == 0) | (z == 3)
    mids = (z == 1) | (z == 2)

    def at(xx, yy, zz, kk):
        return (zz * 4 + yy * 2 + kk, xx)

    sib = at(x, y, z, 1 - k)
    xn = at(1 - x, y, z, k)
    yn = at(x, 1 - y, z, k)
    dg = at(x, 1 - y, z, 1 - k)
    zr = at(x, y, jnp.minimum(z + 1, 3), k)
    zl = at(x, y, jnp.maximum(z - 1, 0), k)
    q_y = 2 * (1 - y) + k
    q_s = 2 * y + 1 - k
    q_d = 3 - q

    count = [0]
    sent_by = {}
    pending = {}

    def new():
        count[0] += 1
        return count[0] - 1

    def when(cond, fn):
        if cond is None:
            fn()
        else:
            pl.when(cond)(fn)

    def copy(i, src, dst, to):
        return pltpu.make_async_remote_copy(
            src_ref=src, dst_ref=dst, send_sem=ssem.at[i], recv_sem=rsem.at[i],
            device_id=to, device_id_type=MESH,
        )

    def send(i, src, dst, to, cond=None, rcond=None):
        c = copy(i, src, dst, to)
        when(cond, c.start)
        sent_by[i] = (c, cond)
        pending[i] = (dst, rcond)

    def recv(i, dst, cond=None):
        pending.pop(i, None)
        c = copy(i, dst, dst, sib)
        when(cond, c.wait_recv)

    def slice_at(o):
        return [z, z + 1 - 2 * (z % 2), 2 - z // 2, 3 - 3 * (z // 2)][o]

    def mult(v, n):
        return pl.multiple_of(v, n)

    barrier = pltpu.get_barrier_semaphore()
    near = [(sib, None), (xn, None), (yn, None), (zr, z <= 2), (zl, z >= 1)]
    for peer, cond in near:
        when(cond, lambda peer=peer: pl.semaphore_signal(
            barrier, inc=1, device_id=peer, device_id_type=MESH
        ))

    w_copy = pltpu.make_async_copy(w_ref, wv, lsem.at[0])
    h_copy = pltpu.make_async_copy(feat_ref, hid.at[z], lsem.at[1])
    t_copy = pltpu.make_async_copy(tiles_hbm, tiles_ref, lsem.at[2])
    c_copy = pltpu.make_async_copy(cot_hbm, cot_ref, lsem.at[3])
    t_copy.start()
    h_copy.start()
    t_copy.wait()

    for c in range(2):
        @pl.loop(0, 16)
        def _(t, c=c):
            slot = jnp.int32(0)
            for i in range(32):
                slot = jnp.where(ids_ref[i] == c * 16 + t, i, slot)
            live = jnp.where(slot < count_ref[0], 1.0, 0.0)
            tile = tiles_ref[slot].astype(F32) * live
            adj[pl.ds(mult(c * 512 + q * 128, 128), 128), pl.ds(mult(t * 128, 128), 128)] = (
                tile.astype(BF16)
            )
    for i in range(4):
        sbuf[q, 2 * i:2 * i + 2, :] = scale_ref[...]
    bias32[...] = bias_ref[...].astype(F32)
    h_copy.wait()
    w_copy.start()
    c_copy.start()
    pl.semaphore_wait(barrier, jnp.where(ends, 4, 5))

    def h_part(s, c):
        return hid.at[s, pl.ds(c * (2048 // NC), 2048 // NC)]

    right = {(d, c): new() for d in (1, 2, 3) for c in range(NC)}
    left = {(d, c): new() for d in (1, 2, 3) for c in range(NC)}

    def line_send(ids, part, d, c, own_ok=True):
        sr, sl = jnp.maximum(z - (d - 1), 0), jnp.minimum(z + d - 1, 3)
        send(ids[0][d, c], part(sr, c), part(sr, c), zr, (z >= d - 1) & (z <= 2), z >= d)
        send(ids[1][d, c], part(sl, c), part(sl, c), zl, (z <= 4 - d) & (z >= 1), z <= 3 - d)

    def line_recv(ids, part, d, c):
        sr, sl = jnp.maximum(z - d, 0), jnp.minimum(z + d, 3)
        recv(ids[0][d, c], part(sr, c), z >= d)
        recv(ids[1][d, c], part(sl, c), z <= 3 - d)

    hz = (right, left)
    for c in range(NC):
        line_send(hz, h_part, 1, c)

    s_id = [new() for _ in range(3)]
    send(s_id[0], sbuf.at[q], sbuf.at[q], yn)
    send(s_id[1], sbuf.at[q], sbuf.at[q], sib)

    def a_part(qq, c):
        return adj.at[pl.ds(mult(c * 512 + qq * 128, 128), 128)]

    halves = (1 - x, x)
    ay, asib, afwd = ([new(), new()] for _ in range(3))
    for i, c in enumerate(halves):
        send(asib[i], a_part(q, c), a_part(q, c), sib)
    send(ay[0], a_part(q, 1 - x), a_part(q, 1 - x), yn)

    line_recv(hz, h_part, 1, 0)
    line_send(hz, h_part, 2, 0)
    send(ay[1], a_part(q, x), a_part(q, x), yn)

    recv(s_id[0], sbuf.at[q_y])
    send(s_id[2], sbuf.at[q_y], sbuf.at[q_y], sib)
    recv(s_id[1], sbuf.at[q_s])
    recv(s_id[2], sbuf.at[q_d])
    inside = jnp.where(x == z // 2, 1.0, 0.0)
    for b in range(8):
        row = sbuf[b % 4, b // 4:b // 4 + 1, :] * inside
        scol[b] = jnp.broadcast_to(row, (128, 128)).T

    line_recv(hz, h_part, 1, 1)
    line_send(hz, h_part, 2, 1)

    pair = z // 2
    e, m = 3 * pair, 1 + pair
    e2, m2 = 3 - 3 * pair, 2 - pair
    mid_dev, end_dev = at(x, y, m, k), at(x, y, e, k)

    def e_part(qq, c):
        return adj_e.at[pl.ds(mult(c * 512 + qq * 128, 128), 128)]

    ez, ezy, esib, efwd = ([new(), new()] for _ in range(4))
    es = new()
    for c in range(2):
        send(ez[c], a_part(q, c), e_part(q, c), mid_dev, ends, mids)
    send(es, sbuf, sbuf_e, mid_dev, ends, mids)

    x_id = [[new(), new()] for _ in range(4)]
    l_id = [new() for _ in range(4)]
    row_id = [[new() for _ in range(3)] for _ in range(4)]
    w_waited = []

    def aggregate(o, c, u):
        s = slice_at(o)
        first = (1 - y if u == 0 else y) * 256
        rows = pl.ds(mult(first, 256), 256)
        acc = jnp.dot(
            adj[pl.ds(mult(halves[c] * 512 + first, 256), 256), :], hid[s],
            preferred_element_type=F32,
        )
        own = []
        for i in range(2):
            qq = first // 128 + i
            at_node = mult((z % 2) * 1024 + qq * 256 + halves[c] * 128, 128)
            own.append(scol[halves[c] * 4 + qq] * hid[s, pl.ds(at_node, 128), :].astype(F32))
        acc = acc + jnp.concatenate(own, axis=0)
        if c == 0:
            xs[o, rows] = acc.astype(BF16)
            send(x_id[o][u], xs.at[o, rows], xr.at[o, rows], xn)
        else:
            keep[o, rows] = acc

    def combine(o):
        s = slice_at(o)
        sends = list(zip(row_id[o], (q_y, q_d, q_s), (yn, dg, sib)))
        for u in range(2):
            first = (1 - y if u == 0 else y) * 256
            rows = pl.ds(mult(first, 256), 256)
            recv(x_id[o][u], xr.at[o, rows])
            mine = pl.ds(mult(x * 512 + first, 256), 256)
            lay[s, mine, :] = (keep[o, rows] + xr[o, rows].astype(F32)).astype(BF16)
            for i, qq, to in (sends[:2], sends[2:])[u]:
                piece_rows = pl.ds(mult(x * 512 + qq * 128, 128), 128)
                send(i, lay.at[s, piece_rows], xrow.at[s * 4 + q], to)
        xrow[s * 4 + q] = lay[s, pl.ds(mult(x * 512 + q * 128, 128), 128), :]

    def share(o):
        half = lay.at[slice_at(o), pl.ds(mult(x * 512, 512), 512)]
        send(l_id[o], half, half, xn)

    def linear(o):
        s = slice_at(o)
        for i, qq in zip(row_id[o], (q_y, q_d, q_s)):
            recv(i, xrow.at[s * 4 + qq])
        if not w_waited:
            w_copy.wait()
            c_copy.wait()
            w_waited.append(True)
        block = jnp.concatenate([xrow[s * 4 + i] for i in range(4)], axis=1)

        @pl.loop(0, 2)
        def _(t):
            cols = pl.ds(mult(t * 1024, 1024), 1024)
            prod = jnp.dot(
                block, wv[pl.ds(mult(s * 512, 512), 512), cols], preferred_element_type=F32
            )
            if o == 0:
                pre[:, cols] = prod
            else:
                pre[:, cols] += prod

    for i in range(2):
        recv(asib[i], a_part(q_s, halves[i]))
    for o in range(2):
        aggregate(o, 0, 1)
        aggregate(o, 1, 1)
    recv(ay[0], a_part(q_y, 1 - x))
    send(afwd[0], a_part(q_y, 1 - x), a_part(q_y, 1 - x), sib)
    recv(afwd[0], a_part(q_d, 1 - x))
    aggregate(0, 0, 0)
    line_recv(hz, h_part, 2, 0)
    line_send(hz, h_part, 3, 0)
    aggregate(1, 0, 0)
    line_recv(hz, h_part, 2, 1)
    line_send(hz, h_part, 3, 1)
    for c, u in ((0, 0), (0, 1), (1, 1)):
        aggregate(2, c, u)
    recv(ay[1], a_part(q_y, x))
    send(afwd[1], a_part(q_y, x), a_part(q_y, x), sib)
    for c in range(2):
        send(ezy[c], a_part(q_y, c), e_part(q_y, c), mid_dev, ends, mids)
    recv(afwd[1], a_part(q_d, x))
    for o in range(3):
        aggregate(o, 1, 0)
        combine(o)
        if o < 2:
            share(o)
    linear(0)
    linear(1)
    for c in range(NC):
        line_recv(hz, h_part, 3, c)
    for c, u in ((0, 0), (0, 1), (1, 0), (1, 1)):
        aggregate(3, c, u)
    linear(2)
    combine(3)
    share(3)
    share(2)
    linear(3)

    def p_part(c, h):
        return pt.at[pl.ds(mult(c * 1024 + PARTS[h][0], 256), PARTS[h][1])]

    def activate(c, h):
        @pl.loop(PARTS[h][0] // 128, sum(PARTS[h]) // 128)
        def _(i):
            t = c * 8 + i
            cols = pl.ds(mult(t * 128, 128), 128)
            v = pre[:, cols] + bias32[pl.ds(t, 1), :]
            sig = jax.nn.sigmoid(v)
            out_ref[:, cols] = v * sig
            slope = sig * (1.0 + v * (1.0 - sig))
            d32 = (cot_ref[:, cols].astype(F32) * slope).astype(BF16).astype(F32)
            pt[pl.ds(mult(t * 128, 128), 128), :] = d32.T.astype(BF16)
            bsum[0, pl.ds(t, 1), :] = jnp.sum(d32, axis=0, keepdims=True)

    b_own, b_x = x * 4 + q, (1 - x) * 4 + q
    px, py, pyf, ps, psf, pd, pdf = ([new() for _ in PARTS] for _ in range(7))
    b_ids = [new() for _ in range(6)]

    def p_at(b, h):
        return ptg.at[b, pl.ds(*PARTS[h])]

    def p_send(h):
        send(px[h], p_part(1 - x, h), p_at(b_own, h), xn)
        send(py[h], p_part(x, h), p_at(b_own, h), yn)
        send(ps[h], p_part(x, h), p_at(b_own, h), sib)
        first, n = PARTS[h]
        ptg[b_own, first:first + n] = pt[pl.ds(mult(x * 1024 + first, 256), n), :]

    def p_relay_x(h):
        recv(px[h], p_at(b_x, h))
        send(pyf[h], p_at(b_x, h), p_at(b_x, h), yn)
        send(psf[h], p_at(b_x, h), p_at(b_x, h), sib)
        recv(py[h], p_at(x * 4 + q_y, h))
        send(pd[h], p_at(x * 4 + q_y, h), p_at(x * 4 + q_y, h), sib)

    def p_relay_y(h):
        recv(pyf[h], p_at((1 - x) * 4 + q_y, h))
        send(pdf[h], p_at((1 - x) * 4 + q_y, h), p_at((1 - x) * 4 + q_y, h), sib)

    def p_last(h):
        recv(ps[h], p_at(x * 4 + q_s, h))
        recv(psf[h], p_at((1 - x) * 4 + q_s, h))
        recv(pd[h], p_at(x * 4 + q_d, h))
        recv(pdf[h], p_at((1 - x) * 4 + q_d, h))

    activate(1 - x, 0)
    activate(x, 0)
    p_send(0)
    activate(1 - x, 1)
    activate(x, 1)
    if len(PARTS) > 2:
        p_send(1)
        activate(1 - x, 2)
        activate(x, 2)

    @pl.loop(0, 2)
    def _(i):
        acc = jnp.dot(
            wv[pl.ds(mult(i * 1024, 1024), 1024), :], pt[...], preferred_element_type=F32
        ).astype(BF16)
        for j in range(2):
            for qq in range(4):
                first = j * 512 + qq * 128
                dls[qq, i * 2 + j] = acc[first:first + 128]

    dl_to = [
        (1 - x, y, k), (1 - x, y, 1 - k), (x, y, 1 - k),
        (x, 1 - y, k), (x, 1 - y, 1 - k), (1 - x, 1 - y, k), (1 - x, 1 - y, 1 - k),
    ]
    dl_ids = [new() for _ in dl_to]

    def send_layer_grad(which):
        for i in which:
            xx, yy, kk = dl_to[i]
            send(dl_ids[i], dls.at[2 * yy + kk], dlq.at[b_own], at(xx, yy, z, kk))

    p_send(len(PARTS) - 1)
    send(b_ids[0], bsum.at[0], bsum.at[1], xn)
    dlq[b_own] = dls[q]
    p_relay_x(0)
    send_layer_grad((0, 1, 2))
    p_relay_x(1)
    p_relay_y(0)
    recv(b_ids[0], bsum.at[1])
    bsum[2] = bsum[0] + bsum[1]
    send(b_ids[1], bsum.at[2], bsum.at[3], yn)
    for o in range(4):
        recv(l_id[o], lay.at[slice_at(o), pl.ds(mult((1 - x) * 512, 512), 512)])
    p_last(0)

    dw_ids = [[new() for _ in range(5)] for _ in PARTS]

    def weight_grad(h):
        rows = pl.ds(*PARTS[h])
        lhs = jnp.concatenate([ptg[b, rows, :] for b in range(8)], axis=1)
        rhs = jnp.concatenate([lay[s] for s in range(4)], axis=1)
        acc = jnp.dot(lhs, rhs, preferred_element_type=F32)
        for s in range(4):
            dwf[s, rows, :] = acc[:, s * 128:(s + 1) * 128]
            dwp[s, rows, :] = acc[:, s * 128:(s + 1) * 128].astype(BF16)

    def weight_send(h):
        rows = pl.ds(*PARTS[h])
        for i, s_to in enumerate((m2, e2)):
            send(dw_ids[h][i], dwp.at[s_to, rows], dwr.at[i, rows], mid_dev, ends, mids)
        beside = at(x, y, m + e - z, k)
        send(dw_ids[h][2], dwp.at[m + e - z, rows], dwr.at[2, rows], beside)

    def weight_pass(h):
        rows = pl.ds(*PARTS[h])
        for i, s_to in enumerate((m2, e2)):
            recv(dw_ids[h][i], dwr.at[i, rows], mids)

            @pl.when(mids)
            def _(i=i, s_to=s_to):
                dwp[s_to, rows, :] = (
                    dwf[s_to, rows, :] + dwr[i, rows, :].astype(F32)
                ).astype(BF16)
            send(dw_ids[h][3 + i], dwp.at[s_to, rows], dwr.at[3, rows],
                 at(x, y, s_to, k), mids, (mids, ends)[i])

    weight_grad(0)
    weight_send(0)
    if len(PARTS) > 2:
        p_relay_x(2)
    p_relay_y(1)
    send_layer_grad((3, 4, 5, 6))
    recv(b_ids[1], bsum.at[3])
    bsum[4] = bsum[2] + bsum[3]
    send(b_ids[2], bsum.at[4], bsum.at[5], sib)
    p_last(1)
    weight_grad(1)
    weight_send(1)
    weight_pass(0)
    if len(PARTS) > 2:
        p_relay_y(2)
        p_last(2)
        weight_grad(2)
        weight_send(2)
        weight_pass(1)
    recv(b_ids[2], bsum.at[5])
    bsum[6] = bsum[4] + bsum[5]
    for d in (1, 2, 3):
        send(b_ids[2 + d], bsum.at[6], bsum.at[6 + d], at(x, y, (z + d) % 4, k))

    def layer_grads_here():
        for i, (xx, yy, kk) in zip(dl_ids, dl_to):
            recv(i, dlq.at[xx * 4 + 2 * yy + kk])

    f_in = [new() for _ in range(3)]
    f_out = [[new(), new()] for _ in range(2)]
    f_fin = [new(), new()]
    f_slices = (e2, m2, m)
    own_half = x == z // 2

    def grads(dl, a, scale, at_z, first, n, t, width):
        cols = pl.ds(mult(t * width, width), width)
        lhs = jnp.concatenate(
            [dl[b, pl.ds(first, n)].reshape(n * 128, 128) for b in range(8)], axis=1
        )
        acc = jnp.dot(lhs, a[:, cols], preferred_element_type=F32)
        per = width // 256
        own = jnp.where(own_half & (t // (4 // per) == at_z % 2), 1.0, 0.0)
        diag = []
        for j in range(per):
            qq = (t % (4 // per)) * per + j
            for c in range(2):
                row = scale[qq, c:c + 1, :] * own
                diag.append(
                    dl[c * 4 + qq, pl.ds(first, n)].reshape(n * 128, 128).astype(F32) * row
                )
        return acc + jnp.concatenate(diag, axis=1), cols

    def grads_here(first, n):
        @pl.loop(0, 4)
        def _(t):
            acc, cols = grads(dlq, adj, sbuf, z, first, n, t, 512)
            for i in range(n):
                dff[first + i, :, cols] = acc[i * 128:(i + 1) * 128]

    def grads_end(s, c):
        @pl.loop(2 * c, 2 * c + 2)
        def _(t):
            acc, cols = grads(dle, adj_e, sbuf_e, e, s, 1, t, 512)
            tot = dff[s, :, cols] + acc
            dff[s, :, cols] = tot
            dfp[s, :, cols] = tot.astype(BF16)

    def mid_pass():
        recv(es, sbuf_e, mids)
        for i, qq, on in ((ez, q, esib), (ezy, q_y, efwd)):
            for c in range(2):
                recv(i[c], e_part(qq, c), mids)
                send(on[c], e_part(qq, c), e_part(qq, c), sib, mids, mids)

    def end_send(j):
        s = f_slices[j]
        send(f_in[j], dlq.at[:, s], dle.at[:, s], mid_dev, ends, mids)

    def grads_own(i):
        @pl.when(mids)
        def _():
            grads_here(2 * (pair if i else 1 - pair), 2)
        if i == 0:
            @pl.when(ends)
            def _():
                grads_here(e, 1)


    def mid_ready():
        for c in range(2):
            recv(esib[c], e_part(q_s, c), mids)
            recv(efwd[c], e_part(q_d, c), mids)

    def cut(c):
        return pl.ds(c * 1024, 1024)

    def mid_send(j):
        s_to = f_slices[j]
        recv(f_in[j], dle.at[:, s_to], mids)
        for c in range(2):
            @pl.when(mids)
            def _(c=c):
                grads_end(s_to, c)
            if j < 2:
                send(f_out[j][c], dfp.at[s_to, :, cut(c)], fin.at[j, :, cut(c)],
                     at(x, y, m2, k), mids, mids)

    def mid_merge(c):
        recv(f_out[0][c], fin.at[0, :, cut(c)], mids)

        @pl.when(mids)
        def _():
            dfp[e, :, cut(c)] = (
                dff[e, :, cut(c)] + fin[0, :, cut(c)].astype(F32)
            ).astype(BF16)
        send(f_fin[c], dfp.at[e, :, cut(c)], fin.at[1, :, cut(c)], end_dev, mids, ends)

    def piece(s, qq, c, h):
        first, n = PARTS[h]
        return dw_ref.at[pl.ds((s * 4 + qq) * 8 + c * 4 + first // 256, n // 256)]

    gz = tuple({(d, h): new() for d in (1, 2, 3) for h in range(len(PARTS))} for _ in range(2))
    gx, gy, gxy, gyx = (
        {(h, o): new() for h in range(len(PARTS)) for o in range(4)} for _ in range(4)
    )
    gs, gsd = ([new() for _ in range(4)] for _ in range(2))

    def z_piece(s, h):
        return piece(s, q, x, h)

    def finish(h):
        rows = pl.ds(*PARTS[h])
        recv(dw_ids[h][2], dwr.at[2, rows])
        recv(dw_ids[h][3], dwr.at[3, rows], mids)
        recv(dw_ids[h][4], dwr.at[3, rows], ends)
        for t in range(PARTS[h][0] // 128, sum(PARTS[h]) // 128):
            rr = pl.ds(t * 128, 128)
            tot = dwf[z, rr, :] + dwr[2, rr, :].astype(F32) + dwr[3, rr, :].astype(F32)
            half = t % 2 * 128
            dw_ref[(z * 4 + q) * 8 + x * 4 + t // 2, :, half:half + 128] = tot.T.astype(BF16)
        line_send(gz, z_piece, 1, h)
        spread(h, 0)

    def spread(h, o):
        src = piece(slice_at(o), q, x, h)
        send(gx[h, o], src, src, xn)
        send(gy[h, o], src, src, yn)

    def whole(s, qq):
        return dw_ref.at[pl.ds((s * 4 + qq) * 8, 8)]

    def part(ref, i):
        return ref.at[:, pl.ds(i * 64, 64)]

    def relay(h, o):
        s = slice_at(o)
        from_x, from_y = piece(s, q, 1 - x, h), piece(s, q_y, x, h)
        recv(gx[h, o], from_x)
        send(gxy[h, o], part(from_x, 0), part(from_x, 0), yn)
        if h == len(PARTS) - 1:
            send(gs[o], whole(s, q), whole(s, q), sib)
        recv(gy[h, o], from_y)
        send(gyx[h, o], part(from_y, 1), part(from_y, 1), xn)

    def relay_diag(h, o):
        block = piece(slice_at(o), q_y, 1 - x, h)
        recv(gxy[h, o], part(block, 0))
        recv(gyx[h, o], part(block, 1))
        if h == len(PARTS) - 1:
            send(gsd[o], whole(slice_at(o), q_y), whole(slice_at(o), q_y), sib)

    def last(o):
        recv(gs[o], whole(slice_at(o), q_s))
        recv(gsd[o], whole(slice_at(o), q_d))

    def along(h, d):
        line_recv(gz, z_piece, d, h)
        if d < 3:
            line_send(gz, z_piece, d + 1, h)
        spread(h, d)

    steps = {
        "f": finish, "a": along, "r": relay, "d": relay_diag,
        "E": end_send, "M": mid_send, "G": mid_merge, "R": mid_ready, "H": grads_own, "P": mid_pass,
        "L": layer_grads_here, "W": weight_pass,
    }
    for step in (t for group in ORDER for t in group.split()):
        steps[step[0]](*(int(i) for i in step[1:]))
    for d in (1, 2, 3):
        recv(b_ids[2 + d], bsum.at[6 + d])
    db_ref[...] = bsum[6] + bsum[7] + bsum[8] + bsum[9]

    for c in range(2):
        recv(f_out[1][c], fin.at[1, :, cut(c)], mids)
        recv(f_fin[c], fin.at[1, :, cut(c)], ends)

    @pl.loop(0, 16)
    def _(t):
        cols = pl.ds(mult(t * 128, 128), 128)
        tot = dff[z, :, cols] + fin[1, :, cols].astype(F32)
        dfeat_ref[pl.ds(mult(t * 128, 128), 128), :] = tot.T

    for o in range(4):
        last(o)
    assert not pending and count[0] <= N_SEMS, count
    for i, (c, cond) in sent_by.items():
        when(cond, c.wait_send)


def widen_kernel(dw_ref, out_ref, dfeat_ref, db_ref, dw_out, out_out, dfeat_out, db_out, wide, sem):
    copies = [
        pltpu.make_async_copy(src, dst, sem.at[16 + i])
        for i, (src, dst) in enumerate(
            ((out_ref, out_out), (dfeat_ref, dfeat_out), (db_ref, db_out))
        )
    ]
    for c in copies:
        c.start()
    rows = [
        pltpu.make_async_copy(wide.at[i], dw_out.at[pl.ds(i * 128, 128)], sem.at[i])
        for i in range(16)
    ]
    for i in range(16):
        for j in range(8):
            wide[i, :, j * 256:(j + 1) * 256] = dw_ref[8 * i + j].astype(F32)
        rows[i].start()
    for c in copies + rows:
        c.wait()


N_SEMS = 152


def per_device_fused(features, weight, bias, self_scale, adj_tiles, tile_ids, tile_counts, cotangent):
    vmem = pl.BlockSpec(memory_space=pltpu.VMEM)
    smem = pl.BlockSpec(memory_space=pltpu.SMEM)
    hbm = pl.BlockSpec(memory_space=pl.ANY)
    outputs, d_features, gathered, d_bias = pl.pallas_call(
        fused_kernel,
        out_shape=(
            pltpu.VMEM((128, 2048), F32),
            pltpu.VMEM((2048, 128), F32),
            pltpu.VMEM((128, 128, 256), BF16),
            pltpu.VMEM((16, 128), F32),
        ),
        in_specs=[smem, smem, hbm, hbm, hbm, vmem, vmem, hbm],
        out_specs=(vmem, vmem, vmem, vmem),
        scratch_shapes=[
            pltpu.VMEM((32, 128, 128), BF16),
            pltpu.VMEM((128, 2048), BF16),
            pltpu.VMEM((1024, 2048), BF16),
            pltpu.VMEM((1024, 2048), BF16),
            pltpu.VMEM((4, 2048, 128), BF16),
            pltpu.VMEM((2048, 2048), BF16),
            pltpu.VMEM((4, 8, 128), F32),
            pltpu.VMEM((4, 8, 128), F32),
            pltpu.VMEM((8, 128, 128), F32),
            pltpu.VMEM((4, 512, 128), BF16),
            pltpu.VMEM((4, 512, 128), BF16),
            pltpu.VMEM((4, 512, 128), F32),
            pltpu.VMEM((4, 1024, 128), BF16),
            pltpu.VMEM((16, 128, 128), BF16),
            pltpu.VMEM((128, 2048), F32),
            pltpu.VMEM((2048, 128), BF16),
            pltpu.VMEM((8, 1024, 128), BF16),
            pltpu.VMEM((4, 4, 128, 128), BF16),
            pltpu.VMEM((8, 4, 128, 128), BF16),
            pltpu.VMEM((4, 1024, 128), F32),
            pltpu.VMEM((4, 1024, 128), BF16),
            pltpu.VMEM((4, 1024, 128), BF16),
            pltpu.VMEM((4, 128, 2048), F32),
            pltpu.VMEM((4, 128, 2048), BF16),
            pltpu.VMEM((8, 4, 128, 128), BF16),
            pltpu.VMEM((2, 128, 2048), BF16),
            pltpu.VMEM((10, 16, 128), F32),
            pltpu.VMEM((16, 128), F32),
            pltpu.SemaphoreType.DMA((N_SEMS,)),
            pltpu.SemaphoreType.DMA((N_SEMS,)),
            pltpu.SemaphoreType.DMA((4,)),
        ],
        compiler_params=pltpu.CompilerParams(
            collective_id=0, has_side_effects=True, vmem_limit_bytes=53 * MIB
        ),
        cost_estimate=pl.CostEstimate(
            flops=7_600_000_000, bytes_accessed=24 * MIB, transcendentals=262144
        ),
    )(
        tile_ids[0, 0], tile_counts[0], adj_tiles[0, 0], features, weight,
        bias.reshape(16, 128), self_scale.reshape(2, 128), cotangent,
    )
    d_weight, outputs, d_features, d_bias = pl.pallas_call(
        widen_kernel,
        out_shape=(
            jax.ShapeDtypeStruct((2048, 2048), F32),
            jax.ShapeDtypeStruct((128, 2048), F32),
            jax.ShapeDtypeStruct((2048, 128), F32),
            jax.ShapeDtypeStruct((16, 128), F32),
        ),
        in_specs=[vmem] * 4,
        out_specs=(hbm, hbm, hbm, hbm),
        scratch_shapes=[pltpu.VMEM((16, 128, 2048), F32), pltpu.SemaphoreType.DMA((19,))],
        compiler_params=pltpu.CompilerParams(vmem_limit_bytes=30 * MIB),
    )(gathered, outputs, d_features, d_bias)
    return outputs, d_features, d_weight, d_bias.reshape(2048)


def solution(mesh):
    fits = dict(mesh.shape) == {"row": 16, "col": 2}

    def run(*arrays):
        fused = fits and arrays[0].shape == (4096, 2048) and arrays[4].shape[2] == 32
        return jax.shard_map(
            per_device_fused if fused else per_device_any,
            mesh=mesh,
            in_specs=(
                P("col", "row"),
                P(),
                P(),
                P("row"),
                P("row", "col", None, None, None),
                P("row", "col", None),
                P("row", "col"),
                P(("row", "col"), None),
            ),
            out_specs=(P(("row", "col"), None), P("col", "row"), P(), P()),
            check_vma=False,
        )(*arrays)

    return run
```

```python
import jax
import jax.numpy as jnp
from jax import lax
from jax.experimental import pallas as pl
from jax.experimental.pallas import tpu as pltpu
from jax.sharding import PartitionSpec as P

MESH = pl.DeviceIdType.MESH
F32 = jnp.float32
BF16 = jnp.bfloat16
MIB = 2**20
ORDER = (
    "f0 W1 a01 r00",
    "L H0 r01 f1",
    "a02 P H1 E0",
    "R E1 d00 a11",
    "r10 d01 M0 d10",
    "a03 E2 r02 a12",
    "G0 M1 r03 r11",
    "d02 a13 G1 d03",
    "d11 r12 M2 r13",
    "d13 d12",
)
NC = 2
PARTS = ((0, 512), (512, 512))


def dense_block(tiles, ids, count, tile_rows, tile_cols):
    slots = jnp.arange(tiles.shape[0], dtype=jnp.int32)
    live = jnp.where((slots < count)[:, None, None], tiles, jnp.zeros_like(tiles))
    blank = jnp.zeros((tile_rows * tile_cols, 128, 128), tiles.dtype)
    placed = blank.at[ids].add(live, unique_indices=True)
    placed = placed.reshape(tile_rows, tile_cols, 128, 128)
    return placed.transpose(0, 2, 1, 3).reshape(tile_rows * 128, tile_cols * 128)


def per_device_any(features, weight, bias, self_scale, adj_tiles, tile_ids, tile_counts, cotangent):
    row_block = self_scale.shape[0]
    col_block = features.shape[0]
    block = dense_block(
        adj_tiles[0, 0], tile_ids[0, 0], tile_counts[0, 0], row_block // 128, col_block // 128
    )
    start_row = lax.axis_index("row") * row_block
    col_no = lax.axis_index("col")
    inside = col_no == start_row // col_block
    offset = jnp.where(inside, start_row - col_no * col_block, 0)
    self_rows = jnp.where(inside, self_scale, 0.0)[:, None]
    piece = lax.all_gather(features, "row", axis=1, tiled=True)
    terms = jnp.dot(block, piece, preferred_element_type=F32)
    terms = terms + self_rows * lax.dynamic_slice_in_dim(piece, offset, row_block, 0)
    layer_in = lax.psum_scatter(terms, "col", scatter_dimension=0, tiled=True).astype(BF16)
    pre_act = jnp.dot(layer_in, weight, preferred_element_type=F32) + bias.astype(F32)
    sig = jax.nn.sigmoid(pre_act)
    outputs = pre_act * sig
    slope = sig * (1.0 + pre_act * (1.0 - sig))
    d_pre = (cotangent.astype(F32) * slope).astype(BF16)
    d_weight = lax.dot_general(
        layer_in, d_pre, (((0,), (0,)), ((), ())), preferred_element_type=F32
    )
    d_bias = jnp.sum(d_pre.astype(F32), axis=0)
    d_weight, d_bias = lax.psum((d_weight, d_bias), ("row", "col"))
    d_layer = lax.dot_general(
        d_pre, weight, (((1,), (1,)), ((), ())), preferred_element_type=F32
    ).astype(BF16)
    whole = lax.all_gather(d_layer, "col", axis=0, tiled=True)
    spread = lax.dot_general(block, whole, (((0,), (0,)), ((), ())), preferred_element_type=F32)
    own = lax.dynamic_slice_in_dim(spread, offset, row_block, 0) + self_rows * whole
    spread = lax.dynamic_update_slice_in_dim(spread, own, offset, 0)
    d_features = lax.psum_scatter(spread, "row", scatter_dimension=1, tiled=True)
    return outputs, d_features, d_weight, d_bias


def fused_kernel(
    ids_ref, count_ref, tiles_hbm, feat_ref, w_ref, bias_ref, scale_ref, cot_hbm,
    out_ref, dfeat_ref, dw_ref, db_ref,
    tiles_ref, cot_ref, adj, adj_e, hid, wv, sbuf, sbuf_e, scol, xs, xr, keep, lay, xrow, pre, pt, ptg, dls, dlq,
    dwf, dwp, dwr, dff, dfp, dle, fin, bsum, bias32, ssem, rsem, lsem,
):
    r = lax.axis_index("row")
    x = lax.axis_index("col")
    z = r // 4
    y = (r // 2) % 2
    k = r % 2
    q = 2 * y + k
    ends = (z == 0) | (z == 3)
    mids = (z == 1) | (z == 2)

    def at(xx, yy, zz, kk):
        return (zz * 4 + yy * 2 + kk, xx)

    sib = at(x, y, z, 1 - k)
    xn = at(1 - x, y, z, k)
    yn = at(x, 1 - y, z, k)
    dg = at(x, 1 - y, z, 1 - k)
    zr = at(x, y, jnp.minimum(z + 1, 3), k)
    zl = at(x, y, jnp.maximum(z - 1, 0), k)
    q_y = 2 * (1 - y) + k
    q_s = 2 * y + 1 - k
    q_d = 3 - q

    count = [0]
    sent_by = {}
    pending = {}

    def new():
        count[0] += 1
        return count[0] - 1

    def when(cond, fn):
        if cond is None:
            fn()
        else:
            pl.when(cond)(fn)

    def copy(i, src, dst, to):
        return pltpu.make_async_remote_copy(
            src_ref=src, dst_ref=dst, send_sem=ssem.at[i], recv_sem=rsem.at[i],
            device_id=to, device_id_type=MESH,
        )

    def send(i, src, dst, to, cond=None, rcond=None):
        c = copy(i, src, dst, to)
        when(cond, c.start)
        sent_by[i] = (c, cond)
        pending[i] = (dst, rcond)

    def recv(i, dst, cond=None):
        pending.pop(i, None)
        c = copy(i, dst, dst, sib)
        when(cond, c.wait_recv)

    def slice_at(o):
        return [z, z + 1 - 2 * (z % 2), 2 - z // 2, 3 - 3 * (z // 2)][o]

    def mult(v, n):
        return pl.multiple_of(v, n)

    barrier = pltpu.get_barrier_semaphore()
    near = [(sib, None), (xn, None), (yn, None), (zr, z <= 2), (zl, z >= 1)]
    for peer, cond in near:
        when(cond, lambda peer=peer: pl.semaphore_signal(
            barrier, inc=1, device_id=peer, device_id_type=MESH
        ))

    w_copy = pltpu.make_async_copy(w_ref, wv, lsem.at[0])
    h_copy = pltpu.make_async_copy(feat_ref, hid.at[z], lsem.at[1])
    t_copy = pltpu.make_async_copy(tiles_hbm, tiles_ref, lsem.at[2])
    c_copy = pltpu.make_async_copy(cot_hbm, cot_ref, lsem.at[3])
    t_copy.start()
    h_copy.start()
    t_copy.wait()

    for c in range(2):
        @pl.loop(0, 16)
        def _(t, c=c):
            slot = jnp.int32(0)
            for i in range(32):
                slot = jnp.where(ids_ref[i] == c * 16 + t, i, slot)
            live = jnp.where(slot < count_ref[0], 1.0, 0.0)
            tile = tiles_ref[slot].astype(F32) * live
            adj[pl.ds(mult(c * 512 + q * 128, 128), 128), pl.ds(mult(t * 128, 128), 128)] = (
                tile.astype(BF16)
            )
    for i in range(4):
        sbuf[q, 2 * i:2 * i + 2, :] = scale_ref[...]
    bias32[...] = bias_ref[...].astype(F32)
    h_copy.wait()
    w_copy.start()
    c_copy.start()
    pl.semaphore_wait(barrier, jnp.where(ends, 4, 5))

    def h_part(s, c):
        return hid.at[s, pl.ds(c * (2048 // NC), 2048 // NC)]

    right = {(d, c): new() for d in (1, 2, 3) for c in range(NC)}
    left = {(d, c): new() for d in (1, 2, 3) for c in range(NC)}

    def line_send(ids, part, d, c, own_ok=True):
        sr, sl = jnp.maximum(z - (d - 1), 0), jnp.minimum(z + d - 1, 3)
        send(ids[0][d, c], part(sr, c), part(sr, c), zr, (z >= d - 1) & (z <= 2), z >= d)
        send(ids[1][d, c], part(sl, c), part(sl, c), zl, (z <= 4 - d) & (z >= 1), z <= 3 - d)

    def line_recv(ids, part, d, c):
        sr, sl = jnp.maximum(z - d, 0), jnp.minimum(z + d, 3)
        recv(ids[0][d, c], part(sr, c), z >= d)
        recv(ids[1][d, c], part(sl, c), z <= 3 - d)

    hz = (right, left)
    for c in range(NC):
        line_send(hz, h_part, 1, c)

    s_id = [new() for _ in range(3)]
    send(s_id[0], sbuf.at[q], sbuf.at[q], yn)
    send(s_id[1], sbuf.at[q], sbuf.at[q], sib)

    def a_part(qq, c):
        return adj.at[pl.ds(mult(c * 512 + qq * 128, 128), 128)]

    halves = (1 - x, x)
    ay, asib, afwd = ([new(), new()] for _ in range(3))
    for i, c in enumerate(halves):
        send(asib[i], a_part(q, c), a_part(q, c), sib)
    send(ay[0], a_part(q, 1 - x), a_part(q, 1 - x), yn)

    line_recv(hz, h_part, 1, 0)
    line_send(hz, h_part, 2, 0)
    send(ay[1], a_part(q, x), a_part(q, x), yn)

    recv(s_id[0], sbuf.at[q_y])
    send(s_id[2], sbuf.at[q_y], sbuf.at[q_y], sib)
    recv(s_id[1], sbuf.at[q_s])
    recv(s_id[2], sbuf.at[q_d])
    inside = jnp.where(x == z // 2, 1.0, 0.0)
    for b in range(8):
        row = sbuf[b % 4, b // 4:b // 4 + 1, :] * inside
        scol[b] = jnp.broadcast_to(row, (128, 128)).T

    line_recv(hz, h_part, 1, 1)
    line_send(hz, h_part, 2, 1)

    pair = z // 2
    e, m = 3 * pair, 1 + pair
    e2, m2 = 3 - 3 * pair, 2 - pair
    mid_dev, end_dev = at(x, y, m, k), at(x, y, e, k)

    def e_part(qq, c):
        return adj_e.at[pl.ds(mult(c * 512 + qq * 128, 128), 128)]

    ez, ezy, esib, efwd = ([new(), new()] for _ in range(4))
    es = new()
    for c in range(2):
        send(ez[c], a_part(q, c), e_part(q, c), mid_dev, ends, mids)
    send(es, sbuf, sbuf_e, mid_dev, ends, mids)

    x_id = [[new(), new()] for _ in range(4)]
    l_id = [new() for _ in range(4)]
    row_id = [[new() for _ in range(3)] for _ in range(4)]
    w_waited = []

    def aggregate(o, c, u):
        s = slice_at(o)
        first = (1 - y if u == 0 else y) * 256
        rows = pl.ds(mult(first, 256), 256)
        acc = jnp.dot(
            adj[pl.ds(mult(halves[c] * 512 + first, 256), 256), :], hid[s],
            preferred_element_type=F32,
        )
        own = []
        for i in range(2):
            qq = first // 128 + i
            at_node = mult((z % 2) * 1024 + qq * 256 + halves[c] * 128, 128)
            own.append(scol[halves[c] * 4 + qq] * hid[s, pl.ds(at_node, 128), :].astype(F32))
        acc = acc + jnp.concatenate(own, axis=0)
        if c == 0:
            xs[o, rows] = acc.astype(BF16)
            send(x_id[o][u], xs.at[o, rows], xr.at[o, rows], xn)
        else:
            keep[o, rows] = acc

    def combine(o):
        s = slice_at(o)
        sends = list(zip(row_id[o], (q_y, q_d, q_s), (yn, dg, sib)))
        for u in range(2):
            first = (1 - y if u == 0 else y) * 256
            rows = pl.ds(mult(first, 256), 256)
            recv(x_id[o][u], xr.at[o, rows])
            mine = pl.ds(mult(x * 512 + first, 256), 256)
            lay[s, mine, :] = (keep[o, rows] + xr[o, rows].astype(F32)).astype(BF16)
            for i, qq, to in (sends[:2], sends[2:])[u]:
                piece_rows = pl.ds(mult(x * 512 + qq * 128, 128), 128)
                send(i, lay.at[s, piece_rows], xrow.at[s * 4 + q], to)
        xrow[s * 4 + q] = lay[s, pl.ds(mult(x * 512 + q * 128, 128), 128), :]

    def share(o):
        half = lay.at[slice_at(o), pl.ds(mult(x * 512, 512), 512)]
        send(l_id[o], half, half, xn)

    def linear(o):
        s = slice_at(o)
        for i, qq in zip(row_id[o], (q_y, q_d, q_s)):
            recv(i, xrow.at[s * 4 + qq])
        if not w_waited:
            w_copy.wait()
            c_copy.wait()
            w_waited.append(True)
        block = jnp.concatenate([xrow[s * 4 + i] for i in range(4)], axis=1)

        @pl.loop(0, 2)
        def _(t):
            cols = pl.ds(mult(t * 1024, 1024), 1024)
            prod = jnp.dot(
                block, wv[pl.ds(mult(s * 512, 512), 512), cols], preferred_element_type=F32
            )
            if o == 0:
                pre[:, cols] = prod
            else:
                pre[:, cols] += prod

    for i in range(2):
        recv(asib[i], a_part(q_s, halves[i]))
    for o in range(2):
        aggregate(o, 0, 1)
        aggregate(o, 1, 1)
    recv(ay[0], a_part(q_y, 1 - x))
    send(afwd[0], a_part(q_y, 1 - x), a_part(q_y, 1 - x), sib)
    recv(afwd[0], a_part(q_d, 1 - x))
    aggregate(0, 0, 0)
    line_recv(hz, h_part, 2, 0)
    line_send(hz, h_part, 3, 0)
    aggregate(1, 0, 0)
    line_recv(hz, h_part, 2, 1)
    line_send(hz, h_part, 3, 1)
    for c, u in ((0, 0), (0, 1), (1, 1)):
        aggregate(2, c, u)
    recv(ay[1], a_part(q_y, x))
    send(afwd[1], a_part(q_y, x), a_part(q_y, x), sib)
    for c in range(2):
        send(ezy[c], a_part(q_y, c), e_part(q_y, c), mid_dev, ends, mids)
    recv(afwd[1], a_part(q_d, x))
    for o in range(3):
        aggregate(o, 1, 0)
        combine(o)
        if o < 2:
            share(o)
    linear(0)
    linear(1)
    for c in range(NC):
        line_recv(hz, h_part, 3, c)
    for c, u in ((0, 0), (0, 1), (1, 0), (1, 1)):
        aggregate(3, c, u)
    linear(2)
    combine(3)
    share(3)
    share(2)
    linear(3)

    def p_part(c, h):
        return pt.at[pl.ds(mult(c * 1024 + PARTS[h][0], 256), PARTS[h][1])]

    def activate(c, h):
        @pl.loop(PARTS[h][0] // 128, sum(PARTS[h]) // 128)
        def _(i):
            t = c * 8 + i
            cols = pl.ds(mult(t * 128, 128), 128)
            v = pre[:, cols] + bias32[pl.ds(t, 1), :]
            sig = jax.nn.sigmoid(v)
            out_ref[:, cols] = v * sig
            slope = sig * (1.0 + v * (1.0 - sig))
            d32 = (cot_ref[:, cols].astype(F32) * slope).astype(BF16).astype(F32)
            pt[pl.ds(mult(t * 128, 128), 128), :] = d32.T.astype(BF16)
            bsum[0, pl.ds(t, 1), :] = jnp.sum(d32, axis=0, keepdims=True)

    b_own, b_x = x * 4 + q, (1 - x) * 4 + q
    px, py, pyf, ps, psf, pd, pdf = ([new() for _ in PARTS] for _ in range(7))
    b_ids = [new() for _ in range(6)]

    def p_at(b, h):
        return ptg.at[b, pl.ds(*PARTS[h])]

    def p_send(h):
        send(px[h], p_part(1 - x, h), p_at(b_own, h), xn)
        send(py[h], p_part(x, h), p_at(b_own, h), yn)
        send(ps[h], p_part(x, h), p_at(b_own, h), sib)
        first, n = PARTS[h]
        ptg[b_own, first:first + n] = pt[pl.ds(mult(x * 1024 + first, 256), n), :]

    def p_relay_x(h):
        recv(px[h], p_at(b_x, h))
        send(pyf[h], p_at(b_x, h), p_at(b_x, h), yn)
        send(psf[h], p_at(b_x, h), p_at(b_x, h), sib)
        recv(py[h], p_at(x * 4 + q_y, h))
        send(pd[h], p_at(x * 4 + q_y, h), p_at(x * 4 + q_y, h), sib)

    def p_relay_y(h):
        recv(pyf[h], p_at((1 - x) * 4 + q_y, h))
        send(pdf[h], p_at((1 - x) * 4 + q_y, h), p_at((1 - x) * 4 + q_y, h), sib)

    def p_last(h):
        recv(ps[h], p_at(x * 4 + q_s, h))
        recv(psf[h], p_at((1 - x) * 4 + q_s, h))
        recv(pd[h], p_at(x * 4 + q_d, h))
        recv(pdf[h], p_at((1 - x) * 4 + q_d, h))

    activate(1 - x, 0)
    activate(x, 0)
    p_send(0)
    activate(1 - x, 1)
    activate(x, 1)
    if len(PARTS) > 2:
        p_send(1)
        activate(1 - x, 2)
        activate(x, 2)

    @pl.loop(0, 2)
    def _(i):
        acc = jnp.dot(
            wv[pl.ds(mult(i * 1024, 1024), 1024), :], pt[...], preferred_element_type=F32
        ).astype(BF16)
        for j in range(2):
            for qq in range(4):
                first = j * 512 + qq * 128
                dls[qq, i * 2 + j] = acc[first:first + 128]

    dl_to = [
        (1 - x, y, k), (1 - x, y, 1 - k), (x, y, 1 - k),
        (x, 1 - y, k), (x, 1 - y, 1 - k), (1 - x, 1 - y, k), (1 - x, 1 - y, 1 - k),
    ]
    dl_ids = [new() for _ in dl_to]

    def send_layer_grad(which):
        for i in which:
            xx, yy, kk = dl_to[i]
            send(dl_ids[i], dls.at[2 * yy + kk], dlq.at[b_own], at(xx, yy, z, kk))

    p_send(len(PARTS) - 1)
    send(b_ids[0], bsum.at[0], bsum.at[1], xn)
    dlq[b_own] = dls[q]
    p_relay_x(0)
    send_layer_grad((0, 1, 2))
    p_relay_x(1)
    p_relay_y(0)
    recv(b_ids[0], bsum.at[1])
    bsum[2] = bsum[0] + bsum[1]
    send(b_ids[1], bsum.at[2], bsum.at[3], yn)
    for o in range(4):
        recv(l_id[o], lay.at[slice_at(o), pl.ds(mult((1 - x) * 512, 512), 512)])
    p_last(0)

    dw_ids = [[new() for _ in range(5)] for _ in PARTS]

    def weight_grad(h):
        rows = pl.ds(*PARTS[h])
        lhs = jnp.concatenate([ptg[b, rows, :] for b in range(8)], axis=1)
        rhs = jnp.concatenate([lay[s] for s in range(4)], axis=1)
        acc = jnp.dot(lhs, rhs, preferred_element_type=F32)
        for s in range(4):
            dwf[s, rows, :] = acc[:, s * 128:(s + 1) * 128]
            dwp[s, rows, :] = acc[:, s * 128:(s + 1) * 128].astype(BF16)

    def weight_send(h):
        rows = pl.ds(*PARTS[h])
        for i, s_to in enumerate((m2, e2)):
            send(dw_ids[h][i], dwp.at[s_to, rows], dwr.at[i, rows], mid_dev, ends, mids)
        beside = at(x, y, m + e - z, k)
        send(dw_ids[h][2], dwp.at[m + e - z, rows], dwr.at[2, rows], beside)

    def weight_pass(h):
        rows = pl.ds(*PARTS[h])
        for i, s_to in enumerate((m2, e2)):
            recv(dw_ids[h][i], dwr.at[i, rows], mids)

            @pl.when(mids)
            def _(i=i, s_to=s_to):
                dwp[s_to, rows, :] = (
                    dwf[s_to, rows, :] + dwr[i, rows, :].astype(F32)
                ).astype(BF16)
            send(dw_ids[h][3 + i], dwp.at[s_to, rows], dwr.at[3, rows],
                 at(x, y, s_to, k), mids, (mids, ends)[i])

    weight_grad(0)
    weight_send(0)
    if len(PARTS) > 2:
        p_relay_x(2)
    p_relay_y(1)
    send_layer_grad((3, 4, 5, 6))
    recv(b_ids[1], bsum.at[3])
    bsum[4] = bsum[2] + bsum[3]
    send(b_ids[2], bsum.at[4], bsum.at[5], sib)
    p_last(1)
    weight_grad(1)
    weight_send(1)
    weight_pass(0)
    if len(PARTS) > 2:
        p_relay_y(2)
        p_last(2)
        weight_grad(2)
        weight_send(2)
        weight_pass(1)
    recv(b_ids[2], bsum.at[5])
    bsum[6] = bsum[4] + bsum[5]
    for d in (1, 2, 3):
        send(b_ids[2 + d], bsum.at[6], bsum.at[6 + d], at(x, y, (z + d) % 4, k))

    def layer_grads_here():
        for i, (xx, yy, kk) in zip(dl_ids, dl_to):
            recv(i, dlq.at[xx * 4 + 2 * yy + kk])

    f_in = [new() for _ in range(3)]
    f_out = [[new(), new()] for _ in range(2)]
    f_fin = [new(), new()]
    f_slices = (e2, m2, m)
    own_half = x == z // 2

    def grads(dl, a, scale, at_z, first, n, t, width):
        cols = pl.ds(mult(t * width, width), width)
        lhs = jnp.concatenate(
            [dl[b, pl.ds(first, n)].reshape(n * 128, 128) for b in range(8)], axis=1
        )
        acc = jnp.dot(lhs, a[:, cols], preferred_element_type=F32)
        per = width // 256
        own = jnp.where(own_half & (t // (4 // per) == at_z % 2), 1.0, 0.0)
        diag = []
        for j in range(per):
            qq = (t % (4 // per)) * per + j
            for c in range(2):
                row = scale[qq, c:c + 1, :] * own
                diag.append(
                    dl[c * 4 + qq, pl.ds(first, n)].reshape(n * 128, 128).astype(F32) * row
                )
        return acc + jnp.concatenate(diag, axis=1), cols

    def grads_here(first, n):
        @pl.loop(0, 4)
        def _(t):
            acc, cols = grads(dlq, adj, sbuf, z, first, n, t, 512)
            for i in range(n):
                dff[first + i, :, cols] = acc[i * 128:(i + 1) * 128]

    def grads_end(s, c):
        @pl.loop(2 * c, 2 * c + 2)
        def _(t):
            acc, cols = grads(dle, adj_e, sbuf_e, e, s, 1, t, 512)
            tot = dff[s, :, cols] + acc
            dff[s, :, cols] = tot
            dfp[s, :, cols] = tot.astype(BF16)

    def mid_pass():
        recv(es, sbuf_e, mids)
        for i, qq, on in ((ez, q, esib), (ezy, q_y, efwd)):
            for c in range(2):
                recv(i[c], e_part(qq, c), mids)
                send(on[c], e_part(qq, c), e_part(qq, c), sib, mids, mids)

    def end_send(j):
        s = f_slices[j]
        send(f_in[j], dlq.at[:, s], dle.at[:, s], mid_dev, ends, mids)

    def grads_own(i):
        @pl.when(mids)
        def _():
            grads_here(2 * (pair if i else 1 - pair), 2)
        if i == 0:
            @pl.when(ends)
            def _():
                grads_here(e, 1)


    def mid_ready():
        for c in range(2):
            recv(esib[c], e_part(q_s, c), mids)
            recv(efwd[c], e_part(q_d, c), mids)

    def cut(c):
        return pl.ds(c * 1024, 1024)

    def mid_send(j):
        s_to = f_slices[j]
        recv(f_in[j], dle.at[:, s_to], mids)
        for c in range(2):
            @pl.when(mids)
            def _(c=c):
                grads_end(s_to, c)
            if j < 2:
                send(f_out[j][c], dfp.at[s_to, :, cut(c)], fin.at[j, :, cut(c)],
                     at(x, y, m2, k), mids, mids)

    def mid_merge(c):
        recv(f_out[0][c], fin.at[0, :, cut(c)], mids)

        @pl.when(mids)
        def _():
            dfp[e, :, cut(c)] = (
                dff[e, :, cut(c)] + fin[0, :, cut(c)].astype(F32)
            ).astype(BF16)
        send(f_fin[c], dfp.at[e, :, cut(c)], fin.at[1, :, cut(c)], end_dev, mids, ends)

    def piece(s, qq, c, h):
        first, n = PARTS[h]
        return dw_ref.at[pl.ds((s * 4 + qq) * 8 + c * 4 + first // 256, n // 256)]

    gz = tuple({(d, h): new() for d in (1, 2, 3) for h in range(len(PARTS))} for _ in range(2))
    gx, gy, gxy, gyx = (
        {(h, o): new() for h in range(len(PARTS)) for o in range(4)} for _ in range(4)
    )
    gs, gsd = ([new() for _ in range(4)] for _ in range(2))

    def z_piece(s, h):
        return piece(s, q, x, h)

    def finish(h):
        rows = pl.ds(*PARTS[h])
        recv(dw_ids[h][2], dwr.at[2, rows])
        recv(dw_ids[h][3], dwr.at[3, rows], mids)
        recv(dw_ids[h][4], dwr.at[3, rows], ends)
        for t in range(PARTS[h][0] // 128, sum(PARTS[h]) // 128):
            rr = pl.ds(t * 128, 128)
            tot = dwf[z, rr, :] + dwr[2, rr, :].astype(F32) + dwr[3, rr, :].astype(F32)
            half = t % 2 * 128
            dw_ref[(z * 4 + q) * 8 + x * 4 + t // 2, :, half:half + 128] = tot.T.astype(BF16)
        line_send(gz, z_piece, 1, h)
        spread(h, 0)

    def spread(h, o):
        src = piece(slice_at(o), q, x, h)
        send(gx[h, o], src, src, xn)
        send(gy[h, o], src, src, yn)

    def whole(s, qq):
        return dw_ref.at[pl.ds((s * 4 + qq) * 8, 8)]

    def part(ref, i):
        return ref.at[:, pl.ds(i * 64, 64)]

    def relay(h, o):
        s = slice_at(o)
        from_x, from_y = piece(s, q, 1 - x, h), piece(s, q_y, x, h)
        recv(gx[h, o], from_x)
        send(gxy[h, o], part(from_x, 0), part(from_x, 0), yn)
        if h == len(PARTS) - 1:
            send(gs[o], whole(s, q), whole(s, q), sib)
        recv(gy[h, o], from_y)
        send(gyx[h, o], part(from_y, 1), part(from_y, 1), xn)

    def relay_diag(h, o):
        block = piece(slice_at(o), q_y, 1 - x, h)
        recv(gxy[h, o], part(block, 0))
        recv(gyx[h, o], part(block, 1))
        if h == len(PARTS) - 1:
            send(gsd[o], whole(slice_at(o), q_y), whole(slice_at(o), q_y), sib)

    def last(o):
        recv(gs[o], whole(slice_at(o), q_s))
        recv(gsd[o], whole(slice_at(o), q_d))

    def along(h, d):
        line_recv(gz, z_piece, d, h)
        if d < 3:
            line_send(gz, z_piece, d + 1, h)
        spread(h, d)

    steps = {
        "f": finish, "a": along, "r": relay, "d": relay_diag,
        "E": end_send, "M": mid_send, "G": mid_merge, "R": mid_ready, "H": grads_own, "P": mid_pass,
        "L": layer_grads_here, "W": weight_pass,
    }
    for step in (t for group in ORDER for t in group.split()):
        steps[step[0]](*(int(i) for i in step[1:]))
    for d in (1, 2, 3):
        recv(b_ids[2 + d], bsum.at[6 + d])
    db_ref[...] = bsum[6] + bsum[7] + bsum[8] + bsum[9]

    for c in range(2):
        recv(f_out[1][c], fin.at[1, :, cut(c)], mids)
        recv(f_fin[c], fin.at[1, :, cut(c)], ends)

    @pl.loop(0, 16)
    def _(t):
        cols = pl.ds(mult(t * 128, 128), 128)
        tot = dff[z, :, cols] + fin[1, :, cols].astype(F32)
        dfeat_ref[pl.ds(mult(t * 128, 128), 128), :] = tot.T

    for o in range(4):
        last(o)
    assert not pending and count[0] <= N_SEMS, count
    for i, (c, cond) in sent_by.items():
        when(cond, c.wait_send)


def widen_kernel(dw_ref, out_ref, dfeat_ref, db_ref, dw_out, out_out, dfeat_out, db_out, wide, sem):
    copies = [
        pltpu.make_async_copy(src, dst, sem.at[16 + i])
        for i, (src, dst) in enumerate(
            ((out_ref, out_out), (dfeat_ref, dfeat_out), (db_ref, db_out))
        )
    ]
    for c in copies:
        c.start()
    rows = [
        pltpu.make_async_copy(wide.at[i], dw_out.at[pl.ds(i * 128, 128)], sem.at[i])
        for i in range(16)
    ]
    for i in range(16):
        for j in range(8):
            wide[i, :, j * 256:(j + 1) * 256] = dw_ref[8 * i + j].astype(F32)
        rows[i].start()
    for c in copies + rows:
        c.wait()


N_SEMS = 152


def per_device_fused(features, weight, bias, self_scale, adj_tiles, tile_ids, tile_counts, cotangent):
    vmem = pl.BlockSpec(memory_space=pltpu.VMEM)
    smem = pl.BlockSpec(memory_space=pltpu.SMEM)
    hbm = pl.BlockSpec(memory_space=pl.ANY)
    outputs, d_features, gathered, d_bias = pl.pallas_call(
        fused_kernel,
        out_shape=(
            pltpu.VMEM((128, 2048), F32),
            pltpu.VMEM((2048, 128), F32),
            pltpu.VMEM((128, 128, 256), BF16),
            pltpu.VMEM((16, 128), F32),
        ),
        in_specs=[smem, smem, hbm, hbm, hbm, vmem, vmem, hbm],
        out_specs=(vmem, vmem, vmem, vmem),
        scratch_shapes=[
            pltpu.VMEM((32, 128, 128), BF16),
            pltpu.VMEM((128, 2048), BF16),
            pltpu.VMEM((1024, 2048), BF16),
            pltpu.VMEM((1024, 2048), BF16),
            pltpu.VMEM((4, 2048, 128), BF16),
            pltpu.VMEM((2048, 2048), BF16),
            pltpu.VMEM((4, 8, 128), F32),
            pltpu.VMEM((4, 8, 128), F32),
            pltpu.VMEM((8, 128, 128), F32),
            pltpu.VMEM((4, 512, 128), BF16),
            pltpu.VMEM((4, 512, 128), BF16),
            pltpu.VMEM((4, 512, 128), F32),
            pltpu.VMEM((4, 1024, 128), BF16),
            pltpu.VMEM((16, 128, 128), BF16),
            pltpu.VMEM((128, 2048), F32),
            pltpu.VMEM((2048, 128), BF16),
            pltpu.VMEM((8, 1024, 128), BF16),
            pltpu.VMEM((4, 4, 128, 128), BF16),
            pltpu.VMEM((8, 4, 128, 128), BF16),
            pltpu.VMEM((4, 1024, 128), F32),
            pltpu.VMEM((4, 1024, 128), BF16),
            pltpu.VMEM((4, 1024, 128), BF16),
            pltpu.VMEM((4, 128, 2048), F32),
            pltpu.VMEM((4, 128, 2048), BF16),
            pltpu.VMEM((8, 4, 128, 128), BF16),
            pltpu.VMEM((2, 128, 2048), BF16),
            pltpu.VMEM((10, 16, 128), F32),
            pltpu.VMEM((16, 128), F32),
            pltpu.SemaphoreType.DMA((N_SEMS,)),
            pltpu.SemaphoreType.DMA((N_SEMS,)),
            pltpu.SemaphoreType.DMA((4,)),
        ],
        compiler_params=pltpu.CompilerParams(
            collective_id=0, has_side_effects=True, vmem_limit_bytes=53 * MIB
        ),
        cost_estimate=pl.CostEstimate(
            flops=7_600_000_000, bytes_accessed=24 * MIB, transcendentals=262144
        ),
    )(
        tile_ids[0, 0], tile_counts[0], adj_tiles[0, 0], features, weight,
        bias.reshape(16, 128), self_scale.reshape(2, 128), cotangent,
    )
    d_weight, outputs, d_features, d_bias = pl.pallas_call(
        widen_kernel,
        out_shape=(
            jax.ShapeDtypeStruct((2048, 2048), F32),
            jax.ShapeDtypeStruct((128, 2048), F32),
            jax.ShapeDtypeStruct((2048, 128), F32),
            jax.ShapeDtypeStruct((16, 128), F32),
        ),
        in_specs=[vmem] * 4,
        out_specs=(hbm, hbm, hbm, hbm),
        scratch_shapes=[pltpu.VMEM((16, 128, 2048), F32), pltpu.SemaphoreType.DMA((19,))],
        compiler_params=pltpu.CompilerParams(vmem_limit_bytes=30 * MIB),
    )(gathered, outputs, d_features, d_bias)
    return outputs, d_features, d_weight, d_bias.reshape(2048)


def solution(mesh):
    fits = dict(mesh.shape) == {"row": 16, "col": 2}

    def run(*arrays):
        fused = fits and arrays[0].shape == (4096, 2048) and arrays[4].shape[2] == 32
        return jax.shard_map(
            per_device_fused if fused else per_device_any,
            mesh=mesh,
            in_specs=(
                P("col", "row"),
                P(),
                P(),
                P("row"),
                P("row", "col", None, None, None),
                P("row", "col", None),
                P("row", "col"),
                P(("row", "col"), None),
            ),
            out_specs=(P(("row", "col"), None), P("col", "row"), P(), P()),
            check_vma=False,
        )(*arrays)

    return run
```

```python
import jax
import jax.numpy as jnp
from jax import lax
from jax.experimental import pallas as pl
from jax.experimental.pallas import tpu as pltpu
from jax.sharding import PartitionSpec as P

MESH = pl.DeviceIdType.MESH
F32 = jnp.float32
BF16 = jnp.bfloat16
MIB = 2**20
ORDER = (
    "f0 W1 a01 r00",
    "L H0 r01 f1",
    "a02 P H1 E0",
    "R E1 d00 a11",
    "r10 d01 M0 d10",
    "a03 E2 r02 a12",
    "G0 M1 r03 r11",
    "d02 a13 G1 d03",
    "d11 r12 M2 r13",
    "d13 d12",
)
NC = 2
PARTS = ((0, 512), (512, 512))


def dense_block(tiles, ids, count, tile_rows, tile_cols):
    slots = jnp.arange(tiles.shape[0], dtype=jnp.int32)
    live = jnp.where((slots < count)[:, None, None], tiles, jnp.zeros_like(tiles))
    blank = jnp.zeros((tile_rows * tile_cols, 128, 128), tiles.dtype)
    placed = blank.at[ids].add(live, unique_indices=True)
    placed = placed.reshape(tile_rows, tile_cols, 128, 128)
    return placed.transpose(0, 2, 1, 3).reshape(tile_rows * 128, tile_cols * 128)


def per_device_any(features, weight, bias, self_scale, adj_tiles, tile_ids, tile_counts, cotangent):
    row_block = self_scale.shape[0]
    col_block = features.shape[0]
    block = dense_block(
        adj_tiles[0, 0], tile_ids[0, 0], tile_counts[0, 0], row_block // 128, col_block // 128
    )
    start_row = lax.axis_index("row") * row_block
    col_no = lax.axis_index("col")
    inside = col_no == start_row // col_block
    offset = jnp.where(inside, start_row - col_no * col_block, 0)
    self_rows = jnp.where(inside, self_scale, 0.0)[:, None]
    piece = lax.all_gather(features, "row", axis=1, tiled=True)
    terms = jnp.dot(block, piece, preferred_element_type=F32)
    terms = terms + self_rows * lax.dynamic_slice_in_dim(piece, offset, row_block, 0)
    layer_in = lax.psum_scatter(terms, "col", scatter_dimension=0, tiled=True).astype(BF16)
    pre_act = jnp.dot(layer_in, weight, preferred_element_type=F32) + bias.astype(F32)
    sig = jax.nn.sigmoid(pre_act)
    outputs = pre_act * sig
    slope = sig * (1.0 + pre_act * (1.0 - sig))
    d_pre = (cotangent.astype(F32) * slope).astype(BF16)
    d_weight = lax.dot_general(
        layer_in, d_pre, (((0,), (0,)), ((), ())), preferred_element_type=F32
    )
    d_bias = jnp.sum(d_pre.astype(F32), axis=0)
    d_weight, d_bias = lax.psum((d_weight, d_bias), ("row", "col"))
    d_layer = lax.dot_general(
        d_pre, weight, (((1,), (1,)), ((), ())), preferred_element_type=F32
    ).astype(BF16)
    whole = lax.all_gather(d_layer, "col", axis=0, tiled=True)
    spread = lax.dot_general(block, whole, (((0,), (0,)), ((), ())), preferred_element_type=F32)
    own = lax.dynamic_slice_in_dim(spread, offset, row_block, 0) + self_rows * whole
    spread = lax.dynamic_update_slice_in_dim(spread, own, offset, 0)
    d_features = lax.psum_scatter(spread, "row", scatter_dimension=1, tiled=True)
    return outputs, d_features, d_weight, d_bias


def fused_kernel(
    ids_ref, count_ref, tiles_hbm, feat_ref, w_ref, bias_ref, scale_ref, cot_hbm,
    out_ref, dfeat_ref, dw_ref, db_ref,
    tiles_ref, cot_ref, adj, adj_e, hid, wv, sbuf, sbuf_e, scol, xs, xr, keep, lay, xrow, pre, pt, ptg, dls, dlq,
    dwf, dwp, dwr, dff, dfp, dle, fin, bsum, bias32, ssem, rsem, lsem,
):
    r = lax.axis_index("row")
    x = lax.axis_index("col")
    z = r // 4
    y = (r // 2) % 2
    k = r % 2
    q = 2 * y + k
    ends = (z == 0) | (z == 3)
    mids = (z == 1) | (z == 2)

    def at(xx, yy, zz, kk):
        return (zz * 4 + yy * 2 + kk, xx)

    sib = at(x, y, z, 1 - k)
    xn = at(1 - x, y, z, k)
    yn = at(x, 1 - y, z, k)
    dg = at(x, 1 - y, z, 1 - k)
    zr = at(x, y, jnp.minimum(z + 1, 3), k)
    zl = at(x, y, jnp.maximum(z - 1, 0), k)
    q_y = 2 * (1 - y) + k
    q_s = 2 * y + 1 - k
    q_d = 3 - q

    count = [0]
    sent_by = {}
    pending = {}

    def new():
        count[0] += 1
        return count[0] - 1

    def when(cond, fn):
        if cond is None:
            fn()
        else:
            pl.when(cond)(fn)

    def copy(i, src, dst, to):
        return pltpu.make_async_remote_copy(
            src_ref=src, dst_ref=dst, send_sem=ssem.at[i], recv_sem=rsem.at[i],
            device_id=to, device_id_type=MESH,
        )

    def send(i, src, dst, to, cond=None, rcond=None):
        c = copy(i, src, dst, to)
        when(cond, c.start)
        sent_by[i] = (c, cond)
        pending[i] = (dst, rcond)

    def recv(i, dst, cond=None):
        pending.pop(i, None)
        c = copy(i, dst, dst, sib)
        when(cond, c.wait_recv)

    def slice_at(o):
        return [z, z + 1 - 2 * (z % 2), 2 - z // 2, 3 - 3 * (z // 2)][o]

    def mult(v, n):
        return pl.multiple_of(v, n)

    barrier = pltpu.get_barrier_semaphore()
    near = [(sib, None), (xn, None), (yn, None), (zr, z <= 2), (zl, z >= 1)]
    for peer, cond in near:
        when(cond, lambda peer=peer: pl.semaphore_signal(
            barrier, inc=1, device_id=peer, device_id_type=MESH
        ))

    w_copy = pltpu.make_async_copy(w_ref, wv, lsem.at[0])
    h_copy = pltpu.make_async_copy(feat_ref, hid.at[z], lsem.at[1])
    t_copy = pltpu.make_async_copy(tiles_hbm, tiles_ref, lsem.at[2])
    c_copy = pltpu.make_async_copy(cot_hbm, cot_ref, lsem.at[3])
    t_copy.start()
    h_copy.start()
    t_copy.wait()

    for c in range(2):
        @pl.loop(0, 16)
        def _(t, c=c):
            slot = jnp.int32(0)
            for i in range(32):
                slot = jnp.where(ids_ref[i] == c * 16 + t, i, slot)
            live = jnp.where(slot < count_ref[0], 1.0, 0.0)
            tile = tiles_ref[slot].astype(F32) * live
            adj[pl.ds(mult(c * 512 + q * 128, 128), 128), pl.ds(mult(t * 128, 128), 128)] = (
                tile.astype(BF16)
            )
    for i in range(4):
        sbuf[q, 2 * i:2 * i + 2, :] = scale_ref[...]
    bias32[...] = bias_ref[...].astype(F32)
    h_copy.wait()
    w_copy.start()
    c_copy.start()
    pl.semaphore_wait(barrier, jnp.where(ends, 4, 5))

    def h_part(s, c):
        return hid.at[s, pl.ds(c * (2048 // NC), 2048 // NC)]

    right = {(d, c): new() for d in (1, 2, 3) for c in range(NC)}
    left = {(d, c): new() for d in (1, 2, 3) for c in range(NC)}

    def line_send(ids, part, d, c, own_ok=True):
        sr, sl = jnp.maximum(z - (d - 1), 0), jnp.minimum(z + d - 1, 3)
        send(ids[0][d, c], part(sr, c), part(sr, c), zr, (z >= d - 1) & (z <= 2), z >= d)
        send(ids[1][d, c], part(sl, c), part(sl, c), zl, (z <= 4 - d) & (z >= 1), z <= 3 - d)

    def line_recv(ids, part, d, c):
        sr, sl = jnp.maximum(z - d, 0), jnp.minimum(z + d, 3)
        recv(ids[0][d, c], part(sr, c), z >= d)
        recv(ids[1][d, c], part(sl, c), z <= 3 - d)

    hz = (right, left)
    for c in range(NC):
        line_send(hz, h_part, 1, c)

    s_id = [new() for _ in range(3)]
    send(s_id[0], sbuf.at[q], sbuf.at[q], yn)
    send(s_id[1], sbuf.at[q], sbuf.at[q], sib)

    def a_part(qq, c):
        return adj.at[pl.ds(mult(c * 512 + qq * 128, 128), 128)]

    halves = (1 - x, x)
    ay, asib, afwd = ([new(), new()] for _ in range(3))
    for i, c in enumerate(halves):
        send(asib[i], a_part(q, c), a_part(q, c), sib)
    send(ay[0], a_part(q, 1 - x), a_part(q, 1 - x), yn)

    line_recv(hz, h_part, 1, 0)
    line_send(hz, h_part, 2, 0)
    send(ay[1], a_part(q, x), a_part(q, x), yn)

    recv(s_id[0], sbuf.at[q_y])
    send(s_id[2], sbuf.at[q_y], sbuf.at[q_y], sib)
    recv(s_id[1], sbuf.at[q_s])
    recv(s_id[2], sbuf.at[q_d])
    inside = jnp.where(x == z // 2, 1.0, 0.0)
    for b in range(8):
        row = sbuf[b % 4, b // 4:b // 4 + 1, :] * inside
        scol[b] = jnp.broadcast_to(row, (128, 128)).T

    line_recv(hz, h_part, 1, 1)
    line_send(hz, h_part, 2, 1)

    pair = z // 2
    e, m = 3 * pair, 1 + pair
    e2, m2 = 3 - 3 * pair, 2 - pair
    mid_dev, end_dev = at(x, y, m, k), at(x, y, e, k)

    def e_part(qq, c):
        return adj_e.at[pl.ds(mult(c * 512 + qq * 128, 128), 128)]

    ez, ezy, esib, efwd = ([new(), new()] for _ in range(4))
    es = new()
    for c in range(2):
        send(ez[c], a_part(q, c), e_part(q, c), mid_dev, ends, mids)
    send(es, sbuf, sbuf_e, mid_dev, ends, mids)

    x_id = [[new(), new()] for _ in range(4)]
    l_id = [new() for _ in range(4)]
    row_id = [[new() for _ in range(3)] for _ in range(4)]
    w_waited = []

    def aggregate(o, c, u):
        s = slice_at(o)
        first = (1 - y if u == 0 else y) * 256
        rows = pl.ds(mult(first, 256), 256)
        acc = jnp.dot(
            adj[pl.ds(mult(halves[c] * 512 + first, 256), 256), :], hid[s],
            preferred_element_type=F32,
        )
        own = []
        for i in range(2):
            qq = first // 128 + i
            at_node = mult((z % 2) * 1024 + qq * 256 + halves[c] * 128, 128)
            own.append(scol[halves[c] * 4 + qq] * hid[s, pl.ds(at_node, 128), :].astype(F32))
        acc = acc + jnp.concatenate(own, axis=0)
        if c == 0:
            xs[o, rows] = acc.astype(BF16)
            send(x_id[o][u], xs.at[o, rows], xr.at[o, rows], xn)
        else:
            keep[o, rows] = acc

    def combine(o):
        s = slice_at(o)
        sends = list(zip(row_id[o], (q_y, q_d, q_s), (yn, dg, sib)))
        for u in range(2):
            first = (1 - y if u == 0 else y) * 256
            rows = pl.ds(mult(first, 256), 256)
            recv(x_id[o][u], xr.at[o, rows])
            mine = pl.ds(mult(x * 512 + first, 256), 256)
            lay[s, mine, :] = (keep[o, rows] + xr[o, rows].astype(F32)).astype(BF16)
            for i, qq, to in (sends[:2], sends[2:])[u]:
                piece_rows = pl.ds(mult(x * 512 + qq * 128, 128), 128)
                send(i, lay.at[s, piece_rows], xrow.at[s * 4 + q], to)
        xrow[s * 4 + q] = lay[s, pl.ds(mult(x * 512 + q * 128, 128), 128), :]

    def share(o):
        half = lay.at[slice_at(o), pl.ds(mult(x * 512, 512), 512)]
        send(l_id[o], half, half, xn)

    def linear(o):
        s = slice_at(o)
        for i, qq in zip(row_id[o], (q_y, q_d, q_s)):
            recv(i, xrow.at[s * 4 + qq])
        if not w_waited:
            w_copy.wait()
            c_copy.wait()
            w_waited.append(True)
        block = jnp.concatenate([xrow[s * 4 + i] for i in range(4)], axis=1)

        @pl.loop(0, 2)
        def _(t):
            cols = pl.ds(mult(t * 1024, 1024), 1024)
            prod = jnp.dot(
                block, wv[pl.ds(mult(s * 512, 512), 512), cols], preferred_element_type=F32
            )
            if o == 0:
                pre[:, cols] = prod
            else:
                pre[:, cols] += prod

    for i in range(2):
        recv(asib[i], a_part(q_s, halves[i]))
    for o in range(2):
        aggregate(o, 0, 1)
        aggregate(o, 1, 1)
    recv(ay[0], a_part(q_y, 1 - x))
    send(afwd[0], a_part(q_y, 1 - x), a_part(q_y, 1 - x), sib)
    recv(afwd[0], a_part(q_d, 1 - x))
    aggregate(0, 0, 0)
    line_recv(hz, h_part, 2, 0)
    line_send(hz, h_part, 3, 0)
    aggregate(1, 0, 0)
    line_recv(hz, h_part, 2, 1)
    line_send(hz, h_part, 3, 1)
    for c, u in ((0, 0), (0, 1), (1, 1)):
        aggregate(2, c, u)
    recv(ay[1], a_part(q_y, x))
    send(afwd[1], a_part(q_y, x), a_part(q_y, x), sib)
    for c in range(2):
        send(ezy[c], a_part(q_y, c), e_part(q_y, c), mid_dev, ends, mids)
    recv(afwd[1], a_part(q_d, x))
    for o in range(3):
        aggregate(o, 1, 0)
        combine(o)
        if o < 2:
            share(o)
    linear(0)
    linear(1)
    for c in range(NC):
        line_recv(hz, h_part, 3, c)
    for c, u in ((0, 0), (0, 1), (1, 0), (1, 1)):
        aggregate(3, c, u)
    linear(2)
    combine(3)
    share(3)
    share(2)
    linear(3)

    def p_part(c, h):
        return pt.at[pl.ds(mult(c * 1024 + PARTS[h][0], 256), PARTS[h][1])]

    def activate(c, h):
        @pl.loop(PARTS[h][0] // 128, sum(PARTS[h]) // 128)
        def _(i):
            t = c * 8 + i
            cols = pl.ds(mult(t * 128, 128), 128)
            v = pre[:, cols] + bias32[pl.ds(t, 1), :]
            sig = jax.nn.sigmoid(v)
            out_ref[:, cols] = v * sig
            slope = sig * (1.0 + v * (1.0 - sig))
            d32 = (cot_ref[:, cols].astype(F32) * slope).astype(BF16).astype(F32)
            pt[pl.ds(mult(t * 128, 128), 128), :] = d32.T.astype(BF16)
            bsum[0, pl.ds(t, 1), :] = jnp.sum(d32, axis=0, keepdims=True)

    b_own, b_x = x * 4 + q, (1 - x) * 4 + q
    px, py, pyf, ps, psf, pd, pdf = ([new() for _ in PARTS] for _ in range(7))
    b_ids = [new() for _ in range(6)]

    def p_at(b, h):
        return ptg.at[b, pl.ds(*PARTS[h])]

    def p_send(h):
        send(px[h], p_part(1 - x, h), p_at(b_own, h), xn)
        send(py[h], p_part(x, h), p_at(b_own, h), yn)
        send(ps[h], p_part(x, h), p_at(b_own, h), sib)
        first, n = PARTS[h]
        ptg[b_own, first:first + n] = pt[pl.ds(mult(x * 1024 + first, 256), n), :]

    def p_relay_x(h):
        recv(px[h], p_at(b_x, h))
        send(pyf[h], p_at(b_x, h), p_at(b_x, h), yn)
        send(psf[h], p_at(b_x, h), p_at(b_x, h), sib)
        recv(py[h], p_at(x * 4 + q_y, h))
        send(pd[h], p_at(x * 4 + q_y, h), p_at(x * 4 + q_y, h), sib)

    def p_relay_y(h):
        recv(pyf[h], p_at((1 - x) * 4 + q_y, h))
        send(pdf[h], p_at((1 - x) * 4 + q_y, h), p_at((1 - x) * 4 + q_y, h), sib)

    def p_last(h):
        recv(ps[h], p_at(x * 4 + q_s, h))
        recv(psf[h], p_at((1 - x) * 4 + q_s, h))
        recv(pd[h], p_at(x * 4 + q_d, h))
        recv(pdf[h], p_at((1 - x) * 4 + q_d, h))

    activate(1 - x, 0)
    activate(x, 0)
    p_send(0)
    activate(1 - x, 1)
    activate(x, 1)
    if len(PARTS) > 2:
        p_send(1)
        activate(1 - x, 2)
        activate(x, 2)

    @pl.loop(0, 2)
    def _(i):
        acc = jnp.dot(
            wv[pl.ds(mult(i * 1024, 1024), 1024), :], pt[...], preferred_element_type=F32
        ).astype(BF16)
        for j in range(2):
            for qq in range(4):
                first = j * 512 + qq * 128
                dls[qq, i * 2 + j] = acc[first:first + 128]

    dl_to = [
        (1 - x, y, k), (1 - x, y, 1 - k), (x, y, 1 - k),
        (x, 1 - y, k), (x, 1 - y, 1 - k), (1 - x, 1 - y, k), (1 - x, 1 - y, 1 - k),
    ]
    dl_ids = [new() for _ in dl_to]

    def send_layer_grad(which):
        for i in which:
            xx, yy, kk = dl_to[i]
            send(dl_ids[i], dls.at[2 * yy + kk], dlq.at[b_own], at(xx, yy, z, kk))

    p_send(len(PARTS) - 1)
    send(b_ids[0], bsum.at[0], bsum.at[1], xn)
    dlq[b_own] = dls[q]
    p_relay_x(0)
    send_layer_grad((0, 1, 2))
    p_relay_x(1)
    p_relay_y(0)
    recv(b_ids[0], bsum.at[1])
    bsum[2] = bsum[0] + bsum[1]
    send(b_ids[1], bsum.at[2], bsum.at[3], yn)
    for o in range(4):
        recv(l_id[o], lay.at[slice_at(o), pl.ds(mult((1 - x) * 512, 512), 512)])
    p_last(0)

    dw_ids = [[new() for _ in range(5)] for _ in PARTS]

    def weight_grad(h):
        rows = pl.ds(*PARTS[h])
        lhs = jnp.concatenate([ptg[b, rows, :] for b in range(8)], axis=1)
        rhs = jnp.concatenate([lay[s] for s in range(4)], axis=1)
        acc = jnp.dot(lhs, rhs, preferred_element_type=F32)
        for s in range(4):
            dwf[s, rows, :] = acc[:, s * 128:(s + 1) * 128]
            dwp[s, rows, :] = acc[:, s * 128:(s + 1) * 128].astype(BF16)

    def weight_send(h):
        rows = pl.ds(*PARTS[h])
        for i, s_to in enumerate((m2, e2)):
            send(dw_ids[h][i], dwp.at[s_to, rows], dwr.at[i, rows], mid_dev, ends, mids)
        beside = at(x, y, m + e - z, k)
        send(dw_ids[h][2], dwp.at[m + e - z, rows], dwr.at[2, rows], beside)

    def weight_pass(h):
        rows = pl.ds(*PARTS[h])
        for i, s_to in enumerate((m2, e2)):
            recv(dw_ids[h][i], dwr.at[i, rows], mids)

            @pl.when(mids)
            def _(i=i, s_to=s_to):
                dwp[s_to, rows, :] = (
                    dwf[s_to, rows, :] + dwr[i, rows, :].astype(F32)
                ).astype(BF16)
            send(dw_ids[h][3 + i], dwp.at[s_to, rows], dwr.at[3, rows],
                 at(x, y, s_to, k), mids, (mids, ends)[i])

    weight_grad(0)
    weight_send(0)
    if len(PARTS) > 2:
        p_relay_x(2)
    p_relay_y(1)
    send_layer_grad((3, 4, 5, 6))
    recv(b_ids[1], bsum.at[3])
    bsum[4] = bsum[2] + bsum[3]
    send(b_ids[2], bsum.at[4], bsum.at[5], sib)
    p_last(1)
    weight_grad(1)
    weight_send(1)
    weight_pass(0)
    if len(PARTS) > 2:
        p_relay_y(2)
        p_last(2)
        weight_grad(2)
        weight_send(2)
        weight_pass(1)
    recv(b_ids[2], bsum.at[5])
    bsum[6] = bsum[4] + bsum[5]
    for d in (1, 2, 3):
        send(b_ids[2 + d], bsum.at[6], bsum.at[6 + d], at(x, y, (z + d) % 4, k))

    def layer_grads_here():
        for i, (xx, yy, kk) in zip(dl_ids, dl_to):
            recv(i, dlq.at[xx * 4 + 2 * yy + kk])

    f_in = [new() for _ in range(3)]
    f_out = [[new(), new()] for _ in range(2)]
    f_fin = [new(), new()]
    f_slices = (e2, m2, m)
    own_half = x == z // 2

    def grads(dl, a, scale, at_z, first, n, t, width):
        cols = pl.ds(mult(t * width, width), width)
        lhs = jnp.concatenate(
            [dl[b, pl.ds(first, n)].reshape(n * 128, 128) for b in range(8)], axis=1
        )
        acc = jnp.dot(lhs, a[:, cols], preferred_element_type=F32)
        per = width // 256
        own = jnp.where(own_half & (t // (4 // per) == at_z % 2), 1.0, 0.0)
        diag = []
        for j in range(per):
            qq = (t % (4 // per)) * per + j
            for c in range(2):
                row = scale[qq, c:c + 1, :] * own
                diag.append(
                    dl[c * 4 + qq, pl.ds(first, n)].reshape(n * 128, 128).astype(F32) * row
                )
        return acc + jnp.concatenate(diag, axis=1), cols

    def grads_here(first, n):
        @pl.loop(0, 4)
        def _(t):
            acc, cols = grads(dlq, adj, sbuf, z, first, n, t, 512)
            for i in range(n):
                dff[first + i, :, cols] = acc[i * 128:(i + 1) * 128]

    def grads_end(s, c):
        @pl.loop(2 * c, 2 * c + 2)
        def _(t):
            acc, cols = grads(dle, adj_e, sbuf_e, e, s, 1, t, 512)
            tot = dff[s, :, cols] + acc
            dff[s, :, cols] = tot
            dfp[s, :, cols] = tot.astype(BF16)

    def mid_pass():
        recv(es, sbuf_e, mids)
        for i, qq, on in ((ez, q, esib), (ezy, q_y, efwd)):
            for c in range(2):
                recv(i[c], e_part(qq, c), mids)
                send(on[c], e_part(qq, c), e_part(qq, c), sib, mids, mids)

    def end_send(j):
        s = f_slices[j]
        send(f_in[j], dlq.at[:, s], dle.at[:, s], mid_dev, ends, mids)

    def grads_own(i):
        @pl.when(mids)
        def _():
            grads_here(2 * (pair if i else 1 - pair), 2)
        if i == 0:
            @pl.when(ends)
            def _():
                grads_here(e, 1)


    def mid_ready():
        for c in range(2):
            recv(esib[c], e_part(q_s, c), mids)
            recv(efwd[c], e_part(q_d, c), mids)

    def cut(c):
        return pl.ds(c * 1024, 1024)

    def mid_send(j):
        s_to = f_slices[j]
        recv(f_in[j], dle.at[:, s_to], mids)
        for c in range(2):
            @pl.when(mids)
            def _(c=c):
                grads_end(s_to, c)
            if j < 2:
                send(f_out[j][c], dfp.at[s_to, :, cut(c)], fin.at[j, :, cut(c)],
                     at(x, y, m2, k), mids, mids)

    def mid_merge(c):
        recv(f_out[0][c], fin.at[0, :, cut(c)], mids)

        @pl.when(mids)
        def _():
            dfp[e, :, cut(c)] = (
                dff[e, :, cut(c)] + fin[0, :, cut(c)].astype(F32)
            ).astype(BF16)
        send(f_fin[c], dfp.at[e, :, cut(c)], fin.at[1, :, cut(c)], end_dev, mids, ends)

    def piece(s, qq, c, h):
        return dw_ref.at[pl.ds((s * 4 + qq) * 8 + h * 4 + c * 2, 2)]

    gz = tuple({(d, h): new() for d in (1, 2, 3) for h in range(len(PARTS))} for _ in range(2))
    gx, gy, gxy, gyx, gs, gsd = (
        {(h, o): new() for h in range(len(PARTS)) for o in range(4)} for _ in range(6)
    )

    def z_piece(s, h):
        return piece(s, q, x, h)

    def finish(h):
        rows = pl.ds(*PARTS[h])
        recv(dw_ids[h][2], dwr.at[2, rows])
        recv(dw_ids[h][3], dwr.at[3, rows], mids)
        recv(dw_ids[h][4], dwr.at[3, rows], ends)
        for t in range(PARTS[h][0] // 128, sum(PARTS[h]) // 128):
            rr = pl.ds(t * 128, 128)
            tot = dwf[z, rr, :] + dwr[2, rr, :].astype(F32) + dwr[3, rr, :].astype(F32)
            half = t % 2 * 128
            at_block = (z * 4 + q) * 8 + h * 4 + x * 2 + t % 4 // 2
            dw_ref[at_block, :, half:half + 128] = tot.T.astype(BF16)
        line_send(gz, z_piece, 1, h)
        spread(h, 0)

    def spread(h, o):
        src = piece(slice_at(o), q, x, h)
        send(gx[h, o], src, src, xn)
        send(gy[h, o], src, src, yn)

    def both(s, qq, h):
        return dw_ref.at[pl.ds((s * 4 + qq) * 8 + h * 4, 4)]

    def part(ref, i):
        return ref.at[:, pl.ds(i * 64, 64)]

    def relay(h, o):
        s = slice_at(o)
        from_x, from_y = piece(s, q, 1 - x, h), piece(s, q_y, x, h)
        recv(gx[h, o], from_x)
        send(gxy[h, o], part(from_x, 0), part(from_x, 0), yn)
        send(gs[h, o], both(s, q, h), both(s, q, h), sib)
        recv(gy[h, o], from_y)
        send(gyx[h, o], part(from_y, 1), part(from_y, 1), xn)

    def relay_diag(h, o):
        block = piece(slice_at(o), q_y, 1 - x, h)
        recv(gxy[h, o], part(block, 0))
        recv(gyx[h, o], part(block, 1))
        send(gsd[h, o], both(slice_at(o), q_y, h), both(slice_at(o), q_y, h), sib)

    def last(h, o):
        recv(gs[h, o], both(slice_at(o), q_s, h))
        recv(gsd[h, o], both(slice_at(o), q_d, h))

    def along(h, d):
        line_recv(gz, z_piece, d, h)
        if d < 3:
            line_send(gz, z_piece, d + 1, h)
        spread(h, d)

    steps = {
        "f": finish, "a": along, "r": relay, "d": relay_diag,
        "E": end_send, "M": mid_send, "G": mid_merge, "R": mid_ready, "H": grads_own, "P": mid_pass,
        "L": layer_grads_here, "W": weight_pass,
    }
    for step in (t for group in ORDER for t in group.split()):
        steps[step[0]](*(int(i) for i in step[1:]))
    for d in (1, 2, 3):
        recv(b_ids[2 + d], bsum.at[6 + d])
    db_ref[...] = bsum[6] + bsum[7] + bsum[8] + bsum[9]

    for c in range(2):
        recv(f_out[1][c], fin.at[1, :, cut(c)], mids)
        recv(f_fin[c], fin.at[1, :, cut(c)], ends)

    @pl.loop(0, 16)
    def _(t):
        cols = pl.ds(mult(t * 128, 128), 128)
        tot = dff[z, :, cols] + fin[1, :, cols].astype(F32)
        dfeat_ref[pl.ds(mult(t * 128, 128), 128), :] = tot.T

    for h in range(len(PARTS)):
        for o in range(4):
            last(h, o)
    assert not pending and count[0] <= N_SEMS, count
    for i, (c, cond) in sent_by.items():
        when(cond, c.wait_send)


def widen_kernel(dw_ref, out_ref, dfeat_ref, db_ref, dw_out, out_out, dfeat_out, db_out, wide, sem):
    copies = [
        pltpu.make_async_copy(src, dst, sem.at[16 + i])
        for i, (src, dst) in enumerate(
            ((out_ref, out_out), (dfeat_ref, dfeat_out), (db_ref, db_out))
        )
    ]
    for c in copies:
        c.start()
    rows = [
        pltpu.make_async_copy(wide.at[i], dw_out.at[pl.ds(i * 128, 128)], sem.at[i])
        for i in range(16)
    ]
    for i in range(16):
        for j in range(8):
            block = 8 * i + j % 4 // 2 * 4 + j // 4 * 2 + j % 2
            wide[i, :, j * 256:(j + 1) * 256] = dw_ref[block].astype(F32)
        rows[i].start()
    for c in copies + rows:
        c.wait()


N_SEMS = 160


def per_device_fused(features, weight, bias, self_scale, adj_tiles, tile_ids, tile_counts, cotangent):
    vmem = pl.BlockSpec(memory_space=pltpu.VMEM)
    smem = pl.BlockSpec(memory_space=pltpu.SMEM)
    hbm = pl.BlockSpec(memory_space=pl.ANY)
    outputs, d_features, gathered, d_bias = pl.pallas_call(
        fused_kernel,
        out_shape=(
            pltpu.VMEM((128, 2048), F32),
            pltpu.VMEM((2048, 128), F32),
            pltpu.VMEM((128, 128, 256), BF16),
            pltpu.VMEM((16, 128), F32),
        ),
        in_specs=[smem, smem, hbm, hbm, hbm, vmem, vmem, hbm],
        out_specs=(vmem, vmem, vmem, vmem),
        scratch_shapes=[
            pltpu.VMEM((32, 128, 128), BF16),
            pltpu.VMEM((128, 2048), BF16),
            pltpu.VMEM((1024, 2048), BF16),
            pltpu.VMEM((1024, 2048), BF16),
            pltpu.VMEM((4, 2048, 128), BF16),
            pltpu.VMEM((2048, 2048), BF16),
            pltpu.VMEM((4, 8, 128), F32),
            pltpu.VMEM((4, 8, 128), F32),
            pltpu.VMEM((8, 128, 128), F32),
            pltpu.VMEM((4, 512, 128), BF16),
            pltpu.VMEM((4, 512, 128), BF16),
            pltpu.VMEM((4, 512, 128), F32),
            pltpu.VMEM((4, 1024, 128), BF16),
            pltpu.VMEM((16, 128, 128), BF16),
            pltpu.VMEM((128, 2048), F32),
            pltpu.VMEM((2048, 128), BF16),
            pltpu.VMEM((8, 1024, 128), BF16),
            pltpu.VMEM((4, 4, 128, 128), BF16),
            pltpu.VMEM((8, 4, 128, 128), BF16),
            pltpu.VMEM((4, 1024, 128), F32),
            pltpu.VMEM((4, 1024, 128), BF16),
            pltpu.VMEM((4, 1024, 128), BF16),
            pltpu.VMEM((4, 128, 2048), F32),
            pltpu.VMEM((4, 128, 2048), BF16),
            pltpu.VMEM((8, 4, 128, 128), BF16),
            pltpu.VMEM((2, 128, 2048), BF16),
            pltpu.VMEM((10, 16, 128), F32),
            pltpu.VMEM((16, 128), F32),
            pltpu.SemaphoreType.DMA((N_SEMS,)),
            pltpu.SemaphoreType.DMA((N_SEMS,)),
            pltpu.SemaphoreType.DMA((4,)),
        ],
        compiler_params=pltpu.CompilerParams(
            collective_id=0, has_side_effects=True, vmem_limit_bytes=53 * MIB
        ),
        cost_estimate=pl.CostEstimate(
            flops=7_600_000_000, bytes_accessed=24 * MIB, transcendentals=262144
        ),
    )(
        tile_ids[0, 0], tile_counts[0], adj_tiles[0, 0], features, weight,
        bias.reshape(16, 128), self_scale.reshape(2, 128), cotangent,
    )
    d_weight, outputs, d_features, d_bias = pl.pallas_call(
        widen_kernel,
        out_shape=(
            jax.ShapeDtypeStruct((2048, 2048), F32),
            jax.ShapeDtypeStruct((128, 2048), F32),
            jax.ShapeDtypeStruct((2048, 128), F32),
            jax.ShapeDtypeStruct((16, 128), F32),
        ),
        in_specs=[vmem] * 4,
        out_specs=(hbm, hbm, hbm, hbm),
        scratch_shapes=[pltpu.VMEM((16, 128, 2048), F32), pltpu.SemaphoreType.DMA((19,))],
        compiler_params=pltpu.CompilerParams(vmem_limit_bytes=30 * MIB),
    )(gathered, outputs, d_features, d_bias)
    return outputs, d_features, d_weight, d_bias.reshape(2048)


def solution(mesh):
    fits = dict(mesh.shape) == {"row": 16, "col": 2}

    def run(*arrays):
        fused = fits and arrays[0].shape == (4096, 2048) and arrays[4].shape[2] == 32
        return jax.shard_map(
            per_device_fused if fused else per_device_any,
            mesh=mesh,
            in_specs=(
                P("col", "row"),
                P(),
                P(),
                P("row"),
                P("row", "col", None, None, None),
                P("row", "col", None),
                P("row", "col"),
                P(("row", "col"), None),
            ),
            out_specs=(P(("row", "col"), None), P("col", "row"), P(), P()),
            check_vma=False,
        )(*arrays)

    return run
```

```python
import jax
import jax.numpy as jnp
from jax import lax
from jax.experimental import pallas as pl
from jax.experimental.pallas import tpu as pltpu
from jax.sharding import PartitionSpec as P

MESH = pl.DeviceIdType.MESH
F32 = jnp.float32
BF16 = jnp.bfloat16
MIB = 2**20
ORDER = (
    "f0 W1 a01 r00",
    "L H0 r01 f1",
    "a02 P H1 E0",
    "R E1 d00 a11",
    "r10 d01 M0 d10",
    "a03 E2 r02 a12",
    "G0 M1 r03 r11",
    "d02 a13 G1 d03",
    "d11 r12 M2 r13",
    "d13 d12",
)
NC = 2
PARTS = ((0, 512), (512, 512))


def dense_block(tiles, ids, count, tile_rows, tile_cols):
    slots = jnp.arange(tiles.shape[0], dtype=jnp.int32)
    live = jnp.where((slots < count)[:, None, None], tiles, jnp.zeros_like(tiles))
    blank = jnp.zeros((tile_rows * tile_cols, 128, 128), tiles.dtype)
    placed = blank.at[ids].add(live, unique_indices=True)
    placed = placed.reshape(tile_rows, tile_cols, 128, 128)
    return placed.transpose(0, 2, 1, 3).reshape(tile_rows * 128, tile_cols * 128)


def per_device_any(features, weight, bias, self_scale, adj_tiles, tile_ids, tile_counts, cotangent):
    row_block = self_scale.shape[0]
    col_block = features.shape[0]
    block = dense_block(
        adj_tiles[0, 0], tile_ids[0, 0], tile_counts[0, 0], row_block // 128, col_block // 128
    )
    start_row = lax.axis_index("row") * row_block
    col_no = lax.axis_index("col")
    inside = col_no == start_row // col_block
    offset = jnp.where(inside, start_row - col_no * col_block, 0)
    self_rows = jnp.where(inside, self_scale, 0.0)[:, None]
    piece = lax.all_gather(features, "row", axis=1, tiled=True)
    terms = jnp.dot(block, piece, preferred_element_type=F32)
    terms = terms + self_rows * lax.dynamic_slice_in_dim(piece, offset, row_block, 0)
    layer_in = lax.psum_scatter(terms, "col", scatter_dimension=0, tiled=True).astype(BF16)
    pre_act = jnp.dot(layer_in, weight, preferred_element_type=F32) + bias.astype(F32)
    sig = jax.nn.sigmoid(pre_act)
    outputs = pre_act * sig
    slope = sig * (1.0 + pre_act * (1.0 - sig))
    d_pre = (cotangent.astype(F32) * slope).astype(BF16)
    d_weight = lax.dot_general(
        layer_in, d_pre, (((0,), (0,)), ((), ())), preferred_element_type=F32
    )
    d_bias = jnp.sum(d_pre.astype(F32), axis=0)
    d_weight, d_bias = lax.psum((d_weight, d_bias), ("row", "col"))
    d_layer = lax.dot_general(
        d_pre, weight, (((1,), (1,)), ((), ())), preferred_element_type=F32
    ).astype(BF16)
    whole = lax.all_gather(d_layer, "col", axis=0, tiled=True)
    spread = lax.dot_general(block, whole, (((0,), (0,)), ((), ())), preferred_element_type=F32)
    own = lax.dynamic_slice_in_dim(spread, offset, row_block, 0) + self_rows * whole
    spread = lax.dynamic_update_slice_in_dim(spread, own, offset, 0)
    d_features = lax.psum_scatter(spread, "row", scatter_dimension=1, tiled=True)
    return outputs, d_features, d_weight, d_bias


def fused_kernel(
    ids_ref, count_ref, tiles_hbm, feat_ref, w_ref, bias_ref, scale_ref, cot_hbm,
    out_ref, dfeat_ref, dw_ref, db_ref,
    tiles_ref, cot_ref, adj, adj_e, hid, wv, sbuf, sbuf_e, scol, xs, xr, keep, lay, xrow, pre, pt, ptg, dls, dlq,
    dwf, dwp, dwr, dff, dfp, dle, fin, bsum, bias32, ssem, rsem, lsem,
):
    r = lax.axis_index("row")
    x = lax.axis_index("col")
    z = r // 4
    y = (r // 2) % 2
    k = r % 2
    q = 2 * y + k
    ends = (z == 0) | (z == 3)
    mids = (z == 1) | (z == 2)

    def at(xx, yy, zz, kk):
        return (zz * 4 + yy * 2 + kk, xx)

    sib = at(x, y, z, 1 - k)
    xn = at(1 - x, y, z, k)
    yn = at(x, 1 - y, z, k)
    dg = at(x, 1 - y, z, 1 - k)
    zr = at(x, y, jnp.minimum(z + 1, 3), k)
    zl = at(x, y, jnp.maximum(z - 1, 0), k)
    q_y = 2 * (1 - y) + k
    q_s = 2 * y + 1 - k
    q_d = 3 - q

    count = [0]
    sent_by = {}
    pending = {}

    def new():
        count[0] += 1
        return count[0] - 1

    def when(cond, fn):
        if cond is None:
            fn()
        else:
            pl.when(cond)(fn)

    def copy(i, src, dst, to):
        return pltpu.make_async_remote_copy(
            src_ref=src, dst_ref=dst, send_sem=ssem.at[i], recv_sem=rsem.at[i],
            device_id=to, device_id_type=MESH,
        )

    def send(i, src, dst, to, cond=None, rcond=None):
        c = copy(i, src, dst, to)
        when(cond, c.start)
        sent_by[i] = (c, cond)
        pending[i] = (dst, rcond)

    def recv(i, dst, cond=None):
        pending.pop(i, None)
        c = copy(i, dst, dst, sib)
        when(cond, c.wait_recv)

    def slice_at(o):
        return [z, z + 1 - 2 * (z % 2), 2 - z // 2, 3 - 3 * (z // 2)][o]

    def mult(v, n):
        return pl.multiple_of(v, n)

    barrier = pltpu.get_barrier_semaphore()
    near = [(sib, None), (xn, None), (yn, None), (zr, z <= 2), (zl, z >= 1)]
    for peer, cond in near:
        when(cond, lambda peer=peer: pl.semaphore_signal(
            barrier, inc=1, device_id=peer, device_id_type=MESH
        ))

    w_copy = pltpu.make_async_copy(w_ref, wv, lsem.at[0])
    h_copy = pltpu.make_async_copy(feat_ref, hid.at[z], lsem.at[1])
    t_copy = pltpu.make_async_copy(tiles_hbm, tiles_ref, lsem.at[2])
    c_copy = pltpu.make_async_copy(cot_hbm, cot_ref, lsem.at[3])
    t_copy.start()
    h_copy.start()
    t_copy.wait()

    for c in range(2):
        @pl.loop(0, 16)
        def _(t, c=c):
            slot = jnp.int32(0)
            for i in range(32):
                slot = jnp.where(ids_ref[i] == c * 16 + t, i, slot)
            live = jnp.where(slot < count_ref[0], 1.0, 0.0)
            tile = tiles_ref[slot].astype(F32) * live
            adj[pl.ds(mult(c * 512 + q * 128, 128), 128), pl.ds(mult(t * 128, 128), 128)] = (
                tile.astype(BF16)
            )
    for i in range(4):
        sbuf[q, 2 * i:2 * i + 2, :] = scale_ref[...]
    bias32[...] = bias_ref[...].astype(F32)
    h_copy.wait()
    w_copy.start()
    c_copy.start()
    pl.semaphore_wait(barrier, jnp.where(ends, 4, 5))

    def h_part(s, c):
        return hid.at[s, pl.ds(c * (2048 // NC), 2048 // NC)]

    right = {(d, c): new() for d in (1, 2, 3) for c in range(NC)}
    left = {(d, c): new() for d in (1, 2, 3) for c in range(NC)}

    def line_send(ids, part, d, c, own_ok=True):
        sr, sl = jnp.maximum(z - (d - 1), 0), jnp.minimum(z + d - 1, 3)
        send(ids[0][d, c], part(sr, c), part(sr, c), zr, (z >= d - 1) & (z <= 2), z >= d)
        send(ids[1][d, c], part(sl, c), part(sl, c), zl, (z <= 4 - d) & (z >= 1), z <= 3 - d)

    def line_recv(ids, part, d, c):
        sr, sl = jnp.maximum(z - d, 0), jnp.minimum(z + d, 3)
        recv(ids[0][d, c], part(sr, c), z >= d)
        recv(ids[1][d, c], part(sl, c), z <= 3 - d)

    hz = (right, left)
    for c in range(NC):
        line_send(hz, h_part, 1, c)

    s_id = [new() for _ in range(3)]
    send(s_id[0], sbuf.at[q], sbuf.at[q], yn)
    send(s_id[1], sbuf.at[q], sbuf.at[q], sib)

    def a_part(qq, c):
        return adj.at[pl.ds(mult(c * 512 + qq * 128, 128), 128)]

    halves = (1 - x, x)
    ay, asib, afwd = ([new(), new()] for _ in range(3))
    for i, c in enumerate(halves):
        send(asib[i], a_part(q, c), a_part(q, c), sib)
    send(ay[0], a_part(q, 1 - x), a_part(q, 1 - x), yn)

    line_recv(hz, h_part, 1, 0)
    line_send(hz, h_part, 2, 0)
    send(ay[1], a_part(q, x), a_part(q, x), yn)

    recv(s_id[0], sbuf.at[q_y])
    send(s_id[2], sbuf.at[q_y], sbuf.at[q_y], sib)
    recv(s_id[1], sbuf.at[q_s])
    recv(s_id[2], sbuf.at[q_d])
    inside = jnp.where(x == z // 2, 1.0, 0.0)
    for b in range(8):
        row = sbuf[b % 4, b // 4:b // 4 + 1, :] * inside
        scol[b] = jnp.broadcast_to(row, (128, 128)).T

    line_recv(hz, h_part, 1, 1)
    line_send(hz, h_part, 2, 1)

    pair = z // 2
    e, m = 3 * pair, 1 + pair
    e2, m2 = 3 - 3 * pair, 2 - pair
    mid_dev, end_dev = at(x, y, m, k), at(x, y, e, k)

    def e_part(qq, c):
        return adj_e.at[pl.ds(mult(c * 512 + qq * 128, 128), 128)]

    ez, ezy, esib, efwd = ([new(), new()] for _ in range(4))
    es = new()
    for c in range(2):
        send(ez[c], a_part(q, c), e_part(q, c), mid_dev, ends, mids)
    send(es, sbuf, sbuf_e, mid_dev, ends, mids)

    x_id = [[new(), new()] for _ in range(4)]
    l_id = [new() for _ in range(4)]
    row_id = [[new() for _ in range(3)] for _ in range(4)]
    w_waited = []

    def aggregate(o, c, u):
        s = slice_at(o)
        first = (1 - y if u == 0 else y) * 256
        rows = pl.ds(mult(first, 256), 256)
        acc = jnp.dot(
            adj[pl.ds(mult(halves[c] * 512 + first, 256), 256), :], hid[s],
            preferred_element_type=F32,
        )
        own = []
        for i in range(2):
            qq = first // 128 + i
            at_node = mult((z % 2) * 1024 + qq * 256 + halves[c] * 128, 128)
            own.append(scol[halves[c] * 4 + qq] * hid[s, pl.ds(at_node, 128), :].astype(F32))
        acc = acc + jnp.concatenate(own, axis=0)
        if c == 0:
            xs[o, rows] = acc.astype(BF16)
            send(x_id[o][u], xs.at[o, rows], xr.at[o, rows], xn)
        else:
            keep[o, rows] = acc

    def combine(o):
        s = slice_at(o)
        sends = list(zip(row_id[o], (q_y, q_d, q_s), (yn, dg, sib)))
        for u in range(2):
            first = (1 - y if u == 0 else y) * 256
            rows = pl.ds(mult(first, 256), 256)
            recv(x_id[o][u], xr.at[o, rows])
            mine = pl.ds(mult(x * 512 + first, 256), 256)
            lay[s, mine, :] = (keep[o, rows] + xr[o, rows].astype(F32)).astype(BF16)
            for i, qq, to in (sends[:2], sends[2:])[u]:
                piece_rows = pl.ds(mult(x * 512 + qq * 128, 128), 128)
                send(i, lay.at[s, piece_rows], xrow.at[s * 4 + q], to)
        xrow[s * 4 + q] = lay[s, pl.ds(mult(x * 512 + q * 128, 128), 128), :]

    def share(o):
        half = lay.at[slice_at(o), pl.ds(mult(x * 512, 512), 512)]
        send(l_id[o], half, half, xn)

    def linear(o):
        s = slice_at(o)
        for i, qq in zip(row_id[o], (q_y, q_d, q_s)):
            recv(i, xrow.at[s * 4 + qq])
        if not w_waited:
            w_copy.wait()
            c_copy.wait()
            w_waited.append(True)
        block = jnp.concatenate([xrow[s * 4 + i] for i in range(4)], axis=1)

        @pl.loop(0, 2)
        def _(t):
            cols = pl.ds(mult(t * 1024, 1024), 1024)
            prod = jnp.dot(
                block, wv[pl.ds(mult(s * 512, 512), 512), cols], preferred_element_type=F32
            )
            if o == 0:
                pre[:, cols] = prod
            else:
                pre[:, cols] += prod

    for i in range(2):
        recv(asib[i], a_part(q_s, halves[i]))
    for o in range(2):
        aggregate(o, 0, 1)
        aggregate(o, 1, 1)
    recv(ay[0], a_part(q_y, 1 - x))
    send(afwd[0], a_part(q_y, 1 - x), a_part(q_y, 1 - x), sib)
    recv(afwd[0], a_part(q_d, 1 - x))
    aggregate(0, 0, 0)
    line_recv(hz, h_part, 2, 0)
    line_send(hz, h_part, 3, 0)
    aggregate(1, 0, 0)
    line_recv(hz, h_part, 2, 1)
    line_send(hz, h_part, 3, 1)
    for c, u in ((0, 0), (0, 1), (1, 1)):
        aggregate(2, c, u)
    recv(ay[1], a_part(q_y, x))
    send(afwd[1], a_part(q_y, x), a_part(q_y, x), sib)
    for c in range(2):
        send(ezy[c], a_part(q_y, c), e_part(q_y, c), mid_dev, ends, mids)
    recv(afwd[1], a_part(q_d, x))
    for o in range(3):
        aggregate(o, 1, 0)
        combine(o)
        if o < 2:
            share(o)
    linear(0)
    linear(1)
    for c in range(NC):
        line_recv(hz, h_part, 3, c)
    for c, u in ((0, 0), (0, 1), (1, 0), (1, 1)):
        aggregate(3, c, u)
    linear(2)
    combine(3)
    share(3)
    share(2)
    linear(3)

    def p_part(c, h):
        return pt.at[pl.ds(mult(c * 1024 + PARTS[h][0], 256), PARTS[h][1])]

    def activate(c, h):
        @pl.loop(PARTS[h][0] // 128, sum(PARTS[h]) // 128)
        def _(i):
            t = c * 8 + i
            cols = pl.ds(mult(t * 128, 128), 128)
            v = pre[:, cols] + bias32[pl.ds(t, 1), :]
            sig = jax.nn.sigmoid(v)
            out_ref[:, cols] = v * sig
            slope = sig * (1.0 + v * (1.0 - sig))
            d32 = (cot_ref[:, cols].astype(F32) * slope).astype(BF16).astype(F32)
            pt[pl.ds(mult(t * 128, 128), 128), :] = d32.T.astype(BF16)
            bsum[0, pl.ds(t, 1), :] = jnp.sum(d32, axis=0, keepdims=True)

    b_own, b_x = x * 4 + q, (1 - x) * 4 + q
    px, py, pyf, ps, psf, pd, pdf = ([new() for _ in PARTS] for _ in range(7))
    b_ids = [new() for _ in range(6)]

    def p_at(b, h):
        return ptg.at[b, pl.ds(*PARTS[h])]

    def p_send(h):
        send(px[h], p_part(1 - x, h), p_at(b_own, h), xn)
        send(py[h], p_part(x, h), p_at(b_own, h), yn)
        send(ps[h], p_part(x, h), p_at(b_own, h), sib)
        first, n = PARTS[h]
        ptg[b_own, first:first + n] = pt[pl.ds(mult(x * 1024 + first, 256), n), :]

    def p_relay_x(h):
        recv(px[h], p_at(b_x, h))
        send(pyf[h], p_at(b_x, h), p_at(b_x, h), yn)
        send(psf[h], p_at(b_x, h), p_at(b_x, h), sib)
        recv(py[h], p_at(x * 4 + q_y, h))
        send(pd[h], p_at(x * 4 + q_y, h), p_at(x * 4 + q_y, h), sib)

    def p_relay_y(h):
        recv(pyf[h], p_at((1 - x) * 4 + q_y, h))
        send(pdf[h], p_at((1 - x) * 4 + q_y, h), p_at((1 - x) * 4 + q_y, h), sib)

    def p_last(h):
        recv(ps[h], p_at(x * 4 + q_s, h))
        recv(psf[h], p_at((1 - x) * 4 + q_s, h))
        recv(pd[h], p_at(x * 4 + q_d, h))
        recv(pdf[h], p_at((1 - x) * 4 + q_d, h))

    activate(1 - x, 0)
    activate(x, 0)
    p_send(0)
    activate(1 - x, 1)
    activate(x, 1)
    if len(PARTS) > 2:
        p_send(1)
        activate(1 - x, 2)
        activate(x, 2)

    @pl.loop(0, 2)
    def _(i):
        acc = jnp.dot(
            wv[pl.ds(mult(i * 1024, 1024), 1024), :], pt[...], preferred_element_type=F32
        ).astype(BF16)
        for j in range(2):
            for qq in range(4):
                first = j * 512 + qq * 128
                dls[qq, i * 2 + j] = acc[first:first + 128]

    dl_to = [
        (1 - x, y, k), (1 - x, y, 1 - k), (x, y, 1 - k),
        (x, 1 - y, k), (x, 1 - y, 1 - k), (1 - x, 1 - y, k), (1 - x, 1 - y, 1 - k),
    ]
    dl_ids = [new() for _ in dl_to]

    def send_layer_grad(which):
        for i in which:
            xx, yy, kk = dl_to[i]
            send(dl_ids[i], dls.at[2 * yy + kk], dlq.at[b_own], at(xx, yy, z, kk))

    p_send(len(PARTS) - 1)
    send(b_ids[0], bsum.at[0], bsum.at[1], xn)
    dlq[b_own] = dls[q]
    p_relay_x(0)
    send_layer_grad((0, 1, 2))
    p_relay_x(1)
    p_relay_y(0)
    recv(b_ids[0], bsum.at[1])
    bsum[2] = bsum[0] + bsum[1]
    send(b_ids[1], bsum.at[2], bsum.at[3], yn)
    for o in range(4):
        recv(l_id[o], lay.at[slice_at(o), pl.ds(mult((1 - x) * 512, 512), 512)])
    p_last(0)

    dw_ids = [[new() for _ in range(5)] for _ in PARTS]

    def weight_grad(h):
        rows = pl.ds(*PARTS[h])
        lhs = jnp.concatenate([ptg[b, rows, :] for b in range(8)], axis=1)
        rhs = jnp.concatenate([lay[s] for s in range(4)], axis=1)
        acc = jnp.dot(lhs, rhs, preferred_element_type=F32)
        for s in range(4):
            dwf[s, rows, :] = acc[:, s * 128:(s + 1) * 128]
            dwp[s, rows, :] = acc[:, s * 128:(s + 1) * 128].astype(BF16)

    def weight_send(h):
        rows = pl.ds(*PARTS[h])
        for i, s_to in enumerate((m2, e2)):
            send(dw_ids[h][i], dwp.at[s_to, rows], dwr.at[i, rows], mid_dev, ends, mids)
        beside = at(x, y, m + e - z, k)
        send(dw_ids[h][2], dwp.at[m + e - z, rows], dwr.at[2, rows], beside)

    def weight_pass(h):
        rows = pl.ds(*PARTS[h])
        for i, s_to in enumerate((m2, e2)):
            recv(dw_ids[h][i], dwr.at[i, rows], mids)

            @pl.when(mids)
            def _(i=i, s_to=s_to):
                dwp[s_to, rows, :] = (
                    dwf[s_to, rows, :] + dwr[i, rows, :].astype(F32)
                ).astype(BF16)
            send(dw_ids[h][3 + i], dwp.at[s_to, rows], dwr.at[3, rows],
                 at(x, y, s_to, k), mids, (mids, ends)[i])

    weight_grad(0)
    weight_send(0)
    send_layer_grad((3, 4, 5, 6))
    if len(PARTS) > 2:
        p_relay_x(2)
    p_relay_y(1)
    recv(b_ids[1], bsum.at[3])
    bsum[4] = bsum[2] + bsum[3]
    send(b_ids[2], bsum.at[4], bsum.at[5], sib)
    p_last(1)
    weight_grad(1)
    weight_send(1)
    weight_pass(0)
    if len(PARTS) > 2:
        p_relay_y(2)
        p_last(2)
        weight_grad(2)
        weight_send(2)
        weight_pass(1)
    recv(b_ids[2], bsum.at[5])
    bsum[6] = bsum[4] + bsum[5]
    for d in (1, 2, 3):
        send(b_ids[2 + d], bsum.at[6], bsum.at[6 + d], at(x, y, (z + d) % 4, k))

    def layer_grads_here():
        for i, (xx, yy, kk) in zip(dl_ids, dl_to):
            recv(i, dlq.at[xx * 4 + 2 * yy + kk])

    f_in = [new() for _ in range(3)]
    f_out = [[new(), new()] for _ in range(2)]
    f_fin = [new(), new()]
    f_slices = (e2, m2, m)
    own_half = x == z // 2

    def grads(dl, a, scale, at_z, first, n, t, width):
        cols = pl.ds(mult(t * width, width), width)
        lhs = jnp.concatenate(
            [dl[b, pl.ds(first, n)].reshape(n * 128, 128) for b in range(8)], axis=1
        )
        acc = jnp.dot(lhs, a[:, cols], preferred_element_type=F32)
        per = width // 256
        own = jnp.where(own_half & (t // (4 // per) == at_z % 2), 1.0, 0.0)
        diag = []
        for j in range(per):
            qq = (t % (4 // per)) * per + j
            for c in range(2):
                row = scale[qq, c:c + 1, :] * own
                diag.append(
                    dl[c * 4 + qq, pl.ds(first, n)].reshape(n * 128, 128).astype(F32) * row
                )
        return acc + jnp.concatenate(diag, axis=1), cols

    def grads_here(first, n):
        @pl.loop(0, 4)
        def _(t):
            acc, cols = grads(dlq, adj, sbuf, z, first, n, t, 512)
            for i in range(n):
                dff[first + i, :, cols] = acc[i * 128:(i + 1) * 128]

    def grads_end(s, c):
        @pl.loop(2 * c, 2 * c + 2)
        def _(t):
            acc, cols = grads(dle, adj_e, sbuf_e, e, s, 1, t, 512)
            tot = dff[s, :, cols] + acc
            dff[s, :, cols] = tot
            dfp[s, :, cols] = tot.astype(BF16)

    def mid_pass():
        recv(es, sbuf_e, mids)
        for i, qq, on in ((ez, q, esib), (ezy, q_y, efwd)):
            for c in range(2):
                recv(i[c], e_part(qq, c), mids)
                send(on[c], e_part(qq, c), e_part(qq, c), sib, mids, mids)

    def end_send(j):
        s = f_slices[j]
        send(f_in[j], dlq.at[:, s], dle.at[:, s], mid_dev, ends, mids)

    def grads_own(i):
        @pl.when(mids)
        def _():
            grads_here(2 * (pair if i else 1 - pair), 2)
        if i == 0:
            @pl.when(ends)
            def _():
                grads_here(e, 1)


    def mid_ready():
        for c in range(2):
            recv(esib[c], e_part(q_s, c), mids)
            recv(efwd[c], e_part(q_d, c), mids)

    def cut(c):
        return pl.ds(c * 1024, 1024)

    def mid_send(j):
        s_to = f_slices[j]
        recv(f_in[j], dle.at[:, s_to], mids)
        for c in range(2):
            @pl.when(mids)
            def _(c=c):
                grads_end(s_to, c)
            if j < 2:
                send(f_out[j][c], dfp.at[s_to, :, cut(c)], fin.at[j, :, cut(c)],
                     at(x, y, m2, k), mids, mids)

    def mid_merge(c):
        recv(f_out[0][c], fin.at[0, :, cut(c)], mids)

        @pl.when(mids)
        def _():
            dfp[e, :, cut(c)] = (
                dff[e, :, cut(c)] + fin[0, :, cut(c)].astype(F32)
            ).astype(BF16)
        send(f_fin[c], dfp.at[e, :, cut(c)], fin.at[1, :, cut(c)], end_dev, mids, ends)

    def piece(s, qq, c, h):
        return dw_ref.at[pl.ds((s * 4 + qq) * 8 + h * 4 + c * 2, 2)]

    gz = tuple({(d, h): new() for d in (1, 2, 3) for h in range(len(PARTS))} for _ in range(2))
    gx, gy, gxy, gyx, gs, gsd = (
        {(h, o): new() for h in range(len(PARTS)) for o in range(4)} for _ in range(6)
    )

    def z_piece(s, h):
        return piece(s, q, x, h)

    def finish(h):
        rows = pl.ds(*PARTS[h])
        recv(dw_ids[h][2], dwr.at[2, rows])
        recv(dw_ids[h][3], dwr.at[3, rows], mids)
        recv(dw_ids[h][4], dwr.at[3, rows], ends)
        for t in range(PARTS[h][0] // 128, sum(PARTS[h]) // 128):
            rr = pl.ds(t * 128, 128)
            tot = dwf[z, rr, :] + dwr[2, rr, :].astype(F32) + dwr[3, rr, :].astype(F32)
            half = t % 2 * 128
            at_block = (z * 4 + q) * 8 + h * 4 + x * 2 + t % 4 // 2
            dw_ref[at_block, :, half:half + 128] = tot.T.astype(BF16)
        line_send(gz, z_piece, 1, h)
        spread(h, 0)

    def spread(h, o):
        src = piece(slice_at(o), q, x, h)
        send(gx[h, o], src, src, xn)
        send(gy[h, o], src, src, yn)

    def both(s, qq, h):
        return dw_ref.at[pl.ds((s * 4 + qq) * 8 + h * 4, 4)]

    def part(ref, i):
        return ref.at[:, pl.ds(i * 64, 64)]

    def relay(h, o):
        s = slice_at(o)
        from_x, from_y = piece(s, q, 1 - x, h), piece(s, q_y, x, h)
        recv(gx[h, o], from_x)
        send(gxy[h, o], part(from_x, 0), part(from_x, 0), yn)
        send(gs[h, o], both(s, q, h), both(s, q, h), sib)
        recv(gy[h, o], from_y)
        send(gyx[h, o], part(from_y, 1), part(from_y, 1), xn)

    def relay_diag(h, o):
        block = piece(slice_at(o), q_y, 1 - x, h)
        recv(gxy[h, o], part(block, 0))
        recv(gyx[h, o], part(block, 1))
        send(gsd[h, o], both(slice_at(o), q_y, h), both(slice_at(o), q_y, h), sib)

    def last(h, o):
        recv(gs[h, o], both(slice_at(o), q_s, h))
        recv(gsd[h, o], both(slice_at(o), q_d, h))

    def along(h, d):
        line_recv(gz, z_piece, d, h)
        if d < 3:
            line_send(gz, z_piece, d + 1, h)
        spread(h, d)

    steps = {
        "f": finish, "a": along, "r": relay, "d": relay_diag,
        "E": end_send, "M": mid_send, "G": mid_merge, "R": mid_ready, "H": grads_own, "P": mid_pass,
        "L": layer_grads_here, "W": weight_pass,
    }
    for step in (t for group in ORDER for t in group.split()):
        steps[step[0]](*(int(i) for i in step[1:]))
    for d in (1, 2, 3):
        recv(b_ids[2 + d], bsum.at[6 + d])
    db_ref[...] = bsum[6] + bsum[7] + bsum[8] + bsum[9]

    for c in range(2):
        recv(f_out[1][c], fin.at[1, :, cut(c)], mids)
        recv(f_fin[c], fin.at[1, :, cut(c)], ends)

    @pl.loop(0, 16)
    def _(t):
        cols = pl.ds(mult(t * 128, 128), 128)
        tot = dff[z, :, cols] + fin[1, :, cols].astype(F32)
        dfeat_ref[pl.ds(mult(t * 128, 128), 128), :] = tot.T

    for h in range(len(PARTS)):
        for o in range(4):
            last(h, o)
    assert not pending and count[0] <= N_SEMS, count
    for i, (c, cond) in sent_by.items():
        when(cond, c.wait_send)


def widen_kernel(dw_ref, out_ref, dfeat_ref, db_ref, dw_out, out_out, dfeat_out, db_out, wide, sem):
    copies = [
        pltpu.make_async_copy(src, dst, sem.at[16 + i])
        for i, (src, dst) in enumerate(
            ((out_ref, out_out), (dfeat_ref, dfeat_out), (db_ref, db_out))
        )
    ]
    for c in copies:
        c.start()
    rows = [
        pltpu.make_async_copy(wide.at[i], dw_out.at[pl.ds(i * 128, 128)], sem.at[i])
        for i in range(16)
    ]
    for i in range(16):
        for j in range(8):
            block = 8 * i + j % 4 // 2 * 4 + j // 4 * 2 + j % 2
            wide[i, :, j * 256:(j + 1) * 256] = dw_ref[block].astype(F32)
        rows[i].start()
    for c in copies + rows:
        c.wait()


N_SEMS = 160


def per_device_fused(features, weight, bias, self_scale, adj_tiles, tile_ids, tile_counts, cotangent):
    vmem = pl.BlockSpec(memory_space=pltpu.VMEM)
    smem = pl.BlockSpec(memory_space=pltpu.SMEM)
    hbm = pl.BlockSpec(memory_space=pl.ANY)
    outputs, d_features, gathered, d_bias = pl.pallas_call(
        fused_kernel,
        out_shape=(
            pltpu.VMEM((128, 2048), F32),
            pltpu.VMEM((2048, 128), F32),
            pltpu.VMEM((128, 128, 256), BF16),
            pltpu.VMEM((16, 128), F32),
        ),
        in_specs=[smem, smem, hbm, hbm, hbm, vmem, vmem, hbm],
        out_specs=(vmem, vmem, vmem, vmem),
        scratch_shapes=[
            pltpu.VMEM((32, 128, 128), BF16),
            pltpu.VMEM((128, 2048), BF16),
            pltpu.VMEM((1024, 2048), BF16),
            pltpu.VMEM((1024, 2048), BF16),
            pltpu.VMEM((4, 2048, 128), BF16),
            pltpu.VMEM((2048, 2048), BF16),
            pltpu.VMEM((4, 8, 128), F32),
            pltpu.VMEM((4, 8, 128), F32),
            pltpu.VMEM((8, 128, 128), F32),
            pltpu.VMEM((4, 512, 128), BF16),
            pltpu.VMEM((4, 512, 128), BF16),
            pltpu.VMEM((4, 512, 128), F32),
            pltpu.VMEM((4, 1024, 128), BF16),
            pltpu.VMEM((16, 128, 128), BF16),
            pltpu.VMEM((128, 2048), F32),
            pltpu.VMEM((2048, 128), BF16),
            pltpu.VMEM((8, 1024, 128), BF16),
            pltpu.VMEM((4, 4, 128, 128), BF16),
            pltpu.VMEM((8, 4, 128, 128), BF16),
            pltpu.VMEM((4, 1024, 128), F32),
            pltpu.VMEM((4, 1024, 128), BF16),
            pltpu.VMEM((4, 1024, 128), BF16),
            pltpu.VMEM((4, 128, 2048), F32),
            pltpu.VMEM((4, 128, 2048), BF16),
            pltpu.VMEM((8, 4, 128, 128), BF16),
            pltpu.VMEM((2, 128, 2048), BF16),
            pltpu.VMEM((10, 16, 128), F32),
            pltpu.VMEM((16, 128), F32),
            pltpu.SemaphoreType.DMA((N_SEMS,)),
            pltpu.SemaphoreType.DMA((N_SEMS,)),
            pltpu.SemaphoreType.DMA((4,)),
        ],
        compiler_params=pltpu.CompilerParams(
            collective_id=0, has_side_effects=True, vmem_limit_bytes=53 * MIB
        ),
        cost_estimate=pl.CostEstimate(
            flops=7_600_000_000, bytes_accessed=24 * MIB, transcendentals=262144
        ),
    )(
        tile_ids[0, 0], tile_counts[0], adj_tiles[0, 0], features, weight,
        bias.reshape(16, 128), self_scale.reshape(2, 128), cotangent,
    )
    d_weight, outputs, d_features, d_bias = pl.pallas_call(
        widen_kernel,
        out_shape=(
            jax.ShapeDtypeStruct((2048, 2048), F32),
            jax.ShapeDtypeStruct((128, 2048), F32),
            jax.ShapeDtypeStruct((2048, 128), F32),
            jax.ShapeDtypeStruct((16, 128), F32),
        ),
        in_specs=[vmem] * 4,
        out_specs=(hbm, hbm, hbm, hbm),
        scratch_shapes=[pltpu.VMEM((16, 128, 2048), F32), pltpu.SemaphoreType.DMA((19,))],
        compiler_params=pltpu.CompilerParams(vmem_limit_bytes=30 * MIB),
    )(gathered, outputs, d_features, d_bias)
    return outputs, d_features, d_weight, d_bias.reshape(2048)


def solution(mesh):
    fits = dict(mesh.shape) == {"row": 16, "col": 2}

    def run(*arrays):
        fused = fits and arrays[0].shape == (4096, 2048) and arrays[4].shape[2] == 32
        return jax.shard_map(
            per_device_fused if fused else per_device_any,
            mesh=mesh,
            in_specs=(
                P("col", "row"),
                P(),
                P(),
                P("row"),
                P("row", "col", None, None, None),
                P("row", "col", None),
                P("row", "col"),
                P(("row", "col"), None),
            ),
            out_specs=(P(("row", "col"), None), P("col", "row"), P(), P()),
            check_vma=False,
        )(*arrays)

    return run
```
